32 devices in a mesh: seq: 4 (over z), head: 4 (over y, x), dp: 2 (over core).
Axes of the slice: x: 2, y: 2, z: 4, core: 2. Of those that a mesh axis runs over, the one named last changes fastest.
Arguments:
- tokens: float32 [8, 784, 1024], P('dp', 'seq', 'head'), may hold values from -6 to 6
- gain_attn: float32 [1024], P('head'), may hold values from 0.5 to 1.5
- qkv_weight: float32 [1024, 3, 1024], P(None, None, 'head'), may hold values from -0.1875 to 0.1875
- out_weight: float32 [1024, 1024], P('head'), may hold values from -0.75 to 0.75
- gain_ffn: float32 [1024], P('head'), may hold values from 0.5 to 1.5
- up_weight: float32 [1024, 4096], P(None, 'head'), may hold values from -0.1875 to 0.1875
- up_bias: float32 [4096], P('head'), may hold values from -3 to 3
- down_weight: float32 [4096, 1024], P('head'), may hold values from -0.09375 to 0.09375
- down_bias: float32 [1024], P('head'), may hold values from -3 to 3
- out_grad: float32 [8, 784, 1024], P('dp', 'seq', 'head'), may hold values from -6 to 6
Outputs:
- output: float32 [8, 784, 1024], P('dp', 'seq', 'head')
- tokens_grad: float32 [8, 784, 1024], P('dp', 'seq', 'head')
- gain_attn_grad: float32 [1024], P('head')
- qkv_weight_grad: float32 [1024, 3, 1024], P(None, None, 'head')
- out_weight_grad: float32 [1024, 1024], P('head')
- gain_ffn_grad: float32 [1024], P('head')
- up_weight_grad: float32 [1024, 4096], P(None, 'head')
- up_bias_grad: float32 [4096], P('head')
- down_weight_grad: float32 [4096, 1024], P('head')
- down_bias_grad: float32 [1024], P('head')
The draws below stay inside these ranges and needn't reach their ends.
All inputs are finite; a program needn't handle non-finite values.
Results may differ from the reference program's by a relative error of at most 0.0003.
Values sent between devices are 32-bit elements; how exact they have to be, the bound alone decides.
A program may use at most 192 MiB of HBM per device.

```python
import math
import jax
import jax.numpy as jnp
from jax import lax

D = 1024
HEADS = 16
FF = 4096
HEAD_DIM = 64
PIX = 784
IMAGES = 8


def steps_of(rng, extent, split, least, largest):
    level = 1.0
    for dim, shards_of in split:
        steps = jax.random.uniform(jax.random.fold_in(jax.random.fold_in(rng, 6), dim), (shards_of,), jnp.float32, least / len(split), largest / len(split))
        level = level * jnp.repeat(jnp.exp(steps), extent[dim] // shards_of).reshape((-1,) + (1,) * (len(extent) - 1 - dim))
    return level


def bell_draw(own_key, dims, width, most, pieces=(), kind=jnp.bfloat16):
    result = jax.random.normal(own_key, dims, jnp.float32) * width
    if len(pieces) > 0:
        result = steps_of(own_key, dims, pieces, -0.22, 0.18) * result
    return jnp.clip(result, min=-most, max=most).astype(kind)


def setup_inputs(seed: int = 0) -> dict:
    splits = jax.random.split(jax.random.key(seed), 11)
    tokens = bell_draw(splits[0], (IMAGES, PIX, D), 1.0, 6.0, ((0, 2), (1, 4), (2, 4)), jnp.float32)
    gain_attn = jnp.clip(1.0 + 0.1 * jax.random.normal(splits[1], (D,), jnp.float32), 0.5, 1.5)
    qkv_weight = bell_draw(splits[2], (D, 3, D), D ** -0.5, 0.1875, ((2, 4),), jnp.float32)
    out_weight = bell_draw(splits[3], (D, D), (D // 16) ** -0.5, 0.75, ((0, 4),), jnp.float32)
    gain_ffn = jnp.clip(1.0 + 0.1 * jax.random.normal(splits[4], (D,), jnp.float32), 0.5, 1.5)
    up_weight = bell_draw(splits[5], (D, FF), D ** -0.5, 0.1875, ((1, 4),), jnp.float32)
    up_bias = bell_draw(splits[6], (FF,), 0.5, 3.0, ((0, 4),), jnp.float32)
    down_weight = bell_draw(splits[7], (FF, D), FF ** -0.5, 0.09375, ((0, 4),), jnp.float32)
    down_bias = bell_draw(splits[8], (D,), 0.5, 3.0, ((0, 4),), jnp.float32)
    out_grad = bell_draw(splits[9], (IMAGES, PIX, D), 1.0, 6.0, ((0, 2), (1, 4), (2, 4)), jnp.float32)
    return dict(tokens=tokens, gain_attn=gain_attn, qkv_weight=qkv_weight, out_weight=out_weight, gain_ffn=gain_ffn, up_weight=up_weight, up_bias=up_bias, down_weight=down_weight, down_bias=down_bias, out_grad=out_grad)


@jax.custom_vjp
def low(v):
    return lax.optimization_barrier(v.astype(jnp.bfloat16)).astype(jnp.float32)

@jax.custom_vjp
def low_back(v):
    return v

def low_keep(v):
    return (low(v), None)

def low_pass(kept, grad):
    return (grad,)

def back_keep(v):
    return (v, None)

def back_low(kept, grad):
    return (low(grad),)
low.defvjp(low_keep, low_pass)
low_back.defvjp(back_keep, back_low)
highest = lax.Precision.HIGHEST
norm_eps = 1e-05

def feature(values_in):
    return jax.nn.elu(values_in) + 1.0

def layer_norm(values_in, gain):
    row_mean = lax.optimization_barrier(jnp.mean(values_in, axis=-1, keepdims=True))
    centred = values_in - row_mean
    row_var = lax.optimization_barrier(jnp.mean(centred * centred, axis=-1, keepdims=True))
    return centred * lax.rsqrt(row_var + norm_eps) * gain

def causal_attend(query_proj, key_proj, value_proj):
    query_feat = feature(query_proj)
    key_feat = feature(key_proj)
    length_now = query_proj.shape[1]
    scores = jnp.einsum('gihe,gjhe->ghij', query_feat, key_feat, precision=highest)
    row_index = lax.broadcasted_iota(jnp.int32, (length_now, length_now), 0)
    col_index = lax.broadcasted_iota(jnp.int32, (length_now, length_now), 1)
    scores = jnp.where(col_index <= row_index, scores, jnp.float32(0.0))
    numerator = jnp.einsum('ghij,gjhe->gihe', scores, value_proj, precision=highest)
    denominator = jnp.transpose(lax.optimization_barrier(jnp.sum(scores, axis=-1)), (0, 2, 1))
    return numerator / denominator[..., None]

def block_forward(blocks_in, gain_attn, qkv_weight, out_weight, gain_ffn, up_weight, up_bias, down_weight, down_bias):
    group_size, length_now, model_width = blocks_in.shape
    normed_one = layer_norm(blocks_in, gain_attn)
    projected = jnp.einsum('gpd,dke->gpke', normed_one, qkv_weight, precision=highest)
    head_shape = (group_size, length_now, HEADS, HEAD_DIM)
    query_proj = projected[:, :, 0].reshape(head_shape)
    key_proj = projected[:, :, 1].reshape(head_shape)
    value_proj = projected[:, :, 2].reshape(head_shape)
    mixed = causal_attend(query_proj, key_proj, value_proj).reshape(blocks_in.shape)
    residual = blocks_in + jnp.einsum('gpd,de->gpe', mixed, out_weight, precision=highest)
    normed_two = layer_norm(residual, gain_ffn)
    up_proj = jnp.einsum('gpd,df->gpf', normed_two, up_weight, precision=highest) + up_bias
    hidden = jax.nn.gelu(up_proj, approximate=True)
    return residual + jnp.einsum('gpf,fd->gpd', hidden, down_weight, precision=highest) + down_bias

def reference(tokens, gain_attn, qkv_weight, out_weight, gain_ffn, up_weight, up_bias, down_weight, down_bias, out_grad):
    group_size = math.gcd(IMAGES, 4)

    def whole_layer(tokens_in, gain_first, weight_qkv, weight_out, gain_second, weight_up, bias_up, weight_down, bias_down):
        blocks_all = tokens_in.reshape((IMAGES // group_size, group_size, PIX, D))

        def one_block(blocks_in):
            return block_forward(blocks_in, gain_first, weight_qkv, weight_out, gain_second, weight_up, bias_up, weight_down, bias_down)
        return lax.map(jax.checkpoint(one_block), blocks_all).reshape(tokens_in.shape)
    output, pullback = jax.vjp(whole_layer, tokens, gain_attn, qkv_weight, out_weight, gain_ffn, up_weight, up_bias, down_weight, down_bias)
    gradients = pullback(out_grad)
    return (output, gradients[0], gradients[1], gradients[2], gradients[3], gradients[4], gradients[5], gradients[6], gradients[7], gradients[8])
```

```python
import jax
import jax.numpy as jnp
from jax import lax
from jax.sharding import PartitionSpec as P

HEAD_DIM = 64


highest = lax.Precision.HIGH
norm_eps = 1e-05


def entering(part, axis, combine, identity, reverse):
    count = lax.axis_size(axis)
    place = lax.axis_index(axis)
    ahead = count - 1 - place if reverse else place
    gathered = jax.tree.map(lambda a: lax.all_gather(a, axis), part)
    state = jax.tree.map(lambda a, e: jnp.zeros_like(a) + jnp.asarray(e, a.dtype), part, identity)

    def one(turn, state):
        source = count - 1 - turn if reverse else turn
        return combine(
            state, jax.tree.map(lambda a: lax.dynamic_index_in_dim(a, source, 0, False), gathered)
        )

    return lax.fori_loop(0, ahead, one, state)


def feature(values_in):
    return jax.nn.elu(values_in) + 1.0


def layer_norm(values_in, gain):
    row_mean = jnp.mean(values_in, axis=-1, keepdims=True)
    centred = values_in - row_mean
    row_var = jnp.mean(centred * centred, axis=-1, keepdims=True)
    return centred * lax.rsqrt(row_var + norm_eps) * gain


def norm_back(partial_grad, rows_full, gain_full, gain_share):
    local_width = gain_share.shape[0]
    model_width = gain_full.shape[0]
    row_mean = jnp.mean(rows_full, axis=-1, keepdims=True)
    centred = rows_full - row_mean
    row_inv = lax.rsqrt(jnp.mean(centred * centred, axis=-1, keepdims=True) + norm_eps)
    scaled = partial_grad * gain_full
    sums = lax.psum(
        jnp.stack(
            [jnp.sum(scaled, axis=-1), jnp.sum(scaled * (centred * row_inv), axis=-1)]
        ),
        "head",
    )
    means = (sums / model_width)[:, :, None]
    share = lax.psum_scatter(partial_grad, "head", scatter_dimension=1, tiled=True)
    start = lax.axis_index("head") * local_width
    xhat = lax.dynamic_slice_in_dim(centred, start, local_width, 1) * row_inv
    back = (share * gain_share - means[0] - xhat * means[1]) * row_inv
    return back, jnp.sum(share * xhat, axis=0)


def mlp_act(values_in):
    return jax.nn.gelu(values_in, approximate=True)


def block_attend(query_proj, key_proj, value_proj, prior_state, prior_total):
    query_feat = feature(query_proj)
    key_feat = feature(key_proj)
    length_now = query_proj.shape[1]
    scores = jnp.einsum("gihe,gjhe->ghij", query_feat, key_feat, precision=highest)
    row_index = lax.broadcasted_iota(jnp.int32, (length_now, length_now), 0)
    col_index = lax.broadcasted_iota(jnp.int32, (length_now, length_now), 1)
    scores = jnp.where(col_index <= row_index, scores, jnp.float32(0.0))
    numerator = jnp.einsum("ghij,gjhe->gihe", scores, value_proj, precision=highest)
    numerator = numerator + jnp.einsum(
        "gihe,ghef->gihf", query_feat, prior_state, precision=highest
    )
    denominator = jnp.sum(scores, axis=-1) + jnp.einsum(
        "gihe,ghe->ghi", query_feat, prior_total, precision=highest
    )
    return numerator / jnp.transpose(denominator, (0, 2, 1))[..., None]


def block_state(key_proj, value_proj):
    key_feat = feature(key_proj)
    kv_sum = jnp.einsum("gihe,gihf->ghef", key_feat, value_proj, precision=highest)
    return (kv_sum, jnp.sum(key_feat, axis=1))


def add_pair(earlier, later):
    return (earlier[0] + later[0], earlier[1] + later[1])


def per_device(
    tokens,
    gain_attn,
    qkv_weight,
    out_weight,
    gain_ffn,
    up_weight,
    up_bias,
    down_weight,
    down_bias,
    out_grad,
):
    image_count, block_len, local_width = tokens.shape
    row_count = image_count * block_len
    model_width = qkv_weight.shape[0]
    heads_local = local_width // HEAD_DIM
    column_start = lax.axis_index("head") * local_width
    full_tokens, gain_first, gain_second = (
        lax.all_gather(tokens, "head", axis=2, tiled=True),
        lax.all_gather(gain_attn, "head", axis=0, tiled=True),
        lax.all_gather(gain_ffn, "head", axis=0, tiled=True),
    )
    token_rows = full_tokens.reshape(row_count, model_width)
    normed_one = layer_norm(token_rows, gain_first)
    proj_weight = qkv_weight.reshape(model_width, 3 * local_width)
    projected = jnp.dot(normed_one, proj_weight, precision=highest)
    parts_view = projected.reshape(image_count, block_len, 3, heads_local, HEAD_DIM)
    query_proj = parts_view[:, :, 0]
    key_proj = parts_view[:, :, 1]
    value_proj = parts_view[:, :, 2]
    (own_state, own_total), pull_state = jax.vjp(block_state, key_proj, value_proj)
    zero_pair = (jnp.zeros_like(own_state), jnp.zeros_like(own_total))
    prior_state, prior_total = entering((own_state, own_total), "seq", add_pair, zero_pair, False)
    mixed, pull_attend = jax.vjp(
        block_attend, query_proj, key_proj, value_proj, prior_state, prior_total
    )
    mixed_rows = mixed.reshape(row_count, local_width)
    branch_out = jnp.dot(mixed_rows, out_weight, precision=highest)
    token_share = tokens.reshape(row_count, local_width)
    resid_share = token_share + lax.psum_scatter(
        branch_out, "head", scatter_dimension=1, tiled=True
    )
    resid_full = lax.all_gather(resid_share, "head", axis=1, tiled=True)
    normed_two = layer_norm(resid_full, gain_second)
    up_proj = jnp.dot(normed_two, up_weight, precision=highest) + up_bias
    hidden, pull_act = jax.vjp(mlp_act, up_proj)
    down_proj = jnp.dot(hidden, down_weight, precision=highest)
    ffn_share = lax.psum_scatter(down_proj, "head", scatter_dimension=1, tiled=True)
    output = (resid_share + ffn_share + down_bias).reshape(tokens.shape)
    grad_share = out_grad.reshape(row_count, local_width)
    grad_full = lax.all_gather(grad_share, "head", axis=1, tiled=True)
    down_bias_grad = jnp.sum(grad_share, axis=0)
    down_weight_grad = jnp.dot(hidden.T, grad_full, precision=highest)
    hidden_grad = jnp.dot(grad_full, down_weight.T, precision=highest)
    (up_grad,) = pull_act(hidden_grad)
    up_bias_grad = jnp.sum(up_grad, axis=0)
    up_weight_grad = jnp.dot(normed_two.T, up_grad, precision=highest)
    ffn_grads = lax.psum((up_weight_grad, down_weight_grad), ("seq", "dp"))
    resid_back, gain_ffn_share = norm_back(
        jnp.dot(up_grad, up_weight.T, precision=highest), resid_full, gain_second, gain_ffn
    )
    resid_grad_share = grad_share + resid_back
    resid_grad = lax.all_gather(resid_grad_share, "head", axis=1, tiled=True)
    out_weight_grad = jnp.dot(mixed_rows.T, resid_grad, precision=highest)
    mixed_grad = jnp.dot(resid_grad, out_weight.T, precision=highest).reshape(mixed.shape)
    query_grad, key_grad, value_grad, state_grad, total_grad = pull_attend(mixed_grad)
    later_state, later_total = entering((state_grad, total_grad), "seq", add_pair, zero_pair, True)
    key_extra, value_extra = pull_state((later_state, later_total))
    key_grad = key_grad + key_extra
    value_grad = value_grad + value_extra
    proj_grad = jnp.stack([query_grad, key_grad, value_grad], axis=2).reshape(
        row_count, 3 * local_width
    )
    qkv_weight_grad = jnp.dot(normed_one.T, proj_grad, precision=highest).reshape(qkv_weight.shape)
    token_back, gain_attn_share = norm_back(
        jnp.dot(proj_grad, proj_weight.T, precision=highest), token_rows, gain_first, gain_attn
    )
    tokens_grad = (resid_grad_share + token_back).reshape(tokens.shape)
    summed_grads = lax.psum(
        (
            gain_attn_share,
            qkv_weight_grad,
            out_weight_grad,
            gain_ffn_share,
            up_bias_grad,
            down_bias_grad,
        ),
        ("seq", "dp"),
    )
    return (
        output,
        tokens_grad,
        summed_grads[0],
        summed_grads[1],
        summed_grads[2],
        summed_grads[3],
        ffn_grads[0],
        summed_grads[4],
        ffn_grads[1],
        summed_grads[5],
    )


def solution(mesh):
    return jax.shard_map(
        per_device,
        mesh=mesh,
        in_specs=(
            P("dp", "seq", "head"),
            P("head"),
            P(None, None, "head"),
            P("head", None),
            P("head"),
            P(None, "head"),
            P("head"),
            P("head", None),
            P("head"),
            P("dp", "seq", "head"),
        ),
        out_specs=(
            P("dp", "seq", "head"),
            P("dp", "seq", "head"),
            P("head"),
            P(None, None, "head"),
            P("head", None),
            P("head"),
            P(None, "head"),
            P("head"),
            P("head", None),
            P("head"),
        ),
        check_vma=False,
    )
```

```python
import functools

import jax
import jax.numpy as jnp
from jax import lax
from jax.experimental import pallas as pl
from jax.experimental.pallas import tpu as pltpu
from jax.sharding import PartitionSpec as P

HEAD_DIM = 64


highest = lax.Precision.HIGH
norm_eps = 1e-05


def entering(part, axis, combine, identity, reverse):
    count = lax.axis_size(axis)
    place = lax.axis_index(axis)
    ahead = count - 1 - place if reverse else place
    gathered = jax.tree.map(lambda a: lax.all_gather(a, axis), part)
    state = jax.tree.map(lambda a, e: jnp.zeros_like(a) + jnp.asarray(e, a.dtype), part, identity)

    def one(turn, state):
        source = count - 1 - turn if reverse else turn
        return combine(
            state, jax.tree.map(lambda a: lax.dynamic_index_in_dim(a, source, 0, False), gathered)
        )

    return lax.fori_loop(0, ahead, one, state)


def feature(values_in):
    return jax.nn.elu(values_in) + 1.0


def layer_norm(values_in, gain):
    row_mean = jnp.mean(values_in, axis=-1, keepdims=True)
    centred = values_in - row_mean
    row_var = jnp.mean(centred * centred, axis=-1, keepdims=True)
    return centred * lax.rsqrt(row_var + norm_eps) * gain


def norm_back(partial_grad, rows_full, gain_full, gain_share):
    local_width = gain_share.shape[0]
    model_width = gain_full.shape[0]
    row_mean = jnp.mean(rows_full, axis=-1, keepdims=True)
    centred = rows_full - row_mean
    row_inv = lax.rsqrt(jnp.mean(centred * centred, axis=-1, keepdims=True) + norm_eps)
    scaled = partial_grad * gain_full
    sums = lax.psum(
        jnp.stack(
            [jnp.sum(scaled, axis=-1), jnp.sum(scaled * (centred * row_inv), axis=-1)]
        ),
        "head",
    )
    means = (sums / model_width)[:, :, None]
    share = lax.psum_scatter(partial_grad, "head", scatter_dimension=1, tiled=True)
    start = lax.axis_index("head") * local_width
    xhat = lax.dynamic_slice_in_dim(centred, start, local_width, 1) * row_inv
    back = (share * gain_share - means[0] - xhat * means[1]) * row_inv
    return back, jnp.sum(share * xhat, axis=0)


def mlp_act(values_in):
    return jax.nn.gelu(values_in, approximate=True)


def block_attend(query_proj, key_proj, value_proj, prior_state, prior_total):
    query_feat = feature(query_proj)
    key_feat = feature(key_proj)
    length_now = query_proj.shape[1]
    scores = jnp.einsum("gihe,gjhe->ghij", query_feat, key_feat, precision=highest)
    row_index = lax.broadcasted_iota(jnp.int32, (length_now, length_now), 0)
    col_index = lax.broadcasted_iota(jnp.int32, (length_now, length_now), 1)
    scores = jnp.where(col_index <= row_index, scores, jnp.float32(0.0))
    numerator = jnp.einsum("ghij,gjhe->gihe", scores, value_proj, precision=highest)
    numerator = numerator + jnp.einsum(
        "gihe,ghef->gihf", query_feat, prior_state, precision=highest
    )
    denominator = jnp.sum(scores, axis=-1) + jnp.einsum(
        "gihe,ghe->ghi", query_feat, prior_total, precision=highest
    )
    return numerator / jnp.transpose(denominator, (0, 2, 1))[..., None]


def block_state(key_proj, value_proj):
    key_feat = feature(key_proj)
    kv_sum = jnp.einsum("gihe,gihf->ghef", key_feat, value_proj, precision=highest)
    return (kv_sum, jnp.sum(key_feat, axis=1))


def add_pair(earlier, later):
    return (earlier[0] + later[0], earlier[1] + later[1])


def per_device(
    tokens,
    gain_attn,
    qkv_weight,
    out_weight,
    gain_ffn,
    up_weight,
    up_bias,
    down_weight,
    down_bias,
    out_grad,
):
    image_count, block_len, local_width = tokens.shape
    row_count = image_count * block_len
    model_width = qkv_weight.shape[0]
    heads_local = local_width // HEAD_DIM
    column_start = lax.axis_index("head") * local_width
    full_tokens, gain_first, gain_second = (
        lax.all_gather(tokens, "head", axis=2, tiled=True),
        lax.all_gather(gain_attn, "head", axis=0, tiled=True),
        lax.all_gather(gain_ffn, "head", axis=0, tiled=True),
    )
    token_rows = full_tokens.reshape(row_count, model_width)
    normed_one = layer_norm(token_rows, gain_first)
    proj_weight = qkv_weight.reshape(model_width, 3 * local_width)
    projected = jnp.dot(normed_one, proj_weight, precision=highest)
    parts_view = projected.reshape(image_count, block_len, 3, heads_local, HEAD_DIM)
    query_proj = parts_view[:, :, 0]
    key_proj = parts_view[:, :, 1]
    value_proj = parts_view[:, :, 2]
    (own_state, own_total), pull_state = jax.vjp(block_state, key_proj, value_proj)
    zero_pair = (jnp.zeros_like(own_state), jnp.zeros_like(own_total))
    prior_state, prior_total = entering((own_state, own_total), "seq", add_pair, zero_pair, False)
    mixed, pull_attend = jax.vjp(
        block_attend, query_proj, key_proj, value_proj, prior_state, prior_total
    )
    mixed_rows = mixed.reshape(row_count, local_width)
    branch_out = jnp.dot(mixed_rows, out_weight, precision=highest)
    token_share = tokens.reshape(row_count, local_width)
    resid_share = token_share + lax.psum_scatter(
        branch_out, "head", scatter_dimension=1, tiled=True
    )
    resid_full = lax.all_gather(resid_share, "head", axis=1, tiled=True)
    normed_two = layer_norm(resid_full, gain_second)
    up_proj = jnp.dot(normed_two, up_weight, precision=highest) + up_bias
    hidden, pull_act = jax.vjp(mlp_act, up_proj)
    down_proj = jnp.dot(hidden, down_weight, precision=highest)
    ffn_share = lax.psum_scatter(down_proj, "head", scatter_dimension=1, tiled=True)
    output = (resid_share + ffn_share + down_bias).reshape(tokens.shape)
    grad_share = out_grad.reshape(row_count, local_width)
    grad_full = lax.all_gather(grad_share, "head", axis=1, tiled=True)
    down_bias_grad = jnp.sum(grad_share, axis=0)
    down_weight_grad = jnp.dot(hidden.T, grad_full, precision=highest)
    hidden_grad = jnp.dot(grad_full, down_weight.T, precision=highest)
    (up_grad,) = pull_act(hidden_grad)
    up_bias_grad = jnp.sum(up_grad, axis=0)
    up_weight_grad = jnp.dot(normed_two.T, up_grad, precision=highest)
    ffn_grads = lax.psum((up_weight_grad, down_weight_grad), ("seq", "dp"))
    resid_back, gain_ffn_share = norm_back(
        jnp.dot(up_grad, up_weight.T, precision=highest), resid_full, gain_second, gain_ffn
    )
    resid_grad_share = grad_share + resid_back
    resid_grad = lax.all_gather(resid_grad_share, "head", axis=1, tiled=True)
    out_weight_grad = jnp.dot(mixed_rows.T, resid_grad, precision=highest)
    mixed_grad = jnp.dot(resid_grad, out_weight.T, precision=highest).reshape(mixed.shape)
    query_grad, key_grad, value_grad, state_grad, total_grad = pull_attend(mixed_grad)
    later_state, later_total = entering((state_grad, total_grad), "seq", add_pair, zero_pair, True)
    key_extra, value_extra = pull_state((later_state, later_total))
    key_grad = key_grad + key_extra
    value_grad = value_grad + value_extra
    proj_grad = jnp.stack([query_grad, key_grad, value_grad], axis=2).reshape(
        row_count, 3 * local_width
    )
    qkv_weight_grad = jnp.dot(normed_one.T, proj_grad, precision=highest).reshape(qkv_weight.shape)
    token_back, gain_attn_share = norm_back(
        jnp.dot(proj_grad, proj_weight.T, precision=highest), token_rows, gain_first, gain_attn
    )
    tokens_grad = (resid_grad_share + token_back).reshape(tokens.shape)
    summed_grads = lax.psum(
        (
            gain_attn_share,
            qkv_weight_grad,
            out_weight_grad,
            gain_ffn_share,
            up_bias_grad,
            down_bias_grad,
        ),
        ("seq", "dp"),
    )
    return (
        output,
        tokens_grad,
        summed_grads[0],
        summed_grads[1],
        summed_grads[2],
        summed_grads[3],
        ffn_grads[0],
        summed_grads[4],
        ffn_grads[1],
        summed_grads[5],
    )


MESH = pl.DeviceIdType.MESH
BF = jnp.bfloat16
F32 = jnp.float32
LANES = 256
DIMS = {
    "nn": (((1,), (0,)), ((), ())),
    "nt": (((1,), (1,)), ((), ())),
    "tn": (((0,), (0,)), ((), ())),
}


def round_up(value, step):
    return -(-value // step) * step


def dot(left, right, kind):
    return lax.dot_general(left, right, DIMS[kind], preferred_element_type=F32)


def split(values):
    high = values.astype(BF)
    return high, (values - high.astype(F32)).astype(BF)


def dot3(left, right, kind):
    return (
        dot(left[0], right[0], kind) + dot(left[0], right[1], kind) + dot(left[1], right[0], kind)
    )


def dot2(left, right, kind):
    return dot(left[0], right, kind) + dot(left[1], right, kind)


def lanes(index):
    if isinstance(index, int):
        return pl.ds(index * LANES, LANES)
    return pl.ds(pl.multiple_of(index * LANES, LANES), LANES)


def place():
    z, h, c = lax.axis_index("seq"), lax.axis_index("head"), lax.axis_index("dp")
    near_x = h + 1 - 2 * lax.rem(h, 2)
    near_y = lax.rem(h + 2, 4)
    return z, h, c, near_x, near_y, 3 - h


def remote(src, dst, send, recv, device):
    return pltpu.make_async_remote_copy(
        src_ref=src, dst_ref=dst, send_sem=send, recv_sem=recv, device_id=device, device_id_type=MESH
    )


def enter(targets):
    barrier = pltpu.get_barrier_semaphore()
    for device in targets:
        pl.semaphore_signal(barrier, inc=1, device_id=device, device_id_type=MESH)
    pl.semaphore_wait(barrier, len(targets))


class Gather:
    SEMS = 8

    def __init__(self, own, slots, rows, sems):
        self.own, self.slots, self.sems = own, slots, sems
        self.half = round_up(rows // 2, 8)
        self.rows = rows

    def copies(self, i):
        _, h, _, near_x, near_y, _ = place()
        slots, sems = self.slots, self.sems
        first, second = pl.ds(0, self.half), pl.ds(self.half, self.rows - self.half)
        every = pl.ds(0, self.rows)

        def one(src, dst, place_in, device):
            return remote(src, dst, sems.at[i, place_in], sems.at[i, 4 + place_in], {"head": device})

        own = self.own(i)
        return (
            one(own.at[every], slots.at[i, every, lanes(h)], 0, near_x),
            one(own.at[every], slots.at[i, every, lanes(h)], 1, near_y),
            one(slots.at[i, first, lanes(near_x)], slots.at[i, first, lanes(near_x)], 2, near_y),
            one(slots.at[i, second, lanes(near_y)], slots.at[i, second, lanes(near_y)], 3, near_x),
        )

    def arrivals(self, i):
        _, h, _, near_x, near_y, far = place()
        slots, sems = self.slots, self.sems
        first, second = pl.ds(0, self.half), pl.ds(self.half, self.rows - self.half)
        every = pl.ds(0, self.rows)

        def one(dst, place_in, device):
            return remote(dst, dst, sems.at[i, place_in], sems.at[i, 4 + place_in], {"head": device})

        return (
            one(slots.at[i, every, lanes(near_x)], 0, near_x),
            one(slots.at[i, every, lanes(near_y)], 1, near_y),
            one(slots.at[i, first, lanes(far)], 2, near_y),
            one(slots.at[i, second, lanes(far)], 3, near_x),
        )

    def direct(self, i):
        x, y, _, _ = self.copies(i)
        x.start()
        y.start()

    def forward(self, i):
        x, y, _, _ = self.arrivals(i)
        x.wait_recv()
        y.wait_recv()
        _, _, to_y, to_x = self.copies(i)
        to_y.start()
        to_x.start()

    def ready(self, i):
        _, _, x, y = self.arrivals(i)
        x.wait_recv()
        y.wait_recv()

    def finish(self, i):
        for copy in self.copies(i):
            copy.wait_send()


def head_masks(rows):
    head = lax.broadcasted_iota(jnp.int32, (rows, LANES), 1) // HEAD_DIM
    return [head == k for k in range(LANES // HEAD_DIM)]


def diagonal_mask():
    rows = lax.broadcasted_iota(jnp.int32, (LANES, LANES), 0) // HEAD_DIM
    cols = lax.broadcasted_iota(jnp.int32, (LANES, LANES), 1) // HEAD_DIM
    return rows == cols


def pick(mask, pair):
    zero = jnp.zeros((), BF)
    return jnp.where(mask, pair[0], zero), jnp.where(mask, pair[1], zero)


def fold(square):
    square = jnp.where(diagonal_mask(), square, 0.0)
    return (
        square[0:HEAD_DIM]
        + square[HEAD_DIM : 2 * HEAD_DIM]
        + square[2 * HEAD_DIM : 3 * HEAD_DIM]
        + square[3 * HEAD_DIM :]
    )


def unfold(wide):
    return jnp.where(diagonal_mask(), jnp.concatenate([wide] * 4, axis=0), 0.0)


def positive(values):
    return jnp.where(values > 0, values + 1.0, jnp.exp(jnp.minimum(values, 0.0)))


def norm_parts(rows):
    row_mean = jnp.mean(rows, axis=-1, keepdims=True)
    centred = rows - row_mean
    row_inv = lax.rsqrt(jnp.mean(centred * centred, axis=-1, keepdims=True) + norm_eps)
    return centred * row_inv, row_inv


def split_rows(source, high, low, rows, step):
    def one(r, _):
        s = pl.ds(pl.multiple_of(r * step, step), step)
        high[s, :], low[s, :] = split(source[s, :])
        return 0

    lax.fori_loop(0, rows // step, one, 0)


STATE = HEAD_DIM + 8


def attend_kernel(
    dims,
    tok_in, gains_in, wqkv_in, wout_in,
    tok_out, gains_out, proj_out, den_out, prior_out, mix_out, wout_out,
    tok, mix, gains, proj, den, prior, state, state_in, wstage, w_h, w_l, n_h, n_l, wout,
    tok_sem, mix_sem, gain_sem, state_sem, out_sem, pair_sem, load_sem, store_sem,
):
    images, length, used, rows = dims
    width = tok.shape[2]
    z, h, c, near_x, near_y, far = place()
    seq = lax.axis_size("seq")
    out_half = wout_in.shape[0] // 2

    loads = [
        pltpu.make_async_copy(tok_in.at[i], tok.at[i, :, lanes(h)], load_sem.at[i])
        for i in range(images)
    ]
    loads.append(pltpu.make_async_copy(wqkv_in, wstage, load_sem.at[images]))
    loads.append(pltpu.make_async_copy(gains_in, gains.at[:, lanes(h)], load_sem.at[images + 1]))
    for copy in loads:
        copy.start()

    blank = jnp.zeros((rows - used, LANES), F32)
    for i in range(images):
        for other in (near_x, near_y, far):
            tok[i, used:rows, lanes(other)] = blank

    enter(
        [{"head": near_x}, {"head": near_y}, {"head": far}, {"dp": 1 - c}]
        + [{"seq": lax.rem(z + d, seq)} for d in range(1, seq)]
    )
    tokens = Gather(lambda i: tok_in.at[i], tok, used, tok_sem)
    mixes = Gather(lambda i: mix.at[i, :, lanes(h)], mix, used, mix_sem)
    own_half = pl.ds(pl.multiple_of(c * out_half, out_half), out_half)
    tokens.direct(0)
    gain_copies = [
        remote(gains_in, gains.at[:, lanes(h)], gain_sem.at[k], gain_sem.at[3 + k], {"head": other})
        for k, other in enumerate((near_x, near_y, far))
    ]
    for copy in gain_copies:
        copy.start()
    tokens.direct(1)
    loads[images].wait()
    split_rows(wstage, w_h, w_l, width, 16)
    loads[images + 1].wait()
    for k, other in enumerate((near_x, near_y, far)):
        remote(
            gains.at[:, lanes(other)], gains.at[:, lanes(other)], gain_sem.at[k], gain_sem.at[3 + k],
            {"head": other},
        ).wait_recv()
    row_ok = lax.broadcasted_iota(jnp.int32, (rows, LANES), 0) < length

    def project(i):
        loads[i].wait()

        def normed(r, _):
            s = pl.ds(pl.multiple_of(r * 16, 16), 16)
            xhat, _unused = norm_parts(tok[i, s, :])
            n_h[s, :], n_l[s, :] = split(xhat * gains[0:1, :])
            return 0

        lax.fori_loop(0, rows // 16, normed, 0)

        def column(k, _):
            s = lanes(k)
            proj[i, :, s] = dot3((n_h[...], n_l[...]), (w_h[:, s], w_l[:, s]), "nn")
            return 0

        lax.fori_loop(0, 3, column, 0)
        key_feat = jnp.where(row_ok, positive(proj[i, :, lanes(1)]), 0.0)
        state[i, 0:HEAD_DIM, :] = fold(dot3(split(key_feat), split(proj[i, :, lanes(2)]), "tn"))
        state[i, HEAD_DIM:, :] = jnp.broadcast_to(
            jnp.sum(key_feat, axis=0, keepdims=True), (STATE - HEAD_DIM, LANES)
        )
        for d in range(1, seq):

            @pl.when(z + d < seq)
            def _():
                state_copy(i, d, d).start()

    def state_copy(i, d, step):
        return remote(
            state.at[i], state_in.at[d - 1, i], state_sem.at[0, d - 1, i], state_sem.at[1, d - 1, i],
            {"seq": lax.rem(z + step + seq, seq)},
        )

    def attend(i):
        prior[i] = jnp.zeros((STATE, LANES), F32)
        for d in range(1, seq):

            @pl.when(z >= d)
            def _():
                state_copy(i, d, -d).wait_recv()
                prior[i] = prior[i] + state_in[d - 1, i]

        query_feat = positive(proj[i, :, lanes(0)])
        key_feat = jnp.where(row_ok, positive(proj[i, :, lanes(1)]), 0.0)
        query_pair, key_pair = split(query_feat), split(key_feat)
        value_pair = split(proj[i, :, lanes(2)])
        total = prior[i, HEAD_DIM : HEAD_DIM + 1, :]
        ones = jnp.where(diagonal_mask(), 1.0, 0.0).astype(BF)
        num = dot3(query_pair, split(unfold(prior[i, 0:HEAD_DIM, :])), "nn")
        below = dot2(split(query_feat * total), ones, "nn")
        row = lax.broadcasted_iota(jnp.int32, (rows, rows), 0)
        col = lax.broadcasted_iota(jnp.int32, (rows, rows), 1)
        for mask in head_masks(rows):
            scores = dot3(query_pair, pick(mask, key_pair), "nt")
            score_pair = split(jnp.where(col <= row, scores, 0.0))
            num = num + dot3(score_pair, pick(mask, value_pair), "nn")
            below = below + dot2(score_pair, jnp.where(mask, 1.0, 0.0).astype(BF), "nn")
        den[i] = below
        mix[i, :, lanes(h)] = jnp.where(row_ok, num / below, 0.0)
        blank_rows = jnp.zeros((rows - used, LANES), F32)
        for other in (near_x, near_y, far):
            mix[i, used:rows, lanes(other)] = blank_rows

    out_copies = [
        remote(
            wout_in.at[own_half], wout.at[h, own_half], out_sem.at[0, k], out_sem.at[1, k], {"head": other}
        )
        for k, other in enumerate((near_x, near_y, far))
    ]
    out_own = pltpu.make_async_copy(wout_in, wout.at[h], load_sem.at[images + 2])

    def out_arrival(k, other):
        return remote(
            wout.at[other, own_half], wout.at[other, own_half], out_sem.at[0, k], out_sem.at[1, k],
            {"head": other},
        )

    def pair_copy(k, other, which):
        half = pl.ds(pl.multiple_of(which * out_half, out_half), out_half)
        return remote(
            wout.at[other, half], wout.at[other, half], pair_sem.at[0, k], pair_sem.at[1, k],
            {"dp": 1 - c},
        )

    peers = tuple(enumerate((near_x, near_y, far)))
    stores = []

    def store(src, dst):
        copy = pltpu.make_async_copy(src, dst, store_sem.at[len(stores)])
        copy.start()
        stores.append(copy)

    for t in range(images + 2):
        if t < images:
            tokens.forward(t)
            if t + 2 < images:
                tokens.direct(t + 2)
            elif t == images - 1:
                for copy in out_copies:
                    copy.start()
                out_own.start()
        if 1 <= t <= images:
            tokens.ready(t - 1)
            project(t - 1)
            store(tok.at[t - 1], tok_out.at[t - 1])
            store(proj.at[t - 1], proj_out.at[t - 1])
        if t >= 2:
            attend(t - 2)
            mixes.direct(t - 2)
            store(den.at[t - 2], den_out.at[t - 2])
            store(prior.at[t - 2], prior_out.at[t - 2])
    store(gains, gains_out)
    out_own.wait()
    for k, other in peers:
        out_arrival(k, other).wait_recv()
        pair_copy(k, other, c).start()
    for i in range(images):
        mixes.forward(i)
    for k, other in peers:
        pair_copy(k, other, 1 - c).wait_recv()
    store(wout, wout_out)
    for i in range(images):
        mixes.ready(i)
        store(mix.at[i], mix_out.at[i])
    for i in range(images):
        tokens.finish(i)
        mixes.finish(i)
        for d in range(1, seq):

            @pl.when(z + d < seq)
            def _(i=i, d=d):
                state_copy(i, d, d).wait_send()

    for copy in gain_copies + out_copies:
        copy.wait_send()
    for k, other in peers:
        pair_copy(k, other, c).wait_send()
    for copy in stores:
        copy.wait()


def attend_call(tokens, gains, wqkv, wout, length):
    images, rows, _ = tokens.shape
    used = round_up(length, 8)
    width = wqkv.shape[0]
    heads_n = width // LANES
    dma = pltpu.SemaphoreType.DMA
    seq = lax.axis_size("seq")
    any_spec = pl.BlockSpec(memory_space=pl.ANY)
    shape = lambda *s: jax.ShapeDtypeStruct(s, F32)
    return pl.pallas_call(
        functools.partial(attend_kernel, (images, length, used, rows)),
        out_shape=(
            shape(images, rows, width),
            shape(8, width),
            shape(images, rows, 3 * LANES),
            shape(images, rows, LANES),
            shape(images, STATE, LANES),
            shape(images, rows, width),
            shape(heads_n, LANES, width),
        ),
        in_specs=[any_spec] * 4,
        out_specs=(any_spec,) * 7,
        scratch_shapes=[
            pltpu.VMEM((images, rows, width), F32),
            pltpu.VMEM((images, rows, width), F32),
            pltpu.VMEM((8, width), F32),
            pltpu.VMEM((images, rows, 3 * LANES), F32),
            pltpu.VMEM((images, rows, LANES), F32),
            pltpu.VMEM((images, STATE, LANES), F32),
            pltpu.VMEM((images, STATE, LANES), F32),
            pltpu.VMEM((seq - 1, images, STATE, LANES), F32),
            pltpu.VMEM((width, 3 * LANES), F32),
            pltpu.VMEM((width, 3 * LANES), BF),
            pltpu.VMEM((width, 3 * LANES), BF),
            pltpu.VMEM((rows, width), BF),
            pltpu.VMEM((rows, width), BF),
            pltpu.VMEM((heads_n, LANES, width), F32),
            dma((images, Gather.SEMS)),
            dma((images, Gather.SEMS)),
            dma((6,)),
            dma((2, seq - 1, images)),
            dma((2, 3)),
            dma((2, 3)),
            dma((images + 3,)),
            dma((5 * images + 4,)),
        ],
        compiler_params=pltpu.CompilerParams(
            collective_id=0, has_side_effects=True, vmem_limit_bytes=VMEM_BYTES
        ),
    )(tokens, gains, wqkv, wout)


VMEM_BYTES = 60 * 1024 * 1024


def fast_device(
    tokens,
    gain_attn,
    qkv_weight,
    out_weight,
    gain_ffn,
    up_weight,
    up_bias,
    down_weight,
    down_bias,
    out_grad,
):
    image_count, block_len, local_width = tokens.shape
    row_count = image_count * block_len
    model_width = qkv_weight.shape[0]
    heads_local = local_width // HEAD_DIM
    rows = round_up(round_up(block_len, 8) + 8, 16)
    column_start = lax.axis_index("head") * local_width
    pad = ((0, 0), (0, rows - block_len), (0, 0))
    proj_weight = qkv_weight.reshape(model_width, 3 * local_width)
    gains_in = jnp.concatenate([gain_attn[None], gain_ffn[None], jnp.zeros((6, local_width), jnp.float32)])
    tok, gains, proj, den, prior, mix, wout = attend_call(
        jnp.pad(tokens, pad), gains_in, proj_weight, out_weight, block_len
    )
    gain_first, gain_second = gains[0], gains[1]
    token_rows = tok[:, :block_len].reshape(row_count, model_width)
    normed_one = layer_norm(token_rows, gain_first)
    parts_view = proj[:, :block_len].reshape(image_count, block_len, 3, heads_local, HEAD_DIM)
    query_proj = parts_view[:, :, 0]
    key_proj = parts_view[:, :, 1]
    value_proj = parts_view[:, :, 2]
    (own_state, own_total), pull_state = jax.vjp(block_state, key_proj, value_proj)
    zero_pair = (jnp.zeros_like(own_state), jnp.zeros_like(own_total))
    prior_state = prior[:, :HEAD_DIM].reshape(image_count, HEAD_DIM, heads_local, HEAD_DIM).transpose(0, 2, 1, 3)
    prior_total = prior[:, HEAD_DIM].reshape(image_count, heads_local, HEAD_DIM)
    mixed, pull_attend = jax.vjp(
        block_attend, query_proj, key_proj, value_proj, prior_state, prior_total
    )
    mixed_full = mix[:, :block_len].reshape(row_count, model_width)
    mixed_rows = lax.dynamic_slice_in_dim(mixed_full, column_start, local_width, 1)
    resid_full = token_rows + jnp.dot(mixed_full, wout.reshape(model_width, model_width), precision=highest)
    resid_share = lax.dynamic_slice_in_dim(resid_full, column_start, local_width, 1)
    normed_two = layer_norm(resid_full, gain_second)
    up_proj = jnp.dot(normed_two, up_weight, precision=highest) + up_bias
    hidden, pull_act = jax.vjp(mlp_act, up_proj)
    down_proj = jnp.dot(hidden, down_weight, precision=highest)
    ffn_share = lax.psum_scatter(down_proj, "head", scatter_dimension=1, tiled=True)
    output = (resid_share + ffn_share + down_bias).reshape(tokens.shape)
    grad_share = out_grad.reshape(row_count, local_width)
    grad_full = lax.all_gather(grad_share, "head", axis=1, tiled=True)
    down_bias_grad = jnp.sum(grad_share, axis=0)
    down_weight_grad = jnp.dot(hidden.T, grad_full, precision=highest)
    hidden_grad = jnp.dot(grad_full, down_weight.T, precision=highest)
    (up_grad,) = pull_act(hidden_grad)
    up_bias_grad = jnp.sum(up_grad, axis=0)
    up_weight_grad = jnp.dot(normed_two.T, up_grad, precision=highest)
    ffn_grads = lax.psum((up_weight_grad, down_weight_grad), ("seq", "dp"))
    resid_back, gain_ffn_share = norm_back(
        jnp.dot(up_grad, up_weight.T, precision=highest), resid_full, gain_second, gain_ffn
    )
    resid_grad_share = grad_share + resid_back
    resid_grad = lax.all_gather(resid_grad_share, "head", axis=1, tiled=True)
    out_weight_grad = jnp.dot(mixed_rows.T, resid_grad, precision=highest)
    mixed_grad = jnp.dot(resid_grad, out_weight.T, precision=highest).reshape(mixed.shape)
    query_grad, key_grad, value_grad, state_grad, total_grad = pull_attend(mixed_grad)
    later_state, later_total = entering((state_grad, total_grad), "seq", add_pair, zero_pair, True)
    key_extra, value_extra = pull_state((later_state, later_total))
    key_grad = key_grad + key_extra
    value_grad = value_grad + value_extra
    proj_grad = jnp.stack([query_grad, key_grad, value_grad], axis=2).reshape(
        row_count, 3 * local_width
    )
    qkv_weight_grad = jnp.dot(normed_one.T, proj_grad, precision=highest).reshape(qkv_weight.shape)
    token_back, gain_attn_share = norm_back(
        jnp.dot(proj_grad, proj_weight.T, precision=highest), token_rows, gain_first, gain_attn
    )
    tokens_grad = (resid_grad_share + token_back).reshape(tokens.shape)
    summed_grads = lax.psum(
        (
            gain_attn_share,
            qkv_weight_grad,
            out_weight_grad,
            gain_ffn_share,
            up_bias_grad,
            down_bias_grad,
        ),
        ("seq", "dp"),
    )
    return (
        output,
        tokens_grad,
        summed_grads[0],
        summed_grads[1],
        summed_grads[2],
        summed_grads[3],
        ffn_grads[0],
        summed_grads[4],
        ffn_grads[1],
        summed_grads[5],
    )


def device_function(mesh):
    if mesh.shape["head"] == 4 and mesh.shape["dp"] == 2:
        return fast_device
    return per_device


def solution(mesh):
    return jax.shard_map(
        device_function(mesh),
        mesh=mesh,
        in_specs=(
            P("dp", "seq", "head"),
            P("head"),
            P(None, None, "head"),
            P("head", None),
            P("head"),
            P(None, "head"),
            P("head"),
            P("head", None),
            P("head"),
            P("dp", "seq", "head"),
        ),
        out_specs=(
            P("dp", "seq", "head"),
            P("dp", "seq", "head"),
            P("head"),
            P(None, None, "head"),
            P("head", None),
            P("head"),
            P(None, "head"),
            P("head"),
            P("head", None),
            P("head"),
        ),
        check_vma=False,
    )
```

```python
import functools

import jax
import jax.numpy as jnp
from jax import lax
from jax.experimental import pallas as pl
from jax.experimental.pallas import tpu as pltpu
from jax.sharding import PartitionSpec as P

HEAD_DIM = 64


highest = lax.Precision.HIGH
norm_eps = 1e-05


def entering(part, axis, combine, identity, reverse):
    count = lax.axis_size(axis)
    place = lax.axis_index(axis)
    ahead = count - 1 - place if reverse else place
    gathered = jax.tree.map(lambda a: lax.all_gather(a, axis), part)
    state = jax.tree.map(lambda a, e: jnp.zeros_like(a) + jnp.asarray(e, a.dtype), part, identity)

    def one(turn, state):
        source = count - 1 - turn if reverse else turn
        return combine(
            state, jax.tree.map(lambda a: lax.dynamic_index_in_dim(a, source, 0, False), gathered)
        )

    return lax.fori_loop(0, ahead, one, state)


def feature(values_in):
    return jax.nn.elu(values_in) + 1.0


def layer_norm(values_in, gain):
    row_mean = jnp.mean(values_in, axis=-1, keepdims=True)
    centred = values_in - row_mean
    row_var = jnp.mean(centred * centred, axis=-1, keepdims=True)
    return centred * lax.rsqrt(row_var + norm_eps) * gain


def norm_back(partial_grad, rows_full, gain_full, gain_share):
    local_width = gain_share.shape[0]
    model_width = gain_full.shape[0]
    row_mean = jnp.mean(rows_full, axis=-1, keepdims=True)
    centred = rows_full - row_mean
    row_inv = lax.rsqrt(jnp.mean(centred * centred, axis=-1, keepdims=True) + norm_eps)
    scaled = partial_grad * gain_full
    sums = lax.psum(
        jnp.stack(
            [jnp.sum(scaled, axis=-1), jnp.sum(scaled * (centred * row_inv), axis=-1)]
        ),
        "head",
    )
    means = (sums / model_width)[:, :, None]
    share = lax.psum_scatter(partial_grad, "head", scatter_dimension=1, tiled=True)
    start = lax.axis_index("head") * local_width
    xhat = lax.dynamic_slice_in_dim(centred, start, local_width, 1) * row_inv
    back = (share * gain_share - means[0] - xhat * means[1]) * row_inv
    return back, jnp.sum(share * xhat, axis=0)


def mlp_act(values_in):
    return jax.nn.gelu(values_in, approximate=True)


def block_attend(query_proj, key_proj, value_proj, prior_state, prior_total):
    query_feat = feature(query_proj)
    key_feat = feature(key_proj)
    length_now = query_proj.shape[1]
    scores = jnp.einsum("gihe,gjhe->ghij", query_feat, key_feat, precision=highest)
    row_index = lax.broadcasted_iota(jnp.int32, (length_now, length_now), 0)
    col_index = lax.broadcasted_iota(jnp.int32, (length_now, length_now), 1)
    scores = jnp.where(col_index <= row_index, scores, jnp.float32(0.0))
    numerator = jnp.einsum("ghij,gjhe->gihe", scores, value_proj, precision=highest)
    numerator = numerator + jnp.einsum(
        "gihe,ghef->gihf", query_feat, prior_state, precision=highest
    )
    denominator = jnp.sum(scores, axis=-1) + jnp.einsum(
        "gihe,ghe->ghi", query_feat, prior_total, precision=highest
    )
    return numerator / jnp.transpose(denominator, (0, 2, 1))[..., None]


def block_state(key_proj, value_proj):
    key_feat = feature(key_proj)
    kv_sum = jnp.einsum("gihe,gihf->ghef", key_feat, value_proj, precision=highest)
    return (kv_sum, jnp.sum(key_feat, axis=1))


def add_pair(earlier, later):
    return (earlier[0] + later[0], earlier[1] + later[1])


def per_device(
    tokens,
    gain_attn,
    qkv_weight,
    out_weight,
    gain_ffn,
    up_weight,
    up_bias,
    down_weight,
    down_bias,
    out_grad,
):
    image_count, block_len, local_width = tokens.shape
    row_count = image_count * block_len
    model_width = qkv_weight.shape[0]
    heads_local = local_width // HEAD_DIM
    column_start = lax.axis_index("head") * local_width
    full_tokens, gain_first, gain_second = (
        lax.all_gather(tokens, "head", axis=2, tiled=True),
        lax.all_gather(gain_attn, "head", axis=0, tiled=True),
        lax.all_gather(gain_ffn, "head", axis=0, tiled=True),
    )
    token_rows = full_tokens.reshape(row_count, model_width)
    normed_one = layer_norm(token_rows, gain_first)
    proj_weight = qkv_weight.reshape(model_width, 3 * local_width)
    projected = jnp.dot(normed_one, proj_weight, precision=highest)
    parts_view = projected.reshape(image_count, block_len, 3, heads_local, HEAD_DIM)
    query_proj = parts_view[:, :, 0]
    key_proj = parts_view[:, :, 1]
    value_proj = parts_view[:, :, 2]
    (own_state, own_total), pull_state = jax.vjp(block_state, key_proj, value_proj)
    zero_pair = (jnp.zeros_like(own_state), jnp.zeros_like(own_total))
    prior_state, prior_total = entering((own_state, own_total), "seq", add_pair, zero_pair, False)
    mixed, pull_attend = jax.vjp(
        block_attend, query_proj, key_proj, value_proj, prior_state, prior_total
    )
    mixed_rows = mixed.reshape(row_count, local_width)
    branch_out = jnp.dot(mixed_rows, out_weight, precision=highest)
    token_share = tokens.reshape(row_count, local_width)
    resid_share = token_share + lax.psum_scatter(
        branch_out, "head", scatter_dimension=1, tiled=True
    )
    resid_full = lax.all_gather(resid_share, "head", axis=1, tiled=True)
    normed_two = layer_norm(resid_full, gain_second)
    up_proj = jnp.dot(normed_two, up_weight, precision=highest) + up_bias
    hidden, pull_act = jax.vjp(mlp_act, up_proj)
    down_proj = jnp.dot(hidden, down_weight, precision=highest)
    ffn_share = lax.psum_scatter(down_proj, "head", scatter_dimension=1, tiled=True)
    output = (resid_share + ffn_share + down_bias).reshape(tokens.shape)
    grad_share = out_grad.reshape(row_count, local_width)
    grad_full = lax.all_gather(grad_share, "head", axis=1, tiled=True)
    down_bias_grad = jnp.sum(grad_share, axis=0)
    down_weight_grad = jnp.dot(hidden.T, grad_full, precision=highest)
    hidden_grad = jnp.dot(grad_full, down_weight.T, precision=highest)
    (up_grad,) = pull_act(hidden_grad)
    up_bias_grad = jnp.sum(up_grad, axis=0)
    up_weight_grad = jnp.dot(normed_two.T, up_grad, precision=highest)
    ffn_grads = lax.psum((up_weight_grad, down_weight_grad), ("seq", "dp"))
    resid_back, gain_ffn_share = norm_back(
        jnp.dot(up_grad, up_weight.T, precision=highest), resid_full, gain_second, gain_ffn
    )
    resid_grad_share = grad_share + resid_back
    resid_grad = lax.all_gather(resid_grad_share, "head", axis=1, tiled=True)
    out_weight_grad = jnp.dot(mixed_rows.T, resid_grad, precision=highest)
    mixed_grad = jnp.dot(resid_grad, out_weight.T, precision=highest).reshape(mixed.shape)
    query_grad, key_grad, value_grad, state_grad, total_grad = pull_attend(mixed_grad)
    later_state, later_total = entering((state_grad, total_grad), "seq", add_pair, zero_pair, True)
    key_extra, value_extra = pull_state((later_state, later_total))
    key_grad = key_grad + key_extra
    value_grad = value_grad + value_extra
    proj_grad = jnp.stack([query_grad, key_grad, value_grad], axis=2).reshape(
        row_count, 3 * local_width
    )
    qkv_weight_grad = jnp.dot(normed_one.T, proj_grad, precision=highest).reshape(qkv_weight.shape)
    token_back, gain_attn_share = norm_back(
        jnp.dot(proj_grad, proj_weight.T, precision=highest), token_rows, gain_first, gain_attn
    )
    tokens_grad = (resid_grad_share + token_back).reshape(tokens.shape)
    summed_grads = lax.psum(
        (
            gain_attn_share,
            qkv_weight_grad,
            out_weight_grad,
            gain_ffn_share,
            up_bias_grad,
            down_bias_grad,
        ),
        ("seq", "dp"),
    )
    return (
        output,
        tokens_grad,
        summed_grads[0],
        summed_grads[1],
        summed_grads[2],
        summed_grads[3],
        ffn_grads[0],
        summed_grads[4],
        ffn_grads[1],
        summed_grads[5],
    )


MESH = pl.DeviceIdType.MESH
BF = jnp.bfloat16
F32 = jnp.float32
LANES = 256
DIMS = {
    "nn": (((1,), (0,)), ((), ())),
    "nt": (((1,), (1,)), ((), ())),
    "tn": (((0,), (0,)), ((), ())),
}


def round_up(value, step):
    return -(-value // step) * step


def dot(left, right, kind):
    return lax.dot_general(left, right, DIMS[kind], preferred_element_type=F32)


def split(values):
    high = values.astype(BF)
    return high, (values - high.astype(F32)).astype(BF)


def dot3(left, right, kind):
    return (
        dot(left[0], right[0], kind) + dot(left[0], right[1], kind) + dot(left[1], right[0], kind)
    )


def dot2(left, right, kind):
    return dot(left[0], right, kind) + dot(left[1], right, kind)


def lanes(index):
    if isinstance(index, int):
        return pl.ds(index * LANES, LANES)
    return pl.ds(pl.multiple_of(index * LANES, LANES), LANES)


def place():
    z, h, c = lax.axis_index("seq"), lax.axis_index("head"), lax.axis_index("dp")
    near_x = h + 1 - 2 * lax.rem(h, 2)
    near_y = lax.rem(h + 2, 4)
    return z, h, c, near_x, near_y, 3 - h


def remote(src, dst, send, recv, device):
    return pltpu.make_async_remote_copy(
        src_ref=src, dst_ref=dst, send_sem=send, recv_sem=recv, device_id=device, device_id_type=MESH
    )


def enter(targets):
    barrier = pltpu.get_barrier_semaphore()
    for device in targets:
        pl.semaphore_signal(barrier, inc=1, device_id=device, device_id_type=MESH)
    pl.semaphore_wait(barrier, len(targets))


class Gather:
    SEMS = 8

    def __init__(self, own, slots, rows, sems):
        self.own, self.slots, self.sems = own, slots, sems
        self.half = round_up(rows // 2, 8)
        self.rows = rows

    def copies(self, i):
        _, h, _, near_x, near_y, _ = place()
        slots, sems = self.slots, self.sems
        first, second = pl.ds(0, self.half), pl.ds(self.half, self.rows - self.half)
        every = pl.ds(0, self.rows)

        def one(src, dst, place_in, device):
            return remote(src, dst, sems.at[i, place_in], sems.at[i, 4 + place_in], {"head": device})

        own = self.own(i)
        return (
            one(own.at[every], slots.at[i, every, lanes(h)], 0, near_x),
            one(own.at[every], slots.at[i, every, lanes(h)], 1, near_y),
            one(slots.at[i, first, lanes(near_x)], slots.at[i, first, lanes(near_x)], 2, near_y),
            one(slots.at[i, second, lanes(near_y)], slots.at[i, second, lanes(near_y)], 3, near_x),
        )

    def arrivals(self, i):
        _, h, _, near_x, near_y, far = place()
        slots, sems = self.slots, self.sems
        first, second = pl.ds(0, self.half), pl.ds(self.half, self.rows - self.half)
        every = pl.ds(0, self.rows)

        def one(dst, place_in, device):
            return remote(dst, dst, sems.at[i, place_in], sems.at[i, 4 + place_in], {"head": device})

        return (
            one(slots.at[i, every, lanes(near_x)], 0, near_x),
            one(slots.at[i, every, lanes(near_y)], 1, near_y),
            one(slots.at[i, first, lanes(far)], 2, near_y),
            one(slots.at[i, second, lanes(far)], 3, near_x),
        )

    def direct(self, i):
        x, y, _, _ = self.copies(i)
        x.start()
        y.start()

    def forward(self, i):
        x, y, _, _ = self.arrivals(i)
        x.wait_recv()
        y.wait_recv()
        _, _, to_y, to_x = self.copies(i)
        to_y.start()
        to_x.start()

    def ready(self, i):
        _, _, x, y = self.arrivals(i)
        x.wait_recv()
        y.wait_recv()

    def finish(self, i):
        for copy in self.copies(i):
            copy.wait_send()


def head_masks(rows):
    head = lax.broadcasted_iota(jnp.int32, (rows, LANES), 1) // HEAD_DIM
    return [head == k for k in range(LANES // HEAD_DIM)]


def diagonal_mask():
    rows = lax.broadcasted_iota(jnp.int32, (LANES, LANES), 0) // HEAD_DIM
    cols = lax.broadcasted_iota(jnp.int32, (LANES, LANES), 1) // HEAD_DIM
    return rows == cols


def pick(mask, pair):
    zero = jnp.zeros((), BF)
    return jnp.where(mask, pair[0], zero), jnp.where(mask, pair[1], zero)


def fold(square):
    square = jnp.where(diagonal_mask(), square, 0.0)
    return (
        square[0:HEAD_DIM]
        + square[HEAD_DIM : 2 * HEAD_DIM]
        + square[2 * HEAD_DIM : 3 * HEAD_DIM]
        + square[3 * HEAD_DIM :]
    )


def unfold(wide):
    return jnp.where(diagonal_mask(), jnp.concatenate([wide] * 4, axis=0), 0.0)


def positive(values):
    return jnp.where(values > 0, values + 1.0, jnp.exp(jnp.minimum(values, 0.0)))


def norm_parts(rows):
    row_mean = jnp.mean(rows, axis=-1, keepdims=True)
    centred = rows - row_mean
    row_inv = lax.rsqrt(jnp.mean(centred * centred, axis=-1, keepdims=True) + norm_eps)
    return centred * row_inv, row_inv


def split_rows(source, high, low, rows, step):
    def one(r, _):
        s = pl.ds(pl.multiple_of(r * step, step), step)
        high[s, :], low[s, :] = split(source[s, :])
        return 0

    lax.fori_loop(0, rows // step, one, 0)


STATE = HEAD_DIM + 8


def attend_kernel(
    dims,
    tok_in, gains_in, wqkv_in, wout_in,
    tok_out, gains_out, proj_out, den_out, prior_out, mix_out, wout_out,
    tok, mix, gains, proj, den, prior, state, state_in, wstage, w_h, w_l, n_h, n_l, wout,
    tok_sem, mix_sem, gain_sem, state_sem, out_sem, pair_sem, load_sem, store_sem,
):
    images, length, used, rows = dims
    width = tok.shape[2]
    z, h, c, near_x, near_y, far = place()
    seq = lax.axis_size("seq")
    out_half = wout_in.shape[0] // 2

    loads = [
        pltpu.make_async_copy(tok_in.at[i], tok.at[i, :, lanes(h)], load_sem.at[i])
        for i in range(images)
    ]
    loads.append(pltpu.make_async_copy(wqkv_in, wstage, load_sem.at[images]))
    loads.append(pltpu.make_async_copy(gains_in, gains.at[:, lanes(h)], load_sem.at[images + 1]))
    for copy in loads:
        copy.start()

    blank = jnp.zeros((rows - used, LANES), F32)
    for i in range(images):
        for other in (near_x, near_y, far):
            tok[i, used:rows, lanes(other)] = blank

    enter(
        [{"head": near_x}, {"head": near_y}, {"head": far}, {"dp": 1 - c}]
        + [{"seq": lax.rem(z + d, seq)} for d in range(1, seq)]
    )
    tokens = Gather(lambda i: tok_in.at[i], tok, used, tok_sem)
    mixes = Gather(lambda i: mix.at[i, :, lanes(h)], mix, used, mix_sem)
    own_half = pl.ds(pl.multiple_of(c * out_half, out_half), out_half)
    tokens.direct(0)
    gain_copies = [
        remote(gains_in, gains.at[:, lanes(h)], gain_sem.at[k], gain_sem.at[3 + k], {"head": other})
        for k, other in enumerate((near_x, near_y, far))
    ]
    for copy in gain_copies:
        copy.start()
    tokens.direct(1)
    loads[images].wait()
    split_rows(wstage, w_h, w_l, width, 16)
    loads[images + 1].wait()
    for k, other in enumerate((near_x, near_y, far)):
        remote(
            gains.at[:, lanes(other)], gains.at[:, lanes(other)], gain_sem.at[k], gain_sem.at[3 + k],
            {"head": other},
        ).wait_recv()
    row_ok = lax.broadcasted_iota(jnp.int32, (rows, LANES), 0) < length

    def project(i):
        loads[i].wait()

        def normed(r, _):
            s = pl.ds(pl.multiple_of(r * 16, 16), 16)
            xhat, _unused = norm_parts(tok[i, s, :])
            n_h[s, :], n_l[s, :] = split(xhat * gains[0:1, :])
            return 0

        lax.fori_loop(0, rows // 16, normed, 0)

        def column(k, _):
            s = lanes(k)
            proj[i, :, s] = dot3((n_h[...], n_l[...]), (w_h[:, s], w_l[:, s]), "nn")
            return 0

        lax.fori_loop(0, 3, column, 0)
        key_feat = jnp.where(row_ok, positive(proj[i, :, lanes(1)]), 0.0)
        state[i, 0:HEAD_DIM, :] = fold(dot3(split(key_feat), split(proj[i, :, lanes(2)]), "tn"))
        state[i, HEAD_DIM:, :] = jnp.broadcast_to(
            jnp.sum(key_feat, axis=0, keepdims=True), (STATE - HEAD_DIM, LANES)
        )
        for d in range(1, seq):

            @pl.when(z + d < seq)
            def _():
                state_copy(i, d, d).start()

    def state_copy(i, d, step):
        return remote(
            state.at[i], state_in.at[d - 1, i], state_sem.at[0, d - 1, i], state_sem.at[1, d - 1, i],
            {"seq": lax.rem(z + step + seq, seq)},
        )

    def attend(i):
        prior[i] = jnp.zeros((STATE, LANES), F32)
        for d in range(1, seq):

            @pl.when(z >= d)
            def _():
                state_copy(i, d, -d).wait_recv()
                prior[i] = prior[i] + state_in[d - 1, i]

        query_feat = positive(proj[i, :, lanes(0)])
        key_feat = jnp.where(row_ok, positive(proj[i, :, lanes(1)]), 0.0)
        query_pair, key_pair = split(query_feat), split(key_feat)
        value_pair = split(proj[i, :, lanes(2)])
        total = prior[i, HEAD_DIM : HEAD_DIM + 1, :]
        ones = jnp.where(diagonal_mask(), 1.0, 0.0).astype(BF)
        num = dot3(query_pair, split(unfold(prior[i, 0:HEAD_DIM, :])), "nn")
        below = dot2(split(query_feat * total), ones, "nn")
        row = lax.broadcasted_iota(jnp.int32, (rows, rows), 0)
        col = lax.broadcasted_iota(jnp.int32, (rows, rows), 1)
        for mask in head_masks(rows):
            scores = dot3(query_pair, pick(mask, key_pair), "nt")
            score_pair = split(jnp.where(col <= row, scores, 0.0))
            num = num + dot3(score_pair, pick(mask, value_pair), "nn")
            below = below + dot2(score_pair, jnp.where(mask, 1.0, 0.0).astype(BF), "nn")
        den[i] = below
        mix[i, :, lanes(h)] = jnp.where(row_ok, num / below, 0.0)
        blank_rows = jnp.zeros((rows - used, LANES), F32)
        for other in (near_x, near_y, far):
            mix[i, used:rows, lanes(other)] = blank_rows

    out_copies = [
        remote(
            wout_in.at[own_half], wout.at[h, own_half], out_sem.at[0, k], out_sem.at[1, k], {"head": other}
        )
        for k, other in enumerate((near_x, near_y, far))
    ]
    out_own = pltpu.make_async_copy(wout_in, wout.at[h], load_sem.at[images + 2])

    def out_arrival(k, other):
        return remote(
            wout.at[other, own_half], wout.at[other, own_half], out_sem.at[0, k], out_sem.at[1, k],
            {"head": other},
        )

    def pair_copy(k, other, which):
        half = pl.ds(pl.multiple_of(which * out_half, out_half), out_half)
        return remote(
            wout.at[other, half], wout.at[other, half], pair_sem.at[0, k], pair_sem.at[1, k],
            {"dp": 1 - c},
        )

    peers = tuple(enumerate((near_x, near_y, far)))
    stores = []

    def store(src, dst):
        copy = pltpu.make_async_copy(src, dst, store_sem.at[len(stores)])
        copy.start()
        stores.append(copy)

    for t in range(images + 2):
        if t < images:
            tokens.forward(t)
            if t + 2 < images:
                tokens.direct(t + 2)
            elif t == images - 1:
                for copy in out_copies:
                    copy.start()
                out_own.start()
        if 1 <= t <= images:
            tokens.ready(t - 1)
            project(t - 1)
            store(tok.at[t - 1], tok_out.at[t - 1])
            store(proj.at[t - 1], proj_out.at[t - 1])
        if t >= 2:
            attend(t - 2)
            mixes.direct(t - 2)
            store(den.at[t - 2], den_out.at[t - 2])
            store(prior.at[t - 2], prior_out.at[t - 2])
    store(gains, gains_out)
    out_own.wait()
    for k, other in peers:
        out_arrival(k, other).wait_recv()
        pair_copy(k, other, c).start()
    for i in range(images):
        mixes.forward(i)
    for k, other in peers:
        pair_copy(k, other, 1 - c).wait_recv()
    store(wout, wout_out)
    for i in range(images):
        mixes.ready(i)
        store(mix.at[i], mix_out.at[i])
    for i in range(images):
        tokens.finish(i)
        mixes.finish(i)
        for d in range(1, seq):

            @pl.when(z + d < seq)
            def _(i=i, d=d):
                state_copy(i, d, d).wait_send()

    for copy in gain_copies + out_copies:
        copy.wait_send()
    for k, other in peers:
        pair_copy(k, other, c).wait_send()
    for copy in stores:
        copy.wait()


def attend_call(tokens, gains, wqkv, wout, length):
    images, rows, _ = tokens.shape
    used = round_up(length, 8)
    width = wqkv.shape[0]
    heads_n = width // LANES
    dma = pltpu.SemaphoreType.DMA
    seq = lax.axis_size("seq")
    any_spec = pl.BlockSpec(memory_space=pl.ANY)
    shape = lambda *s: jax.ShapeDtypeStruct(s, F32)
    return pl.pallas_call(
        functools.partial(attend_kernel, (images, length, used, rows)),
        out_shape=(
            shape(images, rows, width),
            shape(8, width),
            shape(images, rows, 3 * LANES),
            shape(images, rows, LANES),
            shape(images, STATE, LANES),
            shape(images, rows, width),
            shape(heads_n, LANES, width),
        ),
        in_specs=[any_spec] * 4,
        out_specs=(any_spec,) * 7,
        scratch_shapes=[
            pltpu.VMEM((images, rows, width), F32),
            pltpu.VMEM((images, rows, width), F32),
            pltpu.VMEM((8, width), F32),
            pltpu.VMEM((images, rows, 3 * LANES), F32),
            pltpu.VMEM((images, rows, LANES), F32),
            pltpu.VMEM((images, STATE, LANES), F32),
            pltpu.VMEM((images, STATE, LANES), F32),
            pltpu.VMEM((seq - 1, images, STATE, LANES), F32),
            pltpu.VMEM((width, 3 * LANES), F32),
            pltpu.VMEM((width, 3 * LANES), BF),
            pltpu.VMEM((width, 3 * LANES), BF),
            pltpu.VMEM((rows, width), BF),
            pltpu.VMEM((rows, width), BF),
            pltpu.VMEM((heads_n, LANES, width), F32),
            dma((images, Gather.SEMS)),
            dma((images, Gather.SEMS)),
            dma((6,)),
            dma((2, seq - 1, images)),
            dma((2, 3)),
            dma((2, 3)),
            dma((images + 3,)),
            dma((5 * images + 4,)),
        ],
        compiler_params=pltpu.CompilerParams(
            collective_id=0, has_side_effects=True, vmem_limit_bytes=VMEM_BYTES
        ),
    )(tokens, gains, wqkv, wout)


VMEM_BYTES = 60 * 1024 * 1024
class Scatter:
    SEMS = 12

    def __init__(self, part, buffers, rows, sems):
        self.part, self.buffers, self.sems = part, buffers, sems
        self.half = round_up(rows // 2, 8)
        self.rows = rows
        self.first, self.second = pl.ds(0, self.half), pl.ds(self.half, rows - self.half)
        self.left = pl.ds(0, rows - self.half)

    def slot(self, i, k):
        rows = self.first if k in (0, 2, 5) else self.left
        return self.buffers.at[i, k, rows]

    def copy(self, i, k, src, into=None):
        _, _, _, near_x, near_y, _ = place()
        into = k if into is None else into
        device = near_x if into in (0, 2, 4) else near_y
        return remote(
            src, self.slot(i, into), self.sems.at[i, into], self.sems.at[i, 6 + into], {"head": device}
        )

    def sent(self, i):
        _, _, _, near_x, near_y, far = place()
        part = self.part(i)
        return (
            self.copy(i, 2, part.at[self.first, lanes(far)]),
            self.copy(i, 3, part.at[self.second, lanes(far)]),
            self.copy(i, 0, part.at[self.first, lanes(near_x)]),
            self.copy(i, 1, part.at[self.second, lanes(near_y)]),
        )

    def passed(self, i):
        return (
            self.copy(i, 2, self.slot(i, 2), 5),
            self.copy(i, 3, self.slot(i, 3), 4),
        )

    def direct(self, i):
        for copy in self.sent(i):
            copy.start()

    def relay(self, i):
        _, _, _, near_x, near_y, _ = place()
        part = self.part(i)
        to_y, to_x = self.passed(i)
        self.copy(i, 2, self.slot(i, 2)).wait_recv()
        self.buffers[i, 2, self.first] = self.buffers[i, 2, self.first] + part[self.first, lanes(near_y)]
        to_y.start()
        self.copy(i, 3, self.slot(i, 3)).wait_recv()
        self.buffers[i, 3, self.left] = self.buffers[i, 3, self.left] + part[self.second, lanes(near_x)]
        to_x.start()

    def total(self, i):
        _, h, _, _, _, _ = place()
        part = self.part(i)
        for k in (0, 5, 1, 4):
            self.copy(i, k, self.slot(i, k)).wait_recv()
        first = (
            part[self.first, lanes(h)] + self.buffers[i, 0, self.first] + self.buffers[i, 5, self.first]
        )
        second = part[self.second, lanes(h)] + self.buffers[i, 1, self.left] + self.buffers[i, 4, self.left]
        return jnp.concatenate([first, second], axis=0)

    def finish(self, i):
        for copy in self.sent(i) + self.passed(i):
            copy.wait_send()


def activation(values):
    scale = 0.7978845608028654
    square = values * values
    bent = jnp.tanh(scale * values * (1.0 + 0.044715 * square))
    half = 0.5 * (1.0 + bent)
    slope = half + 0.5 * values * (1.0 - bent * bent) * (scale * (1.0 + 0.134145 * square))
    return values * half, slope


def to_lanes(first, second, rows):
    lane = lax.broadcasted_iota(jnp.int32, (rows, 128), 1)
    both = jnp.where(lane == 0, first, jnp.where(lane == 1, second, 0.0))
    both = jnp.concatenate([both, jnp.zeros((LANES - rows, 128), F32)], axis=0)
    return jnp.transpose(both)[0:8]


def to_columns(block, rows):
    tall = jnp.concatenate([block, jnp.zeros((120, LANES), F32)], axis=0)
    turned = jnp.transpose(tall)[0:rows]
    return turned[:, 0:1], turned[:, 1:2]


def ffn_kernel(
    dims,
    tok_in, mix_in, gains_in, wout_in, up_in, bias_in, down_in, down_bias_in, grad_in,
    out_out, resid_grad_out, down_grad_out, up_grad_out, bias_grad_out, share_grad_out,
    w_out_h, w_out_l, w_up_h, w_up_l, w_dn_h, w_dn_l, stage, gains, bias, down_bias,
    grad, tok, mix, pair_h, pair_l, xhat, n_h, n_l, hid_h, hid_l, slope, ug_h, ug_l, g_h, g_l,
    part_ffn, part_norm, buf_ffn, buf_norm, xhat_own, inv_own, resid_grad, d_down, d_up, d_bias, d_share, out_own,
    grad_sem, ffn_sem, norm_sem, back_sem, load_sem, stage_sem, image_sem, store_sem,
):
    images, length, used, rows = dims
    width = tok.shape[2]
    hidden = up_in.shape[1]
    z, h, c, near_x, near_y, far = place()
    row_tile = 16

    small = [
        pltpu.make_async_copy(gains_in, gains, load_sem.at[0]),
        pltpu.make_async_copy(bias_in, bias, load_sem.at[1]),
        pltpu.make_async_copy(down_bias_in, down_bias, load_sem.at[2]),
    ]
    small += [
        pltpu.make_async_copy(grad_in.at[i], grad.at[i, :, lanes(h)], load_sem.at[3 + i])
        for i in range(images)
    ]
    depth = stage.shape[1]
    pieces = []
    for source, high, low in ((wout_in, w_out_h, w_out_l), (up_in, w_up_h, w_up_l), (down_in, w_dn_h, w_dn_l)):
        for r in range(source.shape[0] // depth):
            pieces.append((source.at[pl.ds(r * depth, depth)], high, low, r * depth))

    def piece_copy(k):
        return pltpu.make_async_copy(pieces[k][0], stage.at[k % 2], stage_sem.at[k % 2])

    def image_copies(i):
        return (
            pltpu.make_async_copy(tok_in.at[i], tok.at[i % 2], image_sem.at[0, i % 2]),
            pltpu.make_async_copy(mix_in.at[i], mix.at[i % 2], image_sem.at[1, i % 2]),
        )

    piece_copy(0).start()
    for copy in image_copies(0):
        copy.start()
    piece_copy(1).start()
    for copy in small:
        copy.start()
    blank = jnp.zeros((rows - used, LANES), F32)
    for i in range(images):
        for other in (near_x, near_y, far):
            grad[i, used:rows, lanes(other)] = blank
            resid_grad[i, used:rows, lanes(other)] = blank
    enter([{"head": near_x}, {"head": near_y}])
    grads = Gather(lambda i: grad_in.at[i], grad, used, grad_sem)
    ffn = Scatter(lambda i: part_ffn.at[i % 2], buf_ffn, used, ffn_sem)
    norm = Scatter(lambda i: part_norm.at[i % 2], buf_norm, rows, norm_sem)
    back = Gather(lambda i: resid_grad.at[i, :, lanes(h)], resid_grad, used, back_sem)
    grads.direct(0)
    grads.direct(1)

    def take(k):
        piece_copy(k).wait()
        _, high, low, at = pieces[k]

        def one(r, _):
            s = pl.ds(pl.multiple_of(r * row_tile, row_tile), row_tile)
            t = pl.ds(pl.multiple_of(at + r * row_tile, row_tile), row_tile)
            high[t, :], low[t, :] = split(stage[k % 2, s, :])
            return 0

        lax.fori_loop(0, depth // row_tile, one, 0)
        if k + 2 < len(pieces):
            piece_copy(k + 2).start()

    per = len(pieces) // 3
    row_ok = lax.broadcasted_iota(jnp.int32, (rows, LANES), 0) < length
    d_share[...] = jnp.zeros_like(d_share)
    d_bias[...] = jnp.zeros_like(d_bias)
    stores = []

    def store(src, dst):
        copy = pltpu.make_async_copy(src, dst, store_sem.at[len(stores)])
        copy.start()
        stores.append(copy)

    def halves(source, high, low):
        split_rows(source, high, low, rows, row_tile)

    def forward(i):
        for copy in image_copies(i):
            copy.wait()
        if i + 1 < images:
            for copy in image_copies(i + 1):
                copy.start()
        halves(mix.at[i % 2], pair_h, pair_l)
        if i == 0:
            for k in range(per):
                take(k)

        def branch(k, _):
            s = lanes(k)
            xhat[:, s] = tok[i % 2, :, s] + dot3(
                (pair_h[...], pair_l[...]), (w_out_h[:, s], w_out_l[:, s]), "nn"
            )
            return 0

        lax.fori_loop(0, width // LANES, branch, 0)
        out_own[i] = xhat[:, lanes(h)]

        def normed(r, _):
            s = pl.ds(pl.multiple_of(r * row_tile, row_tile), row_tile)
            hat, inv = norm_parts(xhat[s, :])
            xhat[s, :] = hat
            inv_own[i, s, :] = jnp.broadcast_to(inv, (row_tile, 128))
            n_h[s, :], n_l[s, :] = split(hat * gains[1:2, :])
            return 0

        lax.fori_loop(0, rows // row_tile, normed, 0)
        xhat_own[i] = xhat[:, lanes(h)]
        if i == 0:
            for k in range(per, 2 * per):
                take(k)

        def up(k, _):
            s = lanes(k)
            proj = dot3((n_h[...], n_l[...]), (w_up_h[:, s], w_up_l[:, s]), "nn") + bias[0:1, s]
            act, by = activation(proj)
            hid_h[:, s], hid_l[:, s] = split(act)
            slope[:, s] = by
            return 0

        lax.fori_loop(0, hidden // LANES, up, 0)
        if i == 0:
            for k in range(2 * per, 3 * per):
                take(k)
        if i >= 2:
            ffn.finish(i - 2)

        def down(k, _):
            s = lanes(k)
            part_ffn[i % 2, :, s] = dot3((hid_h[...], hid_l[...]), (w_dn_h[:, s], w_dn_l[:, s]), "nn")
            return 0

        lax.fori_loop(0, width // LANES, down, 0)

    def hidden_back(i):
        halves(grad.at[i], g_h, g_l)

        def one(k, _):
            s = lanes(k)
            ug = dot3((g_h[...], g_l[...]), (w_dn_h[s, :], w_dn_l[s, :]), "nt") * slope[:, s]
            ug_h[:, s], ug_l[:, s] = split(ug)
            d_bias[0:1, s] = d_bias[0:1, s] + jnp.sum(ug, axis=0, keepdims=True)
            return 0

        lax.fori_loop(0, hidden // LANES, one, 0)

    def norm_back(i):
        if i >= 2:
            norm.finish(i - 2)

        def one(k, sums):
            s = lanes(k)
            term = dot3((ug_h[...], ug_l[...]), (w_up_h[s, :], w_up_l[s, :]), "nt")
            part_norm[i % 2, :, s] = term
            scaled = term * gains[1:2, s]
            return (
                sums[0] + jnp.sum(scaled, axis=-1, keepdims=True),
                sums[1] + jnp.sum(scaled * xhat[:, s], axis=-1, keepdims=True),
            )

        none = jnp.zeros((rows, 1), F32)
        first, second = lax.fori_loop(0, width // LANES, one, (none, none))
        block = to_lanes(first, second, rows)
        for k in range(width // LANES):
            part_norm[i % 2, rows - 8 : rows, lanes(k)] = block

    def weight_grads(i):
        def one(k, _):
            s = lanes(k)
            down = dot3((hid_h[:, s], hid_l[:, s]), (g_h[...], g_l[...]), "tn")
            up = dot3((n_h[:, s], n_l[:, s]), (ug_h[...], ug_l[...]), "tn")
            if i == 0:
                d_down[s, :] = down
                d_up[s, :] = up
            else:
                d_down[s, :] = d_down[s, :] + down
                d_up[s, :] = d_up[s, :] + up
            return 0

        lax.fori_loop(0, hidden // LANES, one, 0)

    def output(i):
        out_own[i, 0:used] = out_own[i, 0:used] + ffn.total(i) + down_bias[0:1, :]
        store(out_own.at[i], out_out.at[i])

    def resid_back(i):
        both = norm.total(i)
        mean, cross = to_columns(both[rows - 8 : rows], rows)
        own = jnp.where(row_ok, both, 0.0)
        hat = xhat_own[i]
        inv = inv_own[i, :, 0:1]
        scaled = own * gains[1:2, lanes(h)]
        share = (scaled - mean * (1.0 / width) - hat * (cross * (1.0 / width))) * inv
        resid_grad[i, :, lanes(h)] = jnp.where(row_ok, grad[i, :, lanes(h)] + share, 0.0)
        d_share[0:1, :] = d_share[0:1, :] + jnp.sum(own * hat, axis=0, keepdims=True)
        d_share[1:2, :] = d_share[1:2, :] + jnp.sum(grad[i, :, lanes(h)], axis=0, keepdims=True)
        back.direct(i)

    for copy in small:
        copy.wait()
    for i in range(images):
        grads.forward(i)
        if i + 2 < images:
            grads.direct(i + 2)
        forward(i)
        ffn.direct(i)
        grads.ready(i)
        hidden_back(i)
        ffn.relay(i)
        if i >= 1:
            norm.relay(i - 1)
        norm_back(i)
        norm.direct(i)
        if i >= 1:
            resid_back(i - 1)
        weight_grads(i)
        output(i)
        if i >= 1:
            back.forward(i - 1)
        if i >= 2:
            back.ready(i - 2)
            store(resid_grad.at[i - 2], resid_grad_out.at[i - 2])
    store(d_down, down_grad_out)
    store(d_up, up_grad_out)
    last = images - 1
    norm.relay(last)
    resid_back(last)
    store(d_bias, bias_grad_out)
    store(d_share, share_grad_out)
    back.ready(last - 1)
    store(resid_grad.at[last - 1], resid_grad_out.at[last - 1])
    back.forward(last)
    back.ready(last)
    store(resid_grad.at[last], resid_grad_out.at[last])
    for i in range(images):
        grads.finish(i)
        back.finish(i)
        if i >= images - 2:
            ffn.finish(i)
            norm.finish(i)
    for copy in stores:
        copy.wait()


def ffn_call(tok, mix, gains, wout, up_weight, up_bias, down_weight, down_bias, grads, length):
    images, rows, width = tok.shape
    hidden = up_weight.shape[1]
    used = round_up(length, 8)
    dma = pltpu.SemaphoreType.DMA
    any_spec = pl.BlockSpec(memory_space=pl.ANY)
    shape = lambda *s: jax.ShapeDtypeStruct(s, F32)
    vmem = pltpu.VMEM
    half_used, half_rows = round_up(used // 2, 8), round_up(rows // 2, 8)
    return pl.pallas_call(
        functools.partial(ffn_kernel, (images, length, used, rows)),
        out_shape=(
            shape(images, rows, LANES),
            shape(images, rows, width),
            shape(hidden, width),
            shape(width, hidden),
            shape(8, hidden),
            shape(8, LANES),
        ),
        in_specs=[any_spec] * 9,
        out_specs=(any_spec,) * 6,
        scratch_shapes=[
            vmem((width, width), BF), vmem((width, width), BF),
            vmem((width, hidden), BF), vmem((width, hidden), BF),
            vmem((hidden, width), BF), vmem((hidden, width), BF),
            vmem((2, width // 2, width), F32),
            vmem((8, width), F32), vmem((8, hidden), F32), vmem((8, LANES), F32),
            vmem((images, rows, width), F32),
            vmem((2, rows, width), F32), vmem((2, rows, width), F32),
            vmem((rows, width), BF), vmem((rows, width), BF),
            vmem((rows, width), F32),
            vmem((rows, width), BF), vmem((rows, width), BF),
            vmem((rows, hidden), BF), vmem((rows, hidden), BF),
            vmem((rows, hidden), F32),
            vmem((rows, hidden), BF), vmem((rows, hidden), BF),
            vmem((rows, width), BF), vmem((rows, width), BF),
            vmem((2, rows, width), F32), vmem((2, rows, width), F32),
            vmem((images, 6, half_used, LANES), F32), vmem((images, 6, half_rows, LANES), F32),
            vmem((images, rows, LANES), F32), vmem((images, rows, 128), F32),
            vmem((images, rows, width), F32),
            vmem((hidden, width), F32), vmem((width, hidden), F32),
            vmem((8, hidden), F32), vmem((8, LANES), F32),
            vmem((images, rows, LANES), F32),
            dma((images, Gather.SEMS)), dma((images, Scatter.SEMS)), dma((images, Scatter.SEMS)),
            dma((images, Gather.SEMS)), dma((images + 3,)), dma((2,)), dma((2, 2)), dma((2 * images + 4,)),
        ],
        compiler_params=pltpu.CompilerParams(
            collective_id=1, has_side_effects=True, vmem_limit_bytes=VMEM_BYTES
        ),
    )(tok, mix, gains, wout, up_weight, up_bias, down_weight, down_bias, grads)


def fast_device(
    tokens,
    gain_attn,
    qkv_weight,
    out_weight,
    gain_ffn,
    up_weight,
    up_bias,
    down_weight,
    down_bias,
    out_grad,
):
    image_count, block_len, local_width = tokens.shape
    row_count = image_count * block_len
    model_width = qkv_weight.shape[0]
    heads_local = local_width // HEAD_DIM
    rows = round_up(round_up(block_len, 8) + 8, 16)
    column_start = lax.axis_index("head") * local_width
    pad = ((0, 0), (0, rows - block_len), (0, 0))
    proj_weight = qkv_weight.reshape(model_width, 3 * local_width)
    gains_in = jnp.concatenate([gain_attn[None], gain_ffn[None], jnp.zeros((6, local_width), jnp.float32)])
    tok, gains, proj, den, prior, mix, wout = attend_call(
        jnp.pad(tokens, pad), gains_in, proj_weight, out_weight, block_len
    )
    gain_first = gains[0]
    wide = lambda a: jnp.concatenate([a[None], jnp.zeros((7, a.shape[0]), jnp.float32)])
    out, resid_grad, down_weight_grad, up_weight_grad, bias_grad, share_grad = ffn_call(
        tok, mix, gains, wout.reshape(model_width, model_width), up_weight, wide(up_bias), down_weight,
        wide(down_bias), jnp.pad(out_grad, pad), block_len,
    )
    output = out[:, :block_len]
    up_bias_grad, gain_ffn_share, down_bias_grad = bias_grad[0], share_grad[0], share_grad[1]
    ffn_grads = lax.psum((up_weight_grad, down_weight_grad), ("seq", "dp"))
    resid_grad = resid_grad[:, :block_len].reshape(row_count, model_width)
    resid_grad_share = lax.dynamic_slice_in_dim(resid_grad, column_start, local_width, 1)
    mixed_rows = lax.dynamic_slice_in_dim(
        mix[:, :block_len].reshape(row_count, model_width), column_start, local_width, 1
    )
    token_rows = tok[:, :block_len].reshape(row_count, model_width)
    normed_one = layer_norm(token_rows, gain_first)
    parts_view = proj[:, :block_len].reshape(image_count, block_len, 3, heads_local, HEAD_DIM)
    query_proj = parts_view[:, :, 0]
    key_proj = parts_view[:, :, 1]
    value_proj = parts_view[:, :, 2]
    (own_state, own_total), pull_state = jax.vjp(block_state, key_proj, value_proj)
    zero_pair = (jnp.zeros_like(own_state), jnp.zeros_like(own_total))
    prior_state = prior[:, :HEAD_DIM].reshape(image_count, HEAD_DIM, heads_local, HEAD_DIM).transpose(0, 2, 1, 3)
    prior_total = prior[:, HEAD_DIM].reshape(image_count, heads_local, HEAD_DIM)
    mixed, pull_attend = jax.vjp(
        block_attend, query_proj, key_proj, value_proj, prior_state, prior_total
    )
    out_weight_grad = jnp.dot(mixed_rows.T, resid_grad, precision=highest)
    mixed_grad = jnp.dot(resid_grad, out_weight.T, precision=highest).reshape(mixed.shape)
    query_grad, key_grad, value_grad, state_grad, total_grad = pull_attend(mixed_grad)
    later_state, later_total = entering((state_grad, total_grad), "seq", add_pair, zero_pair, True)
    key_extra, value_extra = pull_state((later_state, later_total))
    key_grad = key_grad + key_extra
    value_grad = value_grad + value_extra
    proj_grad = jnp.stack([query_grad, key_grad, value_grad], axis=2).reshape(
        row_count, 3 * local_width
    )
    qkv_weight_grad = jnp.dot(normed_one.T, proj_grad, precision=highest).reshape(qkv_weight.shape)
    token_back, gain_attn_share = norm_back(
        jnp.dot(proj_grad, proj_weight.T, precision=highest), token_rows, gain_first, gain_attn
    )
    tokens_grad = (resid_grad_share + token_back).reshape(tokens.shape)
    summed_grads = lax.psum(
        (
            gain_attn_share,
            qkv_weight_grad,
            out_weight_grad,
            gain_ffn_share,
            up_bias_grad,
            down_bias_grad,
        ),
        ("seq", "dp"),
    )
    return (
        output,
        tokens_grad,
        summed_grads[0],
        summed_grads[1],
        summed_grads[2],
        summed_grads[3],
        ffn_grads[0],
        summed_grads[4],
        ffn_grads[1],
        summed_grads[5],
    )


def device_function(mesh):
    if mesh.shape["head"] == 4 and mesh.shape["dp"] == 2:
        return fast_device
    return per_device


def solution(mesh):
    return jax.shard_map(
        device_function(mesh),
        mesh=mesh,
        in_specs=(
            P("dp", "seq", "head"),
            P("head"),
            P(None, None, "head"),
            P("head", None),
            P("head"),
            P(None, "head"),
            P("head"),
            P("head", None),
            P("head"),
            P("dp", "seq", "head"),
        ),
        out_specs=(
            P("dp", "seq", "head"),
            P("dp", "seq", "head"),
            P("head"),
            P(None, None, "head"),
            P("head", None),
            P("head"),
            P(None, "head"),
            P("head"),
            P("head", None),
            P("head"),
        ),
        check_vma=False,
    )
```

```python
import functools

import jax
import jax.numpy as jnp
from jax import lax
from jax.experimental import pallas as pl
from jax.experimental.pallas import tpu as pltpu
from jax.sharding import PartitionSpec as P

HEAD_DIM = 64


highest = lax.Precision.HIGH
norm_eps = 1e-05


def entering(part, axis, combine, identity, reverse):
    count = lax.axis_size(axis)
    place = lax.axis_index(axis)
    ahead = count - 1 - place if reverse else place
    gathered = jax.tree.map(lambda a: lax.all_gather(a, axis), part)
    state = jax.tree.map(lambda a, e: jnp.zeros_like(a) + jnp.asarray(e, a.dtype), part, identity)

    def one(turn, state):
        source = count - 1 - turn if reverse else turn
        return combine(
            state, jax.tree.map(lambda a: lax.dynamic_index_in_dim(a, source, 0, False), gathered)
        )

    return lax.fori_loop(0, ahead, one, state)


def feature(values_in):
    return jax.nn.elu(values_in) + 1.0


def layer_norm(values_in, gain):
    row_mean = jnp.mean(values_in, axis=-1, keepdims=True)
    centred = values_in - row_mean
    row_var = jnp.mean(centred * centred, axis=-1, keepdims=True)
    return centred * lax.rsqrt(row_var + norm_eps) * gain


def norm_back(partial_grad, rows_full, gain_full, gain_share):
    local_width = gain_share.shape[0]
    model_width = gain_full.shape[0]
    row_mean = jnp.mean(rows_full, axis=-1, keepdims=True)
    centred = rows_full - row_mean
    row_inv = lax.rsqrt(jnp.mean(centred * centred, axis=-1, keepdims=True) + norm_eps)
    scaled = partial_grad * gain_full
    sums = lax.psum(
        jnp.stack(
            [jnp.sum(scaled, axis=-1), jnp.sum(scaled * (centred * row_inv), axis=-1)]
        ),
        "head",
    )
    means = (sums / model_width)[:, :, None]
    share = lax.psum_scatter(partial_grad, "head", scatter_dimension=1, tiled=True)
    start = lax.axis_index("head") * local_width
    xhat = lax.dynamic_slice_in_dim(centred, start, local_width, 1) * row_inv
    back = (share * gain_share - means[0] - xhat * means[1]) * row_inv
    return back, jnp.sum(share * xhat, axis=0)


def mlp_act(values_in):
    return jax.nn.gelu(values_in, approximate=True)


def block_attend(query_proj, key_proj, value_proj, prior_state, prior_total):
    query_feat = feature(query_proj)
    key_feat = feature(key_proj)
    length_now = query_proj.shape[1]
    scores = jnp.einsum("gihe,gjhe->ghij", query_feat, key_feat, precision=highest)
    row_index = lax.broadcasted_iota(jnp.int32, (length_now, length_now), 0)
    col_index = lax.broadcasted_iota(jnp.int32, (length_now, length_now), 1)
    scores = jnp.where(col_index <= row_index, scores, jnp.float32(0.0))
    numerator = jnp.einsum("ghij,gjhe->gihe", scores, value_proj, precision=highest)
    numerator = numerator + jnp.einsum(
        "gihe,ghef->gihf", query_feat, prior_state, precision=highest
    )
    denominator = jnp.sum(scores, axis=-1) + jnp.einsum(
        "gihe,ghe->ghi", query_feat, prior_total, precision=highest
    )
    return numerator / jnp.transpose(denominator, (0, 2, 1))[..., None]


def block_state(key_proj, value_proj):
    key_feat = feature(key_proj)
    kv_sum = jnp.einsum("gihe,gihf->ghef", key_feat, value_proj, precision=highest)
    return (kv_sum, jnp.sum(key_feat, axis=1))


def add_pair(earlier, later):
    return (earlier[0] + later[0], earlier[1] + later[1])


def per_device(
    tokens,
    gain_attn,
    qkv_weight,
    out_weight,
    gain_ffn,
    up_weight,
    up_bias,
    down_weight,
    down_bias,
    out_grad,
):
    image_count, block_len, local_width = tokens.shape
    row_count = image_count * block_len
    model_width = qkv_weight.shape[0]
    heads_local = local_width // HEAD_DIM
    column_start = lax.axis_index("head") * local_width
    full_tokens, gain_first, gain_second = (
        lax.all_gather(tokens, "head", axis=2, tiled=True),
        lax.all_gather(gain_attn, "head", axis=0, tiled=True),
        lax.all_gather(gain_ffn, "head", axis=0, tiled=True),
    )
    token_rows = full_tokens.reshape(row_count, model_width)
    normed_one = layer_norm(token_rows, gain_first)
    proj_weight = qkv_weight.reshape(model_width, 3 * local_width)
    projected = jnp.dot(normed_one, proj_weight, precision=highest)
    parts_view = projected.reshape(image_count, block_len, 3, heads_local, HEAD_DIM)
    query_proj = parts_view[:, :, 0]
    key_proj = parts_view[:, :, 1]
    value_proj = parts_view[:, :, 2]
    (own_state, own_total), pull_state = jax.vjp(block_state, key_proj, value_proj)
    zero_pair = (jnp.zeros_like(own_state), jnp.zeros_like(own_total))
    prior_state, prior_total = entering((own_state, own_total), "seq", add_pair, zero_pair, False)
    mixed, pull_attend = jax.vjp(
        block_attend, query_proj, key_proj, value_proj, prior_state, prior_total
    )
    mixed_rows = mixed.reshape(row_count, local_width)
    branch_out = jnp.dot(mixed_rows, out_weight, precision=highest)
    token_share = tokens.reshape(row_count, local_width)
    resid_share = token_share + lax.psum_scatter(
        branch_out, "head", scatter_dimension=1, tiled=True
    )
    resid_full = lax.all_gather(resid_share, "head", axis=1, tiled=True)
    normed_two = layer_norm(resid_full, gain_second)
    up_proj = jnp.dot(normed_two, up_weight, precision=highest) + up_bias
    hidden, pull_act = jax.vjp(mlp_act, up_proj)
    down_proj = jnp.dot(hidden, down_weight, precision=highest)
    ffn_share = lax.psum_scatter(down_proj, "head", scatter_dimension=1, tiled=True)
    output = (resid_share + ffn_share + down_bias).reshape(tokens.shape)
    grad_share = out_grad.reshape(row_count, local_width)
    grad_full = lax.all_gather(grad_share, "head", axis=1, tiled=True)
    down_bias_grad = jnp.sum(grad_share, axis=0)
    down_weight_grad = jnp.dot(hidden.T, grad_full, precision=highest)
    hidden_grad = jnp.dot(grad_full, down_weight.T, precision=highest)
    (up_grad,) = pull_act(hidden_grad)
    up_bias_grad = jnp.sum(up_grad, axis=0)
    up_weight_grad = jnp.dot(normed_two.T, up_grad, precision=highest)
    ffn_grads = lax.psum((up_weight_grad, down_weight_grad), ("seq", "dp"))
    resid_back, gain_ffn_share = norm_back(
        jnp.dot(up_grad, up_weight.T, precision=highest), resid_full, gain_second, gain_ffn
    )
    resid_grad_share = grad_share + resid_back
    resid_grad = lax.all_gather(resid_grad_share, "head", axis=1, tiled=True)
    out_weight_grad = jnp.dot(mixed_rows.T, resid_grad, precision=highest)
    mixed_grad = jnp.dot(resid_grad, out_weight.T, precision=highest).reshape(mixed.shape)
    query_grad, key_grad, value_grad, state_grad, total_grad = pull_attend(mixed_grad)
    later_state, later_total = entering((state_grad, total_grad), "seq", add_pair, zero_pair, True)
    key_extra, value_extra = pull_state((later_state, later_total))
    key_grad = key_grad + key_extra
    value_grad = value_grad + value_extra
    proj_grad = jnp.stack([query_grad, key_grad, value_grad], axis=2).reshape(
        row_count, 3 * local_width
    )
    qkv_weight_grad = jnp.dot(normed_one.T, proj_grad, precision=highest).reshape(qkv_weight.shape)
    token_back, gain_attn_share = norm_back(
        jnp.dot(proj_grad, proj_weight.T, precision=highest), token_rows, gain_first, gain_attn
    )
    tokens_grad = (resid_grad_share + token_back).reshape(tokens.shape)
    summed_grads = lax.psum(
        (
            gain_attn_share,
            qkv_weight_grad,
            out_weight_grad,
            gain_ffn_share,
            up_bias_grad,
            down_bias_grad,
        ),
        ("seq", "dp"),
    )
    return (
        output,
        tokens_grad,
        summed_grads[0],
        summed_grads[1],
        summed_grads[2],
        summed_grads[3],
        ffn_grads[0],
        summed_grads[4],
        ffn_grads[1],
        summed_grads[5],
    )


MESH = pl.DeviceIdType.MESH
BF = jnp.bfloat16
F32 = jnp.float32
LANES = 256
DIMS = {
    "nn": (((1,), (0,)), ((), ())),
    "nt": (((1,), (1,)), ((), ())),
    "tn": (((0,), (0,)), ((), ())),
}


def round_up(value, step):
    return -(-value // step) * step


def dot(left, right, kind):
    return lax.dot_general(left, right, DIMS[kind], preferred_element_type=F32)


def split(values):
    high = values.astype(BF)
    return high, (values - high.astype(F32)).astype(BF)


def dot3(left, right, kind):
    return (
        dot(left[0], right[0], kind) + dot(left[0], right[1], kind) + dot(left[1], right[0], kind)
    )


def dot2(left, right, kind):
    return dot(left[0], right, kind) + dot(left[1], right, kind)


def lanes(index):
    if isinstance(index, int):
        return pl.ds(index * LANES, LANES)
    return pl.ds(pl.multiple_of(index * LANES, LANES), LANES)


def place():
    z, h, c = lax.axis_index("seq"), lax.axis_index("head"), lax.axis_index("dp")
    near_x = h + 1 - 2 * lax.rem(h, 2)
    near_y = lax.rem(h + 2, 4)
    return z, h, c, near_x, near_y, 3 - h


def remote(src, dst, send, recv, device):
    return pltpu.make_async_remote_copy(
        src_ref=src, dst_ref=dst, send_sem=send, recv_sem=recv, device_id=device, device_id_type=MESH
    )


def enter(targets):
    barrier = pltpu.get_barrier_semaphore()
    for device in targets:
        pl.semaphore_signal(barrier, inc=1, device_id=device, device_id_type=MESH)
    pl.semaphore_wait(barrier, len(targets))


class Gather:
    SEMS = 8

    def __init__(self, own, slots, rows, sems):
        self.own, self.slots, self.sems = own, slots, sems
        self.half = round_up(rows // 2, 8)
        self.rows = rows

    def copies(self, i):
        _, h, _, near_x, near_y, _ = place()
        slots, sems = self.slots, self.sems
        first, second = pl.ds(0, self.half), pl.ds(self.half, self.rows - self.half)
        every = pl.ds(0, self.rows)

        def one(src, dst, place_in, device):
            return remote(src, dst, sems.at[i, place_in], sems.at[i, 4 + place_in], {"head": device})

        own = self.own(i)
        return (
            one(own.at[every], slots.at[i, every, lanes(h)], 0, near_x),
            one(own.at[every], slots.at[i, every, lanes(h)], 1, near_y),
            one(slots.at[i, first, lanes(near_x)], slots.at[i, first, lanes(near_x)], 2, near_y),
            one(slots.at[i, second, lanes(near_y)], slots.at[i, second, lanes(near_y)], 3, near_x),
        )

    def arrivals(self, i):
        _, h, _, near_x, near_y, far = place()
        slots, sems = self.slots, self.sems
        first, second = pl.ds(0, self.half), pl.ds(self.half, self.rows - self.half)
        every = pl.ds(0, self.rows)

        def one(dst, place_in, device):
            return remote(dst, dst, sems.at[i, place_in], sems.at[i, 4 + place_in], {"head": device})

        return (
            one(slots.at[i, every, lanes(near_x)], 0, near_x),
            one(slots.at[i, every, lanes(near_y)], 1, near_y),
            one(slots.at[i, first, lanes(far)], 2, near_y),
            one(slots.at[i, second, lanes(far)], 3, near_x),
        )

    def direct(self, i):
        x, y, _, _ = self.copies(i)
        x.start()
        y.start()

    def forward(self, i):
        x, y, _, _ = self.arrivals(i)
        x.wait_recv()
        y.wait_recv()
        _, _, to_y, to_x = self.copies(i)
        to_y.start()
        to_x.start()

    def ready(self, i):
        _, _, x, y = self.arrivals(i)
        x.wait_recv()
        y.wait_recv()

    def finish(self, i):
        for copy in self.copies(i):
            copy.wait_send()


def head_masks(rows):
    head = lax.broadcasted_iota(jnp.int32, (rows, LANES), 1) // HEAD_DIM
    return [head == k for k in range(LANES // HEAD_DIM)]


def diagonal_mask():
    rows = lax.broadcasted_iota(jnp.int32, (LANES, LANES), 0) // HEAD_DIM
    cols = lax.broadcasted_iota(jnp.int32, (LANES, LANES), 1) // HEAD_DIM
    return rows == cols


def pick(mask, pair):
    zero = jnp.zeros((), BF)
    return jnp.where(mask, pair[0], zero), jnp.where(mask, pair[1], zero)


def fold(square):
    square = jnp.where(diagonal_mask(), square, 0.0)
    return (
        square[0:HEAD_DIM]
        + square[HEAD_DIM : 2 * HEAD_DIM]
        + square[2 * HEAD_DIM : 3 * HEAD_DIM]
        + square[3 * HEAD_DIM :]
    )


def unfold(wide):
    return jnp.where(diagonal_mask(), jnp.concatenate([wide] * 4, axis=0), 0.0)


def positive(values):
    return jnp.where(values > 0, values + 1.0, jnp.exp(jnp.minimum(values, 0.0)))


def norm_parts(rows):
    row_mean = jnp.mean(rows, axis=-1, keepdims=True)
    centred = rows - row_mean
    row_inv = lax.rsqrt(jnp.mean(centred * centred, axis=-1, keepdims=True) + norm_eps)
    return centred * row_inv, row_inv


def split_rows(source, high, low, rows, step):
    def one(r, _):
        s = pl.ds(pl.multiple_of(r * step, step), step)
        high[s, :], low[s, :] = split(source[s, :])
        return 0

    lax.fori_loop(0, rows // step, one, 0)


STATE = HEAD_DIM + 8


def attend_kernel(
    dims,
    tok_in, gains_in, wqkv_in, wout_in,
    tok_out, gains_out, proj_out, den_out, prior_out, mix_out, wout_out,
    tok, mix, gains, proj, den, prior, state, state_in, wstage, w_h, w_l, n_h, n_l, wout,
    tok_sem, mix_sem, gain_sem, state_sem, out_sem, pair_sem, load_sem, store_sem,
):
    images, length, used, rows = dims
    width = tok.shape[2]
    z, h, c, near_x, near_y, far = place()
    seq = lax.axis_size("seq")
    out_half = wout_in.shape[0] // 2

    loads = [
        pltpu.make_async_copy(tok_in.at[i], tok.at[i, :, lanes(h)], load_sem.at[i])
        for i in range(images)
    ]
    loads.append(pltpu.make_async_copy(wqkv_in, wstage, load_sem.at[images]))
    loads.append(pltpu.make_async_copy(gains_in, gains.at[:, lanes(h)], load_sem.at[images + 1]))
    for copy in loads:
        copy.start()

    blank = jnp.zeros((rows - used, LANES), F32)
    for i in range(images):
        for other in (near_x, near_y, far):
            tok[i, used:rows, lanes(other)] = blank

    enter(
        [{"head": near_x}, {"head": near_y}, {"head": far}, {"dp": 1 - c}]
        + [{"seq": lax.rem(z + d, seq)} for d in range(1, seq)]
    )
    tokens = Gather(lambda i: tok_in.at[i], tok, used, tok_sem)
    mixes = Gather(lambda i: mix.at[i, :, lanes(h)], mix, used, mix_sem)
    own_half = pl.ds(pl.multiple_of(c * out_half, out_half), out_half)
    tokens.direct(0)
    gain_copies = [
        remote(gains_in, gains.at[:, lanes(h)], gain_sem.at[k], gain_sem.at[3 + k], {"head": other})
        for k, other in enumerate((near_x, near_y, far))
    ]
    for copy in gain_copies:
        copy.start()
    tokens.direct(1)
    loads[images].wait()
    split_rows(wstage, w_h, w_l, width, 16)
    loads[images + 1].wait()
    for k, other in enumerate((near_x, near_y, far)):
        remote(
            gains.at[:, lanes(other)], gains.at[:, lanes(other)], gain_sem.at[k], gain_sem.at[3 + k],
            {"head": other},
        ).wait_recv()
    row_ok = lax.broadcasted_iota(jnp.int32, (rows, LANES), 0) < length

    def project(i):
        loads[i].wait()

        def normed(r, _):
            s = pl.ds(pl.multiple_of(r * 16, 16), 16)
            xhat, _unused = norm_parts(tok[i, s, :])
            n_h[s, :], n_l[s, :] = split(xhat * gains[0:1, :])
            return 0

        lax.fori_loop(0, rows // 16, normed, 0)

        def column(k, _):
            s = lanes(k)
            proj[i, :, s] = dot3((n_h[...], n_l[...]), (w_h[:, s], w_l[:, s]), "nn")
            return 0

        lax.fori_loop(0, 3, column, 0)
        key_feat = jnp.where(row_ok, positive(proj[i, :, lanes(1)]), 0.0)
        state[i, 0:HEAD_DIM, :] = fold(dot3(split(key_feat), split(proj[i, :, lanes(2)]), "tn"))
        state[i, HEAD_DIM:, :] = jnp.broadcast_to(
            jnp.sum(key_feat, axis=0, keepdims=True), (STATE - HEAD_DIM, LANES)
        )
        for d in range(1, seq):

            @pl.when(z + d < seq)
            def _():
                state_copy(i, d, d).start()

    def state_copy(i, d, step):
        return remote(
            state.at[i], state_in.at[d - 1, i], state_sem.at[0, d - 1, i], state_sem.at[1, d - 1, i],
            {"seq": lax.rem(z + step + seq, seq)},
        )

    def attend(i):
        prior[i] = jnp.zeros((STATE, LANES), F32)
        for d in range(1, seq):

            @pl.when(z >= d)
            def _():
                state_copy(i, d, -d).wait_recv()
                prior[i] = prior[i] + state_in[d - 1, i]

        query_feat = positive(proj[i, :, lanes(0)])
        key_feat = jnp.where(row_ok, positive(proj[i, :, lanes(1)]), 0.0)
        query_pair, key_pair = split(query_feat), split(key_feat)
        value_pair = split(proj[i, :, lanes(2)])
        total = prior[i, HEAD_DIM : HEAD_DIM + 1, :]
        ones = jnp.where(diagonal_mask(), 1.0, 0.0).astype(BF)
        num = dot3(query_pair, split(unfold(prior[i, 0:HEAD_DIM, :])), "nn")
        below = dot2(split(query_feat * total), ones, "nn")
        row = lax.broadcasted_iota(jnp.int32, (rows, rows), 0)
        col = lax.broadcasted_iota(jnp.int32, (rows, rows), 1)
        for mask in head_masks(rows):
            scores = dot3(query_pair, pick(mask, key_pair), "nt")
            score_pair = split(jnp.where(col <= row, scores, 0.0))
            num = num + dot3(score_pair, pick(mask, value_pair), "nn")
            below = below + dot2(score_pair, jnp.where(mask, 1.0, 0.0).astype(BF), "nn")
        den[i] = below
        mix[i, :, lanes(h)] = jnp.where(row_ok, num / below, 0.0)
        blank_rows = jnp.zeros((rows - used, LANES), F32)
        for other in (near_x, near_y, far):
            mix[i, used:rows, lanes(other)] = blank_rows

    out_copies = [
        remote(
            wout_in.at[own_half], wout.at[h, own_half], out_sem.at[0, k], out_sem.at[1, k], {"head": other}
        )
        for k, other in enumerate((near_x, near_y, far))
    ]
    out_own = pltpu.make_async_copy(wout_in, wout.at[h], load_sem.at[images + 2])

    def out_arrival(k, other):
        return remote(
            wout.at[other, own_half], wout.at[other, own_half], out_sem.at[0, k], out_sem.at[1, k],
            {"head": other},
        )

    def pair_copy(k, other, which):
        half = pl.ds(pl.multiple_of(which * out_half, out_half), out_half)
        return remote(
            wout.at[other, half], wout.at[other, half], pair_sem.at[0, k], pair_sem.at[1, k],
            {"dp": 1 - c},
        )

    peers = tuple(enumerate((near_x, near_y, far)))
    stores = []

    def store(src, dst):
        copy = pltpu.make_async_copy(src, dst, store_sem.at[len(stores)])
        copy.start()
        stores.append(copy)

    for t in range(images + 2):
        if t < images:
            tokens.forward(t)
            if t + 2 < images:
                tokens.direct(t + 2)
            elif t == images - 1:
                for copy in out_copies:
                    copy.start()
                out_own.start()
        if 1 <= t <= images:
            tokens.ready(t - 1)
            project(t - 1)
            store(tok.at[t - 1], tok_out.at[t - 1])
            store(proj.at[t - 1], proj_out.at[t - 1])
        if t >= 2:
            attend(t - 2)
            mixes.direct(t - 2)
            store(den.at[t - 2], den_out.at[t - 2])
            store(prior.at[t - 2], prior_out.at[t - 2])
    store(gains, gains_out)
    out_own.wait()
    for k, other in peers:
        out_arrival(k, other).wait_recv()
        pair_copy(k, other, c).start()
    for i in range(images):
        mixes.forward(i)
    for k, other in peers:
        pair_copy(k, other, 1 - c).wait_recv()
    store(wout, wout_out)
    for i in range(images):
        mixes.ready(i)
        store(mix.at[i], mix_out.at[i])
    for i in range(images):
        tokens.finish(i)
        mixes.finish(i)
        for d in range(1, seq):

            @pl.when(z + d < seq)
            def _(i=i, d=d):
                state_copy(i, d, d).wait_send()

    for copy in gain_copies + out_copies:
        copy.wait_send()
    for k, other in peers:
        pair_copy(k, other, c).wait_send()
    for copy in stores:
        copy.wait()


def attend_call(tokens, gains, wqkv, wout, length):
    images, rows, _ = tokens.shape
    used = round_up(length, 8)
    width = wqkv.shape[0]
    heads_n = width // LANES
    dma = pltpu.SemaphoreType.DMA
    seq = lax.axis_size("seq")
    any_spec = pl.BlockSpec(memory_space=pl.ANY)
    shape = lambda *s: jax.ShapeDtypeStruct(s, F32)
    return pl.pallas_call(
        functools.partial(attend_kernel, (images, length, used, rows)),
        out_shape=(
            shape(images, rows, width),
            shape(8, width),
            shape(images, rows, 3 * LANES),
            shape(images, rows, LANES),
            shape(images, STATE, LANES),
            shape(images, rows, width),
            shape(heads_n, LANES, width),
        ),
        in_specs=[any_spec] * 4,
        out_specs=(any_spec,) * 7,
        scratch_shapes=[
            pltpu.VMEM((images, rows, width), F32),
            pltpu.VMEM((images, rows, width), F32),
            pltpu.VMEM((8, width), F32),
            pltpu.VMEM((images, rows, 3 * LANES), F32),
            pltpu.VMEM((images, rows, LANES), F32),
            pltpu.VMEM((images, STATE, LANES), F32),
            pltpu.VMEM((images, STATE, LANES), F32),
            pltpu.VMEM((seq - 1, images, STATE, LANES), F32),
            pltpu.VMEM((width, 3 * LANES), F32),
            pltpu.VMEM((width, 3 * LANES), BF),
            pltpu.VMEM((width, 3 * LANES), BF),
            pltpu.VMEM((rows, width), BF),
            pltpu.VMEM((rows, width), BF),
            pltpu.VMEM((heads_n, LANES, width), F32),
            dma((images, Gather.SEMS)),
            dma((images, Gather.SEMS)),
            dma((6,)),
            dma((2, seq - 1, images)),
            dma((2, 3)),
            dma((2, 3)),
            dma((images + 3,)),
            dma((5 * images + 4,)),
        ],
        compiler_params=pltpu.CompilerParams(
            collective_id=0, has_side_effects=True, vmem_limit_bytes=VMEM_BYTES
        ),
    )(tokens, gains, wqkv, wout)


VMEM_BYTES = 60 * 1024 * 1024
class Scatter:
    SEMS = 12

    def __init__(self, part, buffers, rows, sems):
        self.part, self.buffers, self.sems = part, buffers, sems
        self.half = round_up(rows // 2, 8)
        self.rows = rows
        self.first, self.second = pl.ds(0, self.half), pl.ds(self.half, rows - self.half)
        self.left = pl.ds(0, rows - self.half)

    def slot(self, i, k):
        rows = self.first if k in (0, 2, 5) else self.left
        return self.buffers.at[i, k, rows]

    def copy(self, i, k, src, into=None):
        _, _, _, near_x, near_y, _ = place()
        into = k if into is None else into
        device = near_x if into in (0, 2, 4) else near_y
        return remote(
            src, self.slot(i, into), self.sems.at[i, into], self.sems.at[i, 6 + into], {"head": device}
        )

    def sent(self, i):
        _, _, _, near_x, near_y, far = place()
        part = self.part(i)
        return (
            self.copy(i, 2, part.at[self.first, lanes(far)]),
            self.copy(i, 3, part.at[self.second, lanes(far)]),
            self.copy(i, 0, part.at[self.first, lanes(near_x)]),
            self.copy(i, 1, part.at[self.second, lanes(near_y)]),
        )

    def passed(self, i):
        return (
            self.copy(i, 2, self.slot(i, 2), 5),
            self.copy(i, 3, self.slot(i, 3), 4),
        )

    def direct(self, i):
        for copy in self.sent(i):
            copy.start()

    def relay(self, i):
        _, _, _, near_x, near_y, _ = place()
        part = self.part(i)
        to_y, to_x = self.passed(i)
        self.copy(i, 2, self.slot(i, 2)).wait_recv()
        self.buffers[i, 2, self.first] = self.buffers[i, 2, self.first] + part[self.first, lanes(near_y)]
        to_y.start()
        self.copy(i, 3, self.slot(i, 3)).wait_recv()
        self.buffers[i, 3, self.left] = self.buffers[i, 3, self.left] + part[self.second, lanes(near_x)]
        to_x.start()

    def total(self, i):
        _, h, _, _, _, _ = place()
        part = self.part(i)
        for k in (0, 5, 1, 4):
            self.copy(i, k, self.slot(i, k)).wait_recv()
        first = (
            part[self.first, lanes(h)] + self.buffers[i, 0, self.first] + self.buffers[i, 5, self.first]
        )
        second = part[self.second, lanes(h)] + self.buffers[i, 1, self.left] + self.buffers[i, 4, self.left]
        return jnp.concatenate([first, second], axis=0)

    def finish(self, i):
        for copy in self.sent(i) + self.passed(i):
            copy.wait_send()


def activation(values):
    scale = 0.7978845608028654
    square = values * values
    bent = jnp.tanh(scale * values * (1.0 + 0.044715 * square))
    half = 0.5 * (1.0 + bent)
    slope = half + 0.5 * values * (1.0 - bent * bent) * (scale * (1.0 + 0.134145 * square))
    return values * half, slope


def to_lanes(first, second, rows):
    lane = lax.broadcasted_iota(jnp.int32, (rows, 128), 1)
    both = jnp.where(lane == 0, first, jnp.where(lane == 1, second, 0.0))
    both = jnp.concatenate([both, jnp.zeros((LANES - rows, 128), F32)], axis=0)
    return jnp.transpose(both)[0:8]


def to_columns(block, rows):
    tall = jnp.concatenate([block, jnp.zeros((120, LANES), F32)], axis=0)
    turned = jnp.transpose(tall)[0:rows]
    return turned[:, 0:1], turned[:, 1:2]


def ffn_kernel(
    dims,
    tok_in, mix_in, gains_in, wout_in, up_in, bias_in, down_in, down_bias_in, grad_in,
    out_out, resid_grad_out, down_grad_out, up_grad_out, bias_grad_out, share_grad_out,
    w_out_h, w_out_l, w_up_h, w_up_l, w_dn_h, w_dn_l, stage, gains, bias, down_bias,
    grad, tok, mix, pair_h, pair_l, xhat, n_h, n_l, hid_h, hid_l, slope, ug_h, ug_l, g_h, g_l,
    part_ffn, part_norm, buf_ffn, buf_norm, xhat_own, inv_own, resid_grad, d_down, d_up, d_bias, d_share, out_own,
    grad_sem, ffn_sem, norm_sem, back_sem, load_sem, stage_sem, image_sem, store_sem,
):
    images, length, used, rows = dims
    width = tok.shape[2]
    hidden = up_in.shape[1]
    z, h, c, near_x, near_y, far = place()
    row_tile = 16

    small = [
        pltpu.make_async_copy(gains_in, gains, load_sem.at[0]),
        pltpu.make_async_copy(bias_in, bias, load_sem.at[1]),
        pltpu.make_async_copy(down_bias_in, down_bias, load_sem.at[2]),
    ]
    small += [
        pltpu.make_async_copy(grad_in.at[i], grad.at[i, :, lanes(h)], load_sem.at[3 + i])
        for i in range(images)
    ]
    depth = stage.shape[1]
    pieces = []
    for source, high, low in ((wout_in, w_out_h, w_out_l), (up_in, w_up_h, w_up_l), (down_in, w_dn_h, w_dn_l)):
        for r in range(source.shape[0] // depth):
            pieces.append((source.at[pl.ds(r * depth, depth)], high, low, r * depth))

    def piece_copy(k):
        return pltpu.make_async_copy(pieces[k][0], stage.at[k % 2], stage_sem.at[k % 2])

    def image_copies(i):
        return (
            pltpu.make_async_copy(tok_in.at[i], tok.at[i % 2], image_sem.at[0, i % 2]),
            pltpu.make_async_copy(mix_in.at[i], mix.at[i % 2], image_sem.at[1, i % 2]),
        )

    piece_copy(0).start()
    for copy in image_copies(0):
        copy.start()
    piece_copy(1).start()
    for copy in small:
        copy.start()
    blank = jnp.zeros((rows - used, LANES), F32)
    for i in range(images):
        for other in (near_x, near_y, far):
            grad[i, used:rows, lanes(other)] = blank
            resid_grad[i, used:rows, lanes(other)] = blank
    enter([{"head": near_x}, {"head": near_y}])
    grads = Gather(lambda i: grad_in.at[i], grad, used, grad_sem)
    ffn = Scatter(lambda i: part_ffn.at[i % 2], buf_ffn, used, ffn_sem)
    norm = Scatter(lambda i: part_norm.at[i % 2], buf_norm, rows, norm_sem)
    back = Gather(lambda i: resid_grad.at[i, :, lanes(h)], resid_grad, used, back_sem)
    grads.direct(0)
    grads.direct(1)

    def take(k):
        piece_copy(k).wait()
        _, high, low, at = pieces[k]

        def one(r, _):
            s = pl.ds(pl.multiple_of(r * row_tile, row_tile), row_tile)
            t = pl.ds(pl.multiple_of(at + r * row_tile, row_tile), row_tile)
            high[t, :], low[t, :] = split(stage[k % 2, s, :])
            return 0

        lax.fori_loop(0, depth // row_tile, one, 0)
        if k + 2 < len(pieces):
            piece_copy(k + 2).start()

    per = len(pieces) // 3
    row_ok = lax.broadcasted_iota(jnp.int32, (rows, LANES), 0) < length
    d_share[...] = jnp.zeros_like(d_share)
    d_bias[...] = jnp.zeros_like(d_bias)
    stores = []

    def store(src, dst):
        copy = pltpu.make_async_copy(src, dst, store_sem.at[len(stores)])
        copy.start()
        stores.append(copy)

    def halves(source, high, low):
        split_rows(source, high, low, rows, row_tile)

    def forward(i):
        for copy in image_copies(i):
            copy.wait()
        if i + 1 < images:
            for copy in image_copies(i + 1):
                copy.start()
        halves(mix.at[i % 2], pair_h, pair_l)
        if i == 0:
            for k in range(per):
                take(k)

        def branch(k, _):
            s = lanes(k)
            xhat[:, s] = tok[i % 2, :, s] + dot3(
                (pair_h[...], pair_l[...]), (w_out_h[:, s], w_out_l[:, s]), "nn"
            )
            return 0

        lax.fori_loop(0, width // LANES, branch, 0)
        out_own[i] = xhat[:, lanes(h)]

        def normed(r, _):
            s = pl.ds(pl.multiple_of(r * row_tile, row_tile), row_tile)
            hat, inv = norm_parts(xhat[s, :])
            xhat[s, :] = hat
            inv_own[i, s, :] = jnp.broadcast_to(inv, (row_tile, 128))
            n_h[s, :], n_l[s, :] = split(hat * gains[1:2, :])
            return 0

        lax.fori_loop(0, rows // row_tile, normed, 0)
        xhat_own[i] = xhat[:, lanes(h)]
        if i == 0:
            for k in range(per, 2 * per):
                take(k)

        def up(k, _):
            s = lanes(k)
            proj = dot3((n_h[...], n_l[...]), (w_up_h[:, s], w_up_l[:, s]), "nn") + bias[0:1, s]
            act, by = activation(proj)
            hid_h[:, s], hid_l[:, s] = split(act)
            slope[:, s] = by
            return 0

        lax.fori_loop(0, hidden // LANES, up, 0)
        if i == 0:
            for k in range(2 * per, 3 * per):
                take(k)
        if i >= 2:
            ffn.finish(i - 2)

        def down(k, _):
            s = lanes(k)
            part_ffn[i % 2, :, s] = dot3((hid_h[...], hid_l[...]), (w_dn_h[:, s], w_dn_l[:, s]), "nn")
            return 0

        lax.fori_loop(0, width // LANES, down, 0)

    def hidden_back(i):
        halves(grad.at[i], g_h, g_l)

        def one(k, _):
            s = lanes(k)
            ug = dot3((g_h[...], g_l[...]), (w_dn_h[s, :], w_dn_l[s, :]), "nt") * slope[:, s]
            ug_h[:, s], ug_l[:, s] = split(ug)
            d_bias[0:1, s] = d_bias[0:1, s] + jnp.sum(ug, axis=0, keepdims=True)
            return 0

        lax.fori_loop(0, hidden // LANES, one, 0)

    def norm_back(i):
        if i >= 2:
            norm.finish(i - 2)

        def one(k, sums):
            s = lanes(k)
            term = dot3((ug_h[...], ug_l[...]), (w_up_h[s, :], w_up_l[s, :]), "nt")
            part_norm[i % 2, :, s] = term
            scaled = term * gains[1:2, s]
            return (
                sums[0] + jnp.sum(scaled, axis=-1, keepdims=True),
                sums[1] + jnp.sum(scaled * xhat[:, s], axis=-1, keepdims=True),
            )

        none = jnp.zeros((rows, 1), F32)
        first, second = lax.fori_loop(0, width // LANES, one, (none, none))
        block = to_lanes(first, second, rows)
        for k in range(width // LANES):
            part_norm[i % 2, rows - 8 : rows, lanes(k)] = block

    def weight_grads(i):
        def one(k, _):
            s = lanes(k)
            down = dot3((hid_h[:, s], hid_l[:, s]), (g_h[...], g_l[...]), "tn")
            up = dot3((n_h[:, s], n_l[:, s]), (ug_h[...], ug_l[...]), "tn")
            if i == 0:
                d_down[s, :] = down
                d_up[s, :] = up
            else:
                d_down[s, :] = d_down[s, :] + down
                d_up[s, :] = d_up[s, :] + up
            return 0

        lax.fori_loop(0, hidden // LANES, one, 0)

    def output(i):
        out_own[i, 0:used] = out_own[i, 0:used] + ffn.total(i) + down_bias[0:1, :]
        store(out_own.at[i], out_out.at[i])

    def resid_back(i):
        both = norm.total(i)
        mean, cross = to_columns(both[rows - 8 : rows], rows)
        own = jnp.where(row_ok, both, 0.0)
        hat = xhat_own[i]
        inv = inv_own[i, :, 0:1]
        scaled = own * gains[1:2, lanes(h)]
        share = (scaled - mean * (1.0 / width) - hat * (cross * (1.0 / width))) * inv
        resid_grad[i, :, lanes(h)] = jnp.where(row_ok, grad[i, :, lanes(h)] + share, 0.0)
        d_share[0:1, :] = d_share[0:1, :] + jnp.sum(own * hat, axis=0, keepdims=True)
        d_share[1:2, :] = d_share[1:2, :] + jnp.sum(grad[i, :, lanes(h)], axis=0, keepdims=True)
        back.direct(i)

    for copy in small:
        copy.wait()
    for i in range(images):
        grads.forward(i)
        if i + 2 < images:
            grads.direct(i + 2)
        forward(i)
        ffn.direct(i)
        grads.ready(i)
        hidden_back(i)
        ffn.relay(i)
        if i >= 1:
            norm.relay(i - 1)
        norm_back(i)
        norm.direct(i)
        if i >= 1:
            resid_back(i - 1)
        weight_grads(i)
        output(i)
        if i >= 1:
            back.forward(i - 1)
        if i >= 2:
            back.ready(i - 2)
            store(resid_grad.at[i - 2], resid_grad_out.at[i - 2])
    store(d_down, down_grad_out)
    store(d_up, up_grad_out)
    last = images - 1
    norm.relay(last)
    resid_back(last)
    store(d_bias, bias_grad_out)
    store(d_share, share_grad_out)
    back.ready(last - 1)
    store(resid_grad.at[last - 1], resid_grad_out.at[last - 1])
    back.forward(last)
    back.ready(last)
    store(resid_grad.at[last], resid_grad_out.at[last])
    for i in range(images):
        grads.finish(i)
        back.finish(i)
        if i >= images - 2:
            ffn.finish(i)
            norm.finish(i)
    for copy in stores:
        copy.wait()


def ffn_call(tok, mix, gains, wout, up_weight, up_bias, down_weight, down_bias, grads, length):
    images, rows, width = tok.shape
    hidden = up_weight.shape[1]
    used = round_up(length, 8)
    dma = pltpu.SemaphoreType.DMA
    any_spec = pl.BlockSpec(memory_space=pl.ANY)
    shape = lambda *s: jax.ShapeDtypeStruct(s, F32)
    vmem = pltpu.VMEM
    half_used, half_rows = round_up(used // 2, 8), round_up(rows // 2, 8)
    return pl.pallas_call(
        functools.partial(ffn_kernel, (images, length, used, rows)),
        out_shape=(
            shape(images, rows, LANES),
            shape(images, rows, width),
            shape(hidden, width),
            shape(width, hidden),
            shape(8, hidden),
            shape(8, LANES),
        ),
        in_specs=[any_spec] * 9,
        out_specs=(any_spec,) * 6,
        scratch_shapes=[
            vmem((width, width), BF), vmem((width, width), BF),
            vmem((width, hidden), BF), vmem((width, hidden), BF),
            vmem((hidden, width), BF), vmem((hidden, width), BF),
            vmem((2, width // 2, width), F32),
            vmem((8, width), F32), vmem((8, hidden), F32), vmem((8, LANES), F32),
            vmem((images, rows, width), F32),
            vmem((2, rows, width), F32), vmem((2, rows, width), F32),
            vmem((rows, width), BF), vmem((rows, width), BF),
            vmem((rows, width), F32),
            vmem((rows, width), BF), vmem((rows, width), BF),
            vmem((rows, hidden), BF), vmem((rows, hidden), BF),
            vmem((rows, hidden), F32),
            vmem((rows, hidden), BF), vmem((rows, hidden), BF),
            vmem((rows, width), BF), vmem((rows, width), BF),
            vmem((2, rows, width), F32), vmem((2, rows, width), F32),
            vmem((images, 6, half_used, LANES), F32), vmem((images, 6, half_rows, LANES), F32),
            vmem((images, rows, LANES), F32), vmem((images, rows, 128), F32),
            vmem((images, rows, width), F32),
            vmem((hidden, width), F32), vmem((width, hidden), F32),
            vmem((8, hidden), F32), vmem((8, LANES), F32),
            vmem((images, rows, LANES), F32),
            dma((images, Gather.SEMS)), dma((images, Scatter.SEMS)), dma((images, Scatter.SEMS)),
            dma((images, Gather.SEMS)), dma((images + 3,)), dma((2,)), dma((2, 2)), dma((2 * images + 4,)),
        ],
        compiler_params=pltpu.CompilerParams(
            collective_id=1, has_side_effects=True, vmem_limit_bytes=VMEM_BYTES
        ),
    )(tok, mix, gains, wout, up_weight, up_bias, down_weight, down_bias, grads)


class Reduce:
    SEMS = 12

    def __init__(self, slots, sems):
        self.slots, self.sems = slots, sems
        self.chunks = []

    def add(self, partial, own, arrived, result, half, rows):
        c = lax.axis_index("dp")
        for r in range(half // rows):
            here = pl.ds(pl.multiple_of(c * half + r * rows, 8), rows)
            there = pl.ds(pl.multiple_of((1 - c) * half + r * rows, 8), rows)
            local = pl.ds(r * rows, rows)
            self.chunks.append(
                dict(
                    mine=own(here, local), theirs=partial.at[there], got=arrived.at[local],
                    result=result.at[here], result_other=result.at[there],
                    slot=self.slots.at[len(self.chunks), :, pl.ds(0, rows), pl.ds(0, partial.shape[1])],
                )
            )

    def side(self, k):
        z = lax.axis_index("seq")
        return z if k % 2 == 0 else 3 - z

    def device(self, k, y):
        return {"seq": y if k % 2 == 0 else 3 - y}

    def sem(self, k, n):
        return self.sems.at[k, n]

    def pair(self, k):
        chunk = self.chunks[k]
        c = lax.axis_index("dp")
        return remote(chunk["theirs"], chunk["got"], self.sem(k, 0), self.sem(k, 1), {"dp": 1 - c})

    def partial(self, k, into, y):
        chunk = self.chunks[k]
        return remote(
            chunk["mine"], chunk["slot"].at[into], self.sem(k, 2), self.sem(k, 3 + into), self.device(k, y)
        )

    def outcome(self, k, src, y, send):
        return remote(src, self.chunks[k]["result"], self.sem(k, send), self.sem(k, 5), self.device(k, y))

    def twin(self, k, src):
        c = lax.axis_index("dp")
        return remote(src, self.chunks[k]["result"], self.sem(k, 8), self.sem(k, 9), {"dp": 1 - c})

    def kept(self, k):
        chunk = self.chunks[k]
        return pltpu.make_async_copy(chunk["mine"], chunk["result"], self.sem(k, 10))

    def exchange(self, k):
        self.pair(k).start()

    def combine(self, k):
        chunk, y = self.chunks[k], self.side(k)
        self.pair(k).wait_recv()
        chunk["mine"][...] = chunk["mine"][...] + chunk["got"][...]

        @pl.when(y == 0)
        def _():
            self.partial(k, 0, 1).start()

        @pl.when(y == 3)
        def _():
            self.partial(k, 0, 2).start()

    def middle(self, k):
        chunk, y = self.chunks[k], self.side(k)

        @pl.when(y == 2)
        def _():
            self.partial(k, 0, 3).wait_recv()
            chunk["mine"][...] = chunk["mine"][...] + chunk["slot"][0]
            self.partial(k, 1, 1).start()

    def root(self, k):
        chunk, y = self.chunks[k], self.side(k)

        @pl.when(y == 1)
        def _():
            self.partial(k, 0, 0).wait_recv()
            self.partial(k, 1, 2).wait_recv()
            chunk["mine"][...] = chunk["mine"][...] + chunk["slot"][0] + chunk["slot"][1]
            self.outcome(k, chunk["mine"], 2, 6).start()
            self.outcome(k, chunk["mine"], 0, 7).start()
            self.kept(k).start()
            self.twin(k, chunk["mine"]).start()

    def onward(self, k):
        chunk, y = self.chunks[k], self.side(k)

        @pl.when(y == 2)
        def _():
            self.outcome(k, chunk["result"], 1, 6).wait_recv()
            self.outcome(k, chunk["result"], 3, 6).start()
            self.twin(k, chunk["result"]).start()

    def leaf(self, k):
        chunk, y = self.chunks[k], self.side(k)

        @pl.when(y == 0)
        def _():
            self.outcome(k, chunk["result"], 1, 6).wait_recv()
            self.twin(k, chunk["result"]).start()

        @pl.when(y == 3)
        def _():
            self.outcome(k, chunk["result"], 2, 6).wait_recv()
            self.twin(k, chunk["result"]).start()

    def finish(self, k):
        chunk, y = self.chunks[k], self.side(k)
        c = lax.axis_index("dp")
        self.pair(k).wait_send()
        remote(
            chunk["result_other"], chunk["result_other"], self.sem(k, 8), self.sem(k, 9), {"dp": 1 - c}
        ).wait_recv()
        self.twin(k, chunk["result"]).wait_send()

        @pl.when(y == 0)
        def _():
            self.partial(k, 0, 1).wait_send()

        @pl.when(y == 3)
        def _():
            self.partial(k, 0, 2).wait_send()

        @pl.when(y == 2)
        def _():
            self.partial(k, 1, 1).wait_send()
            self.outcome(k, chunk["result"], 3, 6).wait_send()

        @pl.when(y == 1)
        def _():
            self.outcome(k, chunk["mine"], 2, 6).wait_send()
            self.outcome(k, chunk["mine"], 0, 7).wait_send()
            self.kept(k).wait()

    def tick(self, t):
        for stage, act in enumerate((self.combine, self.middle, self.root, self.onward, self.leaf)):
            k = t - LAGS[stage]
            if 0 <= k < len(self.chunks):
                act(k)


LAGS = (0, 2, 3, 5, 6)
CHUNK = 64


def back_kernel(
    dims,
    resid_in, tok_in, gains_in, proj_in, den_in, prior_in, mix_in, wout_in, wqkv_in, down_in, up_in, bias_in, share_in,
    tok_grad_out, qkv_out, out_out, up_out, down_out, small_out,
    resid, tok, gains, proj, den, prior, mixed, stage_o, stage_q, wo_h, wo_l, wq_h, wq_l,
    rg_h, rg_l, n_h, n_l, xhat, pg_h, pg_l, dnum, dden, state, state_in, later,
    part, buf, xhat_own, inv_own, resid_own, tok_grad, d_out, d_qkv, d_small, d_ffn,
    got_ffn, got_out, got_qkv, got_small, slots,
    norm_sem, state_sem, chunk_sem, load_sem, image_sem, ffn_sem, store_sem,
):
    images, length, used, rows = dims
    width = resid.shape[2]
    z, h, c, near_x, near_y, far = place()
    seq = lax.axis_size("seq")
    row_tile = 16

    def first_copies(i):
        return (
            pltpu.make_async_copy(resid_in.at[i], resid.at[i % 2], image_sem.at[0, i % 2]),
            pltpu.make_async_copy(mix_in.at[i, :, lanes(h)], mixed.at[i], load_sem.at[4 + 4 * i]),
            pltpu.make_async_copy(den_in.at[i], den.at[i], load_sem.at[5 + 4 * i]),
            pltpu.make_async_copy(proj_in.at[i], proj.at[i], load_sem.at[6 + 4 * i]),
            pltpu.make_async_copy(prior_in.at[i], prior.at[i], load_sem.at[7 + 4 * i]),
        )

    def tok_copy(i):
        return pltpu.make_async_copy(tok_in.at[i], tok.at[i % 2], image_sem.at[1, i % 2])

    weights = (
        pltpu.make_async_copy(wout_in, stage_o, load_sem.at[0]),
        pltpu.make_async_copy(wqkv_in, stage_q, load_sem.at[1]),
        pltpu.make_async_copy(gains_in, gains, load_sem.at[2]),
    )
    half = down_in.shape[0] // 2
    own_rows = pl.ds(pl.multiple_of(c * half, 8), half)
    ffn_loads = (
        pltpu.make_async_copy(down_in.at[own_rows], d_ffn.at[0], ffn_sem.at[0]),
        pltpu.make_async_copy(up_in.at[own_rows], d_ffn.at[1], ffn_sem.at[1]),
    )
    small_loads = (
        pltpu.make_async_copy(bias_in, d_small.at[0:8], load_sem.at[3]),
        pltpu.make_async_copy(share_in, d_small.at[8:16, lanes(1)], ffn_sem.at[2]),
    )
    for copy in first_copies(0) + weights:
        copy.start()
    for i in range(1, images):
        for copy in first_copies(i)[1 if i >= 2 else 0 :]:
            copy.start()
    tok_copy(0).start()
    d_small[...] = jnp.zeros_like(d_small)
    enter(
        [{"head": near_x}, {"head": near_y}, {"dp": 1 - c}]
        + [{"seq": lax.rem(z + d, seq)} for d in range(1, seq)]
    )
    reduce = Reduce(slots, chunk_sem)
    reduce.add(down_in, lambda here, local: d_ffn.at[0, local], got_ffn.at[0], down_out, half, CHUNK)
    reduce.add(up_in, lambda here, local: d_ffn.at[1, local], got_ffn.at[1], up_out, half, CHUNK)
    ffn_chunks = len(reduce.chunks)
    reduce.add(d_out, lambda here, local: d_out.at[here], got_out, out_out, d_out.shape[0] // 2, CHUNK)
    out_chunks = len(reduce.chunks)
    reduce.add(d_small, lambda here, local: d_small.at[here], got_small, small_out, 8, 8)
    reduce.add(d_qkv, lambda here, local: d_qkv.at[here], got_qkv, qkv_out, d_qkv.shape[0] // 2, CHUNK)
    for k in range(ffn_chunks):
        reduce.exchange(k)
    for copy in ffn_loads + small_loads:
        copy.start()
    norm = Scatter(lambda i: part.at[i % 2], buf, rows, norm_sem)
    row_ok = lax.broadcasted_iota(jnp.int32, (rows, LANES), 0) < length
    clock = [0]

    def tick(times=1):
        for _ in range(times):
            reduce.tick(clock[0])
            clock[0] += 1

    def state_copy(i, d, step):
        return remote(
            state.at[i], state_in.at[d - 1, i], state_sem.at[0, d - 1, i], state_sem.at[1, d - 1, i],
            {"seq": lax.rem(z + step + seq, seq)},
        )

    def first_half(i):
        for copy in first_copies(i):
            copy.wait()
        split_rows(resid.at[i % 2], rg_h, rg_l, rows, row_tile)
        resid_own[i] = resid[i % 2, :, lanes(h)]
        if i + 2 < images:
            first_copies(i + 2)[0].start()
        dm = dot3((rg_h[...], rg_l[...]), (wo_h[...], wo_l[...]), "nt")
        ones = jnp.where(diagonal_mask(), 1.0, 0.0).astype(BF)
        inverse = 1.0 / den[i]
        dnum[i] = dm * inverse
        dden[i] = -dot2(split(dm * mixed[i]), ones, "nn") * inverse
        query_feat = positive(proj[i, :, lanes(0)])
        state[i, 0:HEAD_DIM, :] = fold(dot3(split(query_feat), split(dnum[i]), "tn"))
        state[i, HEAD_DIM:, :] = jnp.broadcast_to(
            jnp.sum(query_feat * dden[i], axis=0, keepdims=True), (STATE - HEAD_DIM, LANES)
        )
        for d in range(1, seq):

            @pl.when(z >= d)
            def _():
                state_copy(i, d, -d).start()

        mixed_pair = split(mixed[i])

        def one(k, _):
            s = lanes(k)
            term = dot3(mixed_pair, (rg_h[:, s], rg_l[:, s]), "tn")
            d_out[:, s] = term if i == 0 else d_out[:, s] + term
            return 0

        lax.fori_loop(0, width // LANES, one, 0)

    def second_half(i):
        later[...] = jnp.zeros_like(later)
        for d in range(1, seq):

            @pl.when(z + d < seq)
            def _():
                state_copy(i, d, d).wait_recv()
                later[...] = later[...] + state_in[d - 1, i]

        query, key, value = (proj[i, :, lanes(k)] for k in range(3))
        query_feat = positive(query)
        key_feat = jnp.where(row_ok, positive(key), 0.0)
        query_pair, key_pair, value_pair = split(query_feat), split(key_feat), split(value)
        dnum_i, dden_i = dnum[i], dden[i]
        dnum_pair = split(dnum_i)
        prior_pair = split(unfold(prior[i, 0:HEAD_DIM, :]))
        later_pair = split(unfold(later[0:HEAD_DIM, :]))
        fq = dot3(dnum_pair, prior_pair, "nt") + dden_i * prior[i, HEAD_DIM : HEAD_DIM + 1, :]
        fk = dot3(value_pair, later_pair, "nt") + later[HEAD_DIM : HEAD_DIM + 1, :]
        fv = dot3(key_pair, later_pair, "nn")
        row = lax.broadcasted_iota(jnp.int32, (rows, rows), 0)
        col = lax.broadcasted_iota(jnp.int32, (rows, rows), 1)
        causal = col <= row
        for k, mask in enumerate(head_masks(rows)):
            key_h, query_h = pick(mask, key_pair), pick(mask, query_pair)
            scores = split(jnp.where(causal, dot3(query_pair, key_h, "nt"), 0.0))
            pull = dot3(dnum_pair, pick(mask, value_pair), "nt") + dden_i[:, k * HEAD_DIM : k * HEAD_DIM + 1]
            pull = split(jnp.where(causal, pull, 0.0))
            fq = fq + dot3(pull, key_h, "nn")
            fk = fk + dot3(pull, query_h, "tn")
            fv = fv + dot3(scores, pick(mask, dnum_pair), "tn")
        slope = lambda v: jnp.where(v > 0, 1.0, jnp.exp(jnp.minimum(v, 0.0)))
        pg_h[:, lanes(0)], pg_l[:, lanes(0)] = split(fq * slope(query))
        pg_h[:, lanes(1)], pg_l[:, lanes(1)] = split(jnp.where(row_ok, fk * slope(key), 0.0))
        pg_h[:, lanes(2)], pg_l[:, lanes(2)] = split(fv)

    def weight_grads(i):
        tok_copy(i).wait()

        def normed(r, _):
            s = pl.ds(pl.multiple_of(r * row_tile, row_tile), row_tile)
            hat, inv = norm_parts(tok[i % 2, s, :])
            xhat[s, :] = hat
            inv_own[i, s, :] = jnp.broadcast_to(inv, (row_tile, 128))
            n_h[s, :], n_l[s, :] = split(hat * gains[0:1, :])
            return 0

        lax.fori_loop(0, rows // row_tile, normed, 0)
        xhat_own[i] = xhat[:, lanes(h)]
        if i + 1 < images:
            tok_copy(i + 1).start()

        def one(k, _):
            s = lanes(k)
            term = dot3((n_h[:, s], n_l[:, s]), (pg_h[...], pg_l[...]), "tn")
            d_qkv[s, :] = term if i == 0 else d_qkv[s, :] + term
            return 0

        lax.fori_loop(0, width // LANES, one, 0)

    def norm_back(i):
        if i >= 2:
            norm.finish(i - 2)

        def one(k, sums):
            s = lanes(k)
            term = dot3((pg_h[...], pg_l[...]), (wq_h[s, :], wq_l[s, :]), "nt")
            part[i % 2, :, s] = term
            scaled = term * gains[0:1, s]
            return (
                sums[0] + jnp.sum(scaled, axis=-1, keepdims=True),
                sums[1] + jnp.sum(scaled * xhat[:, s], axis=-1, keepdims=True),
            )

        none = jnp.zeros((rows, 1), F32)
        first, second = lax.fori_loop(0, width // LANES, one, (none, none))
        block = to_lanes(first, second, rows)
        for k in range(width // LANES):
            part[i % 2, rows - 8 : rows, lanes(k)] = block
        norm.direct(i)

    def token_back(i):
        both = norm.total(i)
        mean, cross = to_columns(both[rows - 8 : rows], rows)
        own = jnp.where(row_ok, both, 0.0)
        hat = xhat_own[i]
        scaled = own * gains[0:1, lanes(h)]
        share = (scaled - mean * (1.0 / width) - hat * (cross * (1.0 / width))) * inv_own[i, :, 0:1]
        tok_grad[i] = resid_own[i] + share
        d_small[8:9, lanes(0)] = d_small[8:9, lanes(0)] + jnp.sum(own * hat, axis=0, keepdims=True)
        pltpu.make_async_copy(tok_grad.at[i], tok_grad_out.at[i], store_sem.at[i]).start()

    for copy in weights:
        copy.wait()
    split_rows(stage_o, wo_h, wo_l, LANES, row_tile)
    first_half(0)
    for copy in ffn_loads:
        copy.wait()
    tick()
    tick()
    first_half(1)
    tick()
    split_rows(stage_q, wq_h, wq_l, width, row_tile)
    first_half(2)
    tick()
    first_half(3)
    tick()
    for k in range(ffn_chunks, out_chunks):
        reduce.exchange(k)
    for copy in small_loads:
        copy.wait()
    d_small[8:9, lanes(2)] = d_small[9:10, lanes(1)]
    for i in range(images):
        second_half(i)
        tick()
        weight_grads(i)
        tick()
        norm_back(i)
        if i >= 1:
            token_back(i - 1)
        norm.relay(i)
        tick()
    for k in range(out_chunks + 1, len(reduce.chunks)):
        reduce.exchange(k)
    token_back(images - 1)
    reduce.exchange(out_chunks)
    while clock[0] < len(reduce.chunks) + LAGS[-1]:
        tick()
    for i in range(images):
        pltpu.make_async_copy(tok_grad.at[i], tok_grad_out.at[i], store_sem.at[i]).wait()
        if i >= images - 2:
            norm.finish(i)
        for d in range(1, seq):

            @pl.when(z >= d)
            def _(i=i, d=d):
                state_copy(i, d, -d).wait_send()

    for k in range(len(reduce.chunks)):
        reduce.finish(k)


def back_call(resid, tok, gains, proj, den, prior, mix, wout, wqkv, d_down, d_up, d_bias, d_share, length):
    images, rows, width = tok.shape
    hidden = d_down.shape[0]
    used = round_up(length, 8)
    dma = pltpu.SemaphoreType.DMA
    any_spec = pl.BlockSpec(memory_space=pl.ANY)
    shape = lambda *s: jax.ShapeDtypeStruct(s, F32)
    vmem = pltpu.VMEM
    seq = lax.axis_size("seq")
    chunks = 2 * (hidden // 2 // CHUNK) + LANES // 2 // CHUNK + 1 + width // 2 // CHUNK
    return pl.pallas_call(
        functools.partial(back_kernel, (images, length, used, rows)),
        out_shape=(
            shape(images, rows, LANES),
            shape(width, 3 * LANES),
            shape(LANES, width),
            shape(width, hidden),
            shape(hidden, width),
            shape(16, width),
        ),
        in_specs=[any_spec] * 13,
        out_specs=(any_spec,) * 6,
        scratch_shapes=[
            vmem((2, rows, width), F32), vmem((2, rows, width), F32), vmem((8, width), F32),
            vmem((images, rows, 3 * LANES), F32), vmem((images, rows, LANES), F32), vmem((images, STATE, LANES), F32),
            vmem((images, rows, LANES), F32),
            vmem((LANES, width), F32), vmem((width, 3 * LANES), F32),
            vmem((LANES, width), BF), vmem((LANES, width), BF),
            vmem((width, 3 * LANES), BF), vmem((width, 3 * LANES), BF),
            vmem((rows, width), BF), vmem((rows, width), BF), vmem((rows, width), BF), vmem((rows, width), BF),
            vmem((rows, width), F32), vmem((rows, 3 * LANES), BF), vmem((rows, 3 * LANES), BF),
            vmem((images, rows, LANES), F32), vmem((images, rows, LANES), F32),
            vmem((images, STATE, LANES), F32), vmem((seq - 1, images, STATE, LANES), F32), vmem((STATE, LANES), F32),
            vmem((2, rows, width), F32), vmem((images, 6, round_up(rows // 2, 8), LANES), F32),
            vmem((images, rows, LANES), F32), vmem((images, rows, 128), F32), vmem((images, rows, LANES), F32),
            vmem((images, rows, LANES), F32),
            vmem((LANES, width), F32), vmem((width, 3 * LANES), F32), vmem((16, width), F32),
            vmem((2, hidden // 2, width), F32), vmem((2, hidden // 2, width), F32),
            vmem((LANES // 2, width), F32), vmem((width // 2, 3 * LANES), F32), vmem((8, width), F32),
            vmem((chunks, 2, CHUNK, width), F32),
            dma((images, Scatter.SEMS)), dma((2, seq - 1, images)), dma((chunks, Reduce.SEMS)),
            dma((4 + 4 * images,)), dma((2, 2)), dma((3,)), dma((images,)),
        ],
        compiler_params=pltpu.CompilerParams(
            collective_id=2, has_side_effects=True, vmem_limit_bytes=VMEM_BYTES
        ),
    )(resid, tok, gains, proj, den, prior, mix, wout, wqkv, d_down, d_up, d_bias, d_share)


def fast_device(
    tokens,
    gain_attn,
    qkv_weight,
    out_weight,
    gain_ffn,
    up_weight,
    up_bias,
    down_weight,
    down_bias,
    out_grad,
):
    block_len, local_width = tokens.shape[1:]
    model_width = qkv_weight.shape[0]
    rows = round_up(round_up(block_len, 8) + 8, 16)
    pad = ((0, 0), (0, rows - block_len), (0, 0))
    proj_weight = qkv_weight.reshape(model_width, 3 * local_width)

    def wide(*vectors):
        blank = jnp.zeros((8 - len(vectors), vectors[0].shape[0]), jnp.float32)
        return jnp.concatenate([v[None] for v in vectors] + [blank])

    tok, gains, proj, den, prior, mix, wout = attend_call(
        jnp.pad(tokens, pad), wide(gain_attn, gain_ffn), proj_weight, out_weight, block_len
    )
    out, resid_grad, d_down, d_up, d_bias, d_share = ffn_call(
        tok, mix, gains, wout.reshape(model_width, model_width), up_weight, wide(up_bias), down_weight,
        wide(down_bias), jnp.pad(out_grad, pad), block_len,
    )
    tok_grad, d_qkv, d_out, d_up, d_down, small = back_call(
        resid_grad, tok, gains, proj, den, prior, mix, out_weight, proj_weight, d_down, d_up, d_bias, d_share,
        block_len,
    )
    return (
        out[:, :block_len],
        tok_grad[:, :block_len],
        small[8, 0:LANES],
        d_qkv.reshape(qkv_weight.shape),
        d_out,
        small[8, LANES : 2 * LANES],
        d_up,
        small[0],
        d_down,
        small[8, 2 * LANES : 3 * LANES],
    )


def device_function(mesh):
    if mesh.shape["head"] == 4 and mesh.shape["dp"] == 2:
        return fast_device
    return per_device


def solution(mesh):
    return jax.shard_map(
        device_function(mesh),
        mesh=mesh,
        in_specs=(
            P("dp", "seq", "head"),
            P("head"),
            P(None, None, "head"),
            P("head", None),
            P("head"),
            P(None, "head"),
            P("head"),
            P("head", None),
            P("head"),
            P("dp", "seq", "head"),
        ),
        out_specs=(
            P("dp", "seq", "head"),
            P("dp", "seq", "head"),
            P("head"),
            P(None, None, "head"),
            P("head", None),
            P("head"),
            P(None, "head"),
            P("head"),
            P("head", None),
            P("head"),
        ),
        check_vma=False,
    )
```

```python
import functools

import jax
import jax.numpy as jnp
from jax import lax
from jax.experimental import pallas as pl
from jax.experimental.pallas import tpu as pltpu
from jax.sharding import PartitionSpec as P

HEAD_DIM = 64


highest = lax.Precision.HIGH
norm_eps = 1e-05


def entering(part, axis, combine, identity, reverse):
    count = lax.axis_size(axis)
    place = lax.axis_index(axis)
    ahead = count - 1 - place if reverse else place
    gathered = jax.tree.map(lambda a: lax.all_gather(a, axis), part)
    state = jax.tree.map(lambda a, e: jnp.zeros_like(a) + jnp.asarray(e, a.dtype), part, identity)

    def one(turn, state):
        source = count - 1 - turn if reverse else turn
        return combine(
            state, jax.tree.map(lambda a: lax.dynamic_index_in_dim(a, source, 0, False), gathered)
        )

    return lax.fori_loop(0, ahead, one, state)


def feature(values_in):
    return jax.nn.elu(values_in) + 1.0


def layer_norm(values_in, gain):
    row_mean = jnp.mean(values_in, axis=-1, keepdims=True)
    centred = values_in - row_mean
    row_var = jnp.mean(centred * centred, axis=-1, keepdims=True)
    return centred * lax.rsqrt(row_var + norm_eps) * gain


def norm_back(partial_grad, rows_full, gain_full, gain_share):
    local_width = gain_share.shape[0]
    model_width = gain_full.shape[0]
    row_mean = jnp.mean(rows_full, axis=-1, keepdims=True)
    centred = rows_full - row_mean
    row_inv = lax.rsqrt(jnp.mean(centred * centred, axis=-1, keepdims=True) + norm_eps)
    scaled = partial_grad * gain_full
    sums = lax.psum(
        jnp.stack(
            [jnp.sum(scaled, axis=-1), jnp.sum(scaled * (centred * row_inv), axis=-1)]
        ),
        "head",
    )
    means = (sums / model_width)[:, :, None]
    share = lax.psum_scatter(partial_grad, "head", scatter_dimension=1, tiled=True)
    start = lax.axis_index("head") * local_width
    xhat = lax.dynamic_slice_in_dim(centred, start, local_width, 1) * row_inv
    back = (share * gain_share - means[0] - xhat * means[1]) * row_inv
    return back, jnp.sum(share * xhat, axis=0)


def mlp_act(values_in):
    return jax.nn.gelu(values_in, approximate=True)


def block_attend(query_proj, key_proj, value_proj, prior_state, prior_total):
    query_feat = feature(query_proj)
    key_feat = feature(key_proj)
    length_now = query_proj.shape[1]
    scores = jnp.einsum("gihe,gjhe->ghij", query_feat, key_feat, precision=highest)
    row_index = lax.broadcasted_iota(jnp.int32, (length_now, length_now), 0)
    col_index = lax.broadcasted_iota(jnp.int32, (length_now, length_now), 1)
    scores = jnp.where(col_index <= row_index, scores, jnp.float32(0.0))
    numerator = jnp.einsum("ghij,gjhe->gihe", scores, value_proj, precision=highest)
    numerator = numerator + jnp.einsum(
        "gihe,ghef->gihf", query_feat, prior_state, precision=highest
    )
    denominator = jnp.sum(scores, axis=-1) + jnp.einsum(
        "gihe,ghe->ghi", query_feat, prior_total, precision=highest
    )
    return numerator / jnp.transpose(denominator, (0, 2, 1))[..., None]


def block_state(key_proj, value_proj):
    key_feat = feature(key_proj)
    kv_sum = jnp.einsum("gihe,gihf->ghef", key_feat, value_proj, precision=highest)
    return (kv_sum, jnp.sum(key_feat, axis=1))


def add_pair(earlier, later):
    return (earlier[0] + later[0], earlier[1] + later[1])


def per_device(
    tokens,
    gain_attn,
    qkv_weight,
    out_weight,
    gain_ffn,
    up_weight,
    up_bias,
    down_weight,
    down_bias,
    out_grad,
):
    image_count, block_len, local_width = tokens.shape
    row_count = image_count * block_len
    model_width = qkv_weight.shape[0]
    heads_local = local_width // HEAD_DIM
    column_start = lax.axis_index("head") * local_width
    full_tokens, gain_first, gain_second = (
        lax.all_gather(tokens, "head", axis=2, tiled=True),
        lax.all_gather(gain_attn, "head", axis=0, tiled=True),
        lax.all_gather(gain_ffn, "head", axis=0, tiled=True),
    )
    token_rows = full_tokens.reshape(row_count, model_width)
    normed_one = layer_norm(token_rows, gain_first)
    proj_weight = qkv_weight.reshape(model_width, 3 * local_width)
    projected = jnp.dot(normed_one, proj_weight, precision=highest)
    parts_view = projected.reshape(image_count, block_len, 3, heads_local, HEAD_DIM)
    query_proj = parts_view[:, :, 0]
    key_proj = parts_view[:, :, 1]
    value_proj = parts_view[:, :, 2]
    (own_state, own_total), pull_state = jax.vjp(block_state, key_proj, value_proj)
    zero_pair = (jnp.zeros_like(own_state), jnp.zeros_like(own_total))
    prior_state, prior_total = entering((own_state, own_total), "seq", add_pair, zero_pair, False)
    mixed, pull_attend = jax.vjp(
        block_attend, query_proj, key_proj, value_proj, prior_state, prior_total
    )
    mixed_rows = mixed.reshape(row_count, local_width)
    branch_out = jnp.dot(mixed_rows, out_weight, precision=highest)
    token_share = tokens.reshape(row_count, local_width)
    resid_share = token_share + lax.psum_scatter(
        branch_out, "head", scatter_dimension=1, tiled=True
    )
    resid_full = lax.all_gather(resid_share, "head", axis=1, tiled=True)
    normed_two = layer_norm(resid_full, gain_second)
    up_proj = jnp.dot(normed_two, up_weight, precision=highest) + up_bias
    hidden, pull_act = jax.vjp(mlp_act, up_proj)
    down_proj = jnp.dot(hidden, down_weight, precision=highest)
    ffn_share = lax.psum_scatter(down_proj, "head", scatter_dimension=1, tiled=True)
    output = (resid_share + ffn_share + down_bias).reshape(tokens.shape)
    grad_share = out_grad.reshape(row_count, local_width)
    grad_full = lax.all_gather(grad_share, "head", axis=1, tiled=True)
    down_bias_grad = jnp.sum(grad_share, axis=0)
    down_weight_grad = jnp.dot(hidden.T, grad_full, precision=highest)
    hidden_grad = jnp.dot(grad_full, down_weight.T, precision=highest)
    (up_grad,) = pull_act(hidden_grad)
    up_bias_grad = jnp.sum(up_grad, axis=0)
    up_weight_grad = jnp.dot(normed_two.T, up_grad, precision=highest)
    ffn_grads = lax.psum((up_weight_grad, down_weight_grad), ("seq", "dp"))
    resid_back, gain_ffn_share = norm_back(
        jnp.dot(up_grad, up_weight.T, precision=highest), resid_full, gain_second, gain_ffn
    )
    resid_grad_share = grad_share + resid_back
    resid_grad = lax.all_gather(resid_grad_share, "head", axis=1, tiled=True)
    out_weight_grad = jnp.dot(mixed_rows.T, resid_grad, precision=highest)
    mixed_grad = jnp.dot(resid_grad, out_weight.T, precision=highest).reshape(mixed.shape)
    query_grad, key_grad, value_grad, state_grad, total_grad = pull_attend(mixed_grad)
    later_state, later_total = entering((state_grad, total_grad), "seq", add_pair, zero_pair, True)
    key_extra, value_extra = pull_state((later_state, later_total))
    key_grad = key_grad + key_extra
    value_grad = value_grad + value_extra
    proj_grad = jnp.stack([query_grad, key_grad, value_grad], axis=2).reshape(
        row_count, 3 * local_width
    )
    qkv_weight_grad = jnp.dot(normed_one.T, proj_grad, precision=highest).reshape(qkv_weight.shape)
    token_back, gain_attn_share = norm_back(
        jnp.dot(proj_grad, proj_weight.T, precision=highest), token_rows, gain_first, gain_attn
    )
    tokens_grad = (resid_grad_share + token_back).reshape(tokens.shape)
    summed_grads = lax.psum(
        (
            gain_attn_share,
            qkv_weight_grad,
            out_weight_grad,
            gain_ffn_share,
            up_bias_grad,
            down_bias_grad,
        ),
        ("seq", "dp"),
    )
    return (
        output,
        tokens_grad,
        summed_grads[0],
        summed_grads[1],
        summed_grads[2],
        summed_grads[3],
        ffn_grads[0],
        summed_grads[4],
        ffn_grads[1],
        summed_grads[5],
    )


MESH = pl.DeviceIdType.MESH
BF = jnp.bfloat16
F32 = jnp.float32
LANES = 256
DIMS = {
    "nn": (((1,), (0,)), ((), ())),
    "nt": (((1,), (1,)), ((), ())),
    "tn": (((0,), (0,)), ((), ())),
}


def round_up(value, step):
    return -(-value // step) * step


def padded(length):
    return round_up(round_up(length, 8) + 8, 16)


def row_blocks(rows):
    return [slice(r, r + 16) for r in range(0, rows, 16)]


def pad_rows(raw, slots, i, h):
    length, rows = raw.shape[1], slots.shape[1]
    slots[i, 0:length, lanes(h)] = raw[i]
    slots[i, length:rows, lanes(h)] = jnp.zeros((rows - length, LANES), F32)


def dot(left, right, kind):
    return lax.dot_general(left, right, DIMS[kind], preferred_element_type=F32)


def split(values):
    high = values.astype(BF)
    return high, (values - high.astype(F32)).astype(BF)


def dot3(left, right, kind):
    return (
        dot(left[0], right[0], kind) + dot(left[0], right[1], kind) + dot(left[1], right[0], kind)
    )


def dot2(left, right, kind):
    return dot(left[0], right, kind) + dot(left[1], right, kind)


def lanes(index):
    if isinstance(index, int):
        return pl.ds(index * LANES, LANES)
    return pl.ds(pl.multiple_of(index * LANES, LANES), LANES)


def place():
    z, h, c = lax.axis_index("seq"), lax.axis_index("head"), lax.axis_index("dp")
    near_x = h + 1 - 2 * lax.rem(h, 2)
    near_y = lax.rem(h + 2, 4)
    return z, h, c, near_x, near_y, 3 - h


def remote(src, dst, send, recv, device):
    return pltpu.make_async_remote_copy(
        src_ref=src, dst_ref=dst, send_sem=send, recv_sem=recv, device_id=device, device_id_type=MESH
    )


def enter(targets):
    barrier = pltpu.get_barrier_semaphore()
    for device in targets:
        pl.semaphore_signal(barrier, inc=1, device_id=device, device_id_type=MESH)
    pl.semaphore_wait(barrier, len(targets))


class Gather:
    SEMS = 8

    def __init__(self, own, slots, rows, sems):
        self.own, self.slots, self.sems = own, slots, sems
        self.half = round_up(rows // 2, 8)
        self.rows = rows

    def copies(self, i):
        _, h, _, near_x, near_y, _ = place()
        slots, sems = self.slots, self.sems
        first, second = pl.ds(0, self.half), pl.ds(self.half, self.rows - self.half)
        every = pl.ds(0, self.rows)

        def one(src, dst, place_in, device):
            return remote(src, dst, sems.at[i, place_in], sems.at[i, 4 + place_in], {"head": device})

        own = self.own(i)
        return (
            one(own.at[every], slots.at[i, every, lanes(h)], 0, near_x),
            one(own.at[every], slots.at[i, every, lanes(h)], 1, near_y),
            one(slots.at[i, first, lanes(near_x)], slots.at[i, first, lanes(near_x)], 2, near_y),
            one(slots.at[i, second, lanes(near_y)], slots.at[i, second, lanes(near_y)], 3, near_x),
        )

    def arrivals(self, i):
        _, h, _, near_x, near_y, far = place()
        slots, sems = self.slots, self.sems
        first, second = pl.ds(0, self.half), pl.ds(self.half, self.rows - self.half)
        every = pl.ds(0, self.rows)

        def one(dst, place_in, device):
            return remote(dst, dst, sems.at[i, place_in], sems.at[i, 4 + place_in], {"head": device})

        return (
            one(slots.at[i, every, lanes(near_x)], 0, near_x),
            one(slots.at[i, every, lanes(near_y)], 1, near_y),
            one(slots.at[i, first, lanes(far)], 2, near_y),
            one(slots.at[i, second, lanes(far)], 3, near_x),
        )

    def direct(self, i):
        x, y, _, _ = self.copies(i)
        x.start()
        y.start()

    def forward(self, i):
        x, y, _, _ = self.arrivals(i)
        x.wait_recv()
        y.wait_recv()
        _, _, to_y, to_x = self.copies(i)
        to_y.start()
        to_x.start()

    def ready(self, i):
        _, _, x, y = self.arrivals(i)
        x.wait_recv()
        y.wait_recv()

    def finish(self, i):
        for copy in self.copies(i):
            copy.wait_send()


def head_masks(rows):
    head = lax.broadcasted_iota(jnp.int32, (rows, LANES), 1) // HEAD_DIM
    return [head == k for k in range(LANES // HEAD_DIM)]


def diagonal_mask():
    rows = lax.broadcasted_iota(jnp.int32, (LANES, LANES), 0) // HEAD_DIM
    cols = lax.broadcasted_iota(jnp.int32, (LANES, LANES), 1) // HEAD_DIM
    return rows == cols


def pick(mask, pair):
    zero = jnp.zeros((), BF)
    return jnp.where(mask, pair[0], zero), jnp.where(mask, pair[1], zero)


def fold(square):
    square = jnp.where(diagonal_mask(), square, 0.0)
    return (
        square[0:HEAD_DIM]
        + square[HEAD_DIM : 2 * HEAD_DIM]
        + square[2 * HEAD_DIM : 3 * HEAD_DIM]
        + square[3 * HEAD_DIM :]
    )


def unfold(wide):
    return jnp.where(diagonal_mask(), jnp.concatenate([wide] * 4, axis=0), 0.0)


def positive(values):
    return jnp.where(values > 0, values + 1.0, jnp.exp(jnp.minimum(values, 0.0)))


def norm_parts(rows):
    row_mean = jnp.mean(rows, axis=-1, keepdims=True)
    centred = rows - row_mean
    row_inv = lax.rsqrt(jnp.mean(centred * centred, axis=-1, keepdims=True) + norm_eps)
    return centred * row_inv, row_inv


def split_rows(source, high, low, rows, step):
    def one(r, _):
        s = pl.ds(pl.multiple_of(r * step, step), step)
        high[s, :], low[s, :] = split(source[s, :])
        return 0

    lax.fori_loop(0, rows // step, one, 0)


STATE = HEAD_DIM + 8


def attend_kernel(
    dims,
    tok_in, gains_in, wqkv_in, wout_in,
    tok_out, gains_out, proj_out, den_out, prior_out, mix_out, wout_out,
    raw, tok, mix, gains, proj, den, prior, state, state_in, wstage, w_h, w_l, n_h, n_l, wout,
    tok_sem, mix_sem, gain_sem, state_sem, out_sem, pair_sem, load_sem, store_sem,
):
    images, length, used, rows = dims
    width = tok.shape[2]
    z, h, c, near_x, near_y, far = place()
    seq = lax.axis_size("seq")
    out_half = wout_in.shape[0] // 2

    loads = [
        pltpu.make_async_copy(tok_in.at[i], raw.at[i], load_sem.at[i]) for i in range(images)
    ]
    loads += [
        pltpu.make_async_copy(wqkv_in.at[pl.ds(j * width, width)], wstage.at[:, lanes(j)], load_sem.at[images + j])
        for j in range(3)
    ]
    loads.append(pltpu.make_async_copy(gains_in, gains.at[:, lanes(h)], load_sem.at[images + 3]))
    for copy in loads:
        copy.start()

    blank = jnp.zeros((rows - used, LANES), F32)
    for i in range(images):
        for other in (near_x, near_y, far):
            tok[i, used:rows, lanes(other)] = blank
    for i in range(images):
        loads[i].wait()
        pad_rows(raw, tok, i, h)

    enter(
        [{"head": near_x}, {"head": near_y}, {"head": far}, {"dp": 1 - c}]
        + [{"seq": lax.rem(z + d, seq)} for d in range(1, seq)]
    )
    tokens = Gather(lambda i: tok.at[i, :, lanes(h)], tok, used, tok_sem)
    mixes = Gather(lambda i: mix.at[i, :, lanes(h)], mix, used, mix_sem)
    own_half = pl.ds(pl.multiple_of(c * out_half, out_half), out_half)
    tokens.direct(0)
    gain_copies = [
        remote(gains_in, gains.at[:, lanes(h)], gain_sem.at[k], gain_sem.at[3 + k], {"head": other})
        for k, other in enumerate((near_x, near_y, far))
    ]
    for copy in gain_copies:
        copy.start()
    tokens.direct(1)
    for copy in loads[images:]:
        copy.wait()
    split_rows(wstage, w_h, w_l, wstage.shape[0], 64)
    for k, other in enumerate((near_x, near_y, far)):
        remote(
            gains.at[:, lanes(other)], gains.at[:, lanes(other)], gain_sem.at[k], gain_sem.at[3 + k],
            {"head": other},
        ).wait_recv()
    row_ok = lax.broadcasted_iota(jnp.int32, (rows, LANES), 0) < length

    def project(i):

        for s in row_blocks(rows):
            n_h[s, :], n_l[s, :] = split(norm_parts(tok[i, s, :])[0] * gains[0:1, :])
        proj[i] = dot3((n_h[...], n_l[...]), (w_h[...], w_l[...]), "nn")
        key_feat = jnp.where(row_ok, positive(proj[i, :, lanes(1)]), 0.0)
        state[i, 0:HEAD_DIM, :] = fold(dot3(split(key_feat), split(proj[i, :, lanes(2)]), "tn"))
        state[i, HEAD_DIM:, :] = jnp.broadcast_to(
            jnp.sum(key_feat, axis=0, keepdims=True), (STATE - HEAD_DIM, LANES)
        )
        for d in range(1, seq):

            @pl.when(z + d < seq)
            def _():
                state_copy(i, d, d).start()

    def state_copy(i, d, step):
        return remote(
            state.at[i], state_in.at[d - 1, i], state_sem.at[0, d - 1, i], state_sem.at[1, d - 1, i],
            {"seq": lax.rem(z + step + seq, seq)},
        )

    def attend(i):
        prior[i] = jnp.zeros((STATE, LANES), F32)
        for d in range(1, seq):

            @pl.when(z >= d)
            def _():
                state_copy(i, d, -d).wait_recv()
                prior[i] = prior[i] + state_in[d - 1, i]

        query_feat = positive(proj[i, :, lanes(0)])
        key_feat = jnp.where(row_ok, positive(proj[i, :, lanes(1)]), 0.0)
        query_pair, key_pair = split(query_feat), split(key_feat)
        value_pair = split(proj[i, :, lanes(2)])
        total = prior[i, HEAD_DIM : HEAD_DIM + 1, :]
        ones = jnp.where(diagonal_mask(), 1.0, 0.0).astype(BF)
        num = dot3(query_pair, split(unfold(prior[i, 0:HEAD_DIM, :])), "nn")
        below = dot2(split(query_feat * total), ones, "nn")
        row = lax.broadcasted_iota(jnp.int32, (rows, rows), 0)
        col = lax.broadcasted_iota(jnp.int32, (rows, rows), 1)
        for mask in head_masks(rows):
            scores = dot3(query_pair, pick(mask, key_pair), "nt")
            score_pair = split(jnp.where(col <= row, scores, 0.0))
            num = num + dot3(score_pair, pick(mask, value_pair), "nn")
            below = below + dot2(score_pair, jnp.where(mask, 1.0, 0.0).astype(BF), "nn")
        den[i] = below
        mix[i, :, lanes(h)] = jnp.where(row_ok, num / below, 0.0)
        blank_rows = jnp.zeros((rows - used, LANES), F32)
        for other in (near_x, near_y, far):
            mix[i, used:rows, lanes(other)] = blank_rows

    out_copies = [
        remote(
            wout_in.at[own_half], wout.at[h, own_half], out_sem.at[0, k], out_sem.at[1, k], {"head": other}
        )
        for k, other in enumerate((near_x, near_y, far))
    ]
    out_own = pltpu.make_async_copy(wout_in, wout.at[h], load_sem.at[images + 4])

    def out_arrival(k, other):
        return remote(
            wout.at[other, own_half], wout.at[other, own_half], out_sem.at[0, k], out_sem.at[1, k],
            {"head": other},
        )

    def pair_copy(k, other, which):
        half = pl.ds(pl.multiple_of(which * out_half, out_half), out_half)
        return remote(
            wout.at[other, half], wout.at[other, half], pair_sem.at[0, k], pair_sem.at[1, k],
            {"dp": 1 - c},
        )

    peers = tuple(enumerate((near_x, near_y, far)))
    stores = []

    def store(src, dst):
        copy = pltpu.make_async_copy(src, dst, store_sem.at[len(stores)])
        copy.start()
        stores.append(copy)

    for t in range(images + 2):
        if t < images:
            tokens.forward(t)
            if t + 2 < images:
                tokens.direct(t + 2)
            elif t == images - 1:
                for copy in out_copies:
                    copy.start()
                out_own.start()
        if 1 <= t <= images:
            tokens.ready(t - 1)
            project(t - 1)
            store(tok.at[t - 1], tok_out.at[t - 1])
            store(proj.at[t - 1], proj_out.at[t - 1])
        if t >= 2:
            attend(t - 2)
            mixes.direct(t - 2)
            store(den.at[t - 2], den_out.at[t - 2])
            store(prior.at[t - 2], prior_out.at[t - 2])
    store(gains, gains_out)
    out_own.wait()
    for k, other in peers:
        out_arrival(k, other).wait_recv()
        pair_copy(k, other, c).start()
    for i in range(images):
        mixes.forward(i)
    for k, other in peers:
        pair_copy(k, other, 1 - c).wait_recv()
    store(wout, wout_out)
    for i in range(images):
        mixes.ready(i)
        store(mix.at[i], mix_out.at[i])
    for i in range(images):
        tokens.finish(i)
        mixes.finish(i)
        for d in range(1, seq):

            @pl.when(z + d < seq)
            def _(i=i, d=d):
                state_copy(i, d, d).wait_send()

    for copy in gain_copies + out_copies:
        copy.wait_send()
    for k, other in peers:
        pair_copy(k, other, c).wait_send()
    for copy in stores:
        copy.wait()


def attend_call(tokens, gains, wqkv, wout):
    images, length, _ = tokens.shape
    used = round_up(length, 8)
    rows = padded(length)
    width = wqkv.shape[0] // 3
    heads_n = width // LANES
    dma = pltpu.SemaphoreType.DMA
    seq = lax.axis_size("seq")
    any_spec = pl.BlockSpec(memory_space=pl.ANY)
    shape = lambda *s: jax.ShapeDtypeStruct(s, F32)
    return pl.pallas_call(
        functools.partial(attend_kernel, (images, length, used, rows)),
        out_shape=(
            shape(images, rows, width),
            shape(8, width),
            shape(images, rows, 3 * LANES),
            shape(images, rows, LANES),
            shape(images, STATE, LANES),
            shape(images, rows, width),
            shape(heads_n, LANES, width),
        ),
        in_specs=[any_spec] * 4,
        out_specs=(any_spec,) * 7,
        scratch_shapes=[
            pltpu.VMEM((images, length, LANES), F32),
            pltpu.VMEM((images, rows, width), F32),
            pltpu.VMEM((images, rows, width), F32),
            pltpu.VMEM((8, width), F32),
            pltpu.VMEM((images, rows, 3 * LANES), F32),
            pltpu.VMEM((images, rows, LANES), F32),
            pltpu.VMEM((images, STATE, LANES), F32),
            pltpu.VMEM((images, STATE, LANES), F32),
            pltpu.VMEM((seq - 1, images, STATE, LANES), F32),
            pltpu.VMEM((width, 3 * LANES), F32),
            pltpu.VMEM((width, 3 * LANES), BF),
            pltpu.VMEM((width, 3 * LANES), BF),
            pltpu.VMEM((rows, width), BF),
            pltpu.VMEM((rows, width), BF),
            pltpu.VMEM((heads_n, LANES, width), F32),
            dma((images, Gather.SEMS)),
            dma((images, Gather.SEMS)),
            dma((6,)),
            dma((2, seq - 1, images)),
            dma((2, 3)),
            dma((2, 3)),
            dma((images + 5,)),
            dma((5 * images + 4,)),
        ],
        compiler_params=pltpu.CompilerParams(
            collective_id=0, has_side_effects=True, vmem_limit_bytes=VMEM_BYTES
        ),
    )(tokens, gains, wqkv, wout)


VMEM_BYTES = 60 * 1024 * 1024
class Scatter:
    SEMS = 12

    def __init__(self, part, buffers, rows, sems):
        self.part, self.buffers, self.sems = part, buffers, sems
        self.half = round_up(rows // 2, 8)
        self.rows = rows
        self.first, self.second = pl.ds(0, self.half), pl.ds(self.half, rows - self.half)
        self.left = pl.ds(0, rows - self.half)

    def slot(self, i, k):
        rows = self.first if k in (0, 2, 5) else self.left
        return self.buffers.at[i, k, rows]

    def copy(self, i, k, src, into=None):
        _, _, _, near_x, near_y, _ = place()
        into = k if into is None else into
        device = near_x if into in (0, 2, 4) else near_y
        return remote(
            src, self.slot(i, into), self.sems.at[i, into], self.sems.at[i, 6 + into], {"head": device}
        )

    def sent(self, i):
        _, _, _, near_x, near_y, far = place()
        part = self.part(i)
        return (
            self.copy(i, 2, part.at[self.first, lanes(far)]),
            self.copy(i, 3, part.at[self.second, lanes(far)]),
            self.copy(i, 0, part.at[self.first, lanes(near_x)]),
            self.copy(i, 1, part.at[self.second, lanes(near_y)]),
        )

    def passed(self, i):
        return (
            self.copy(i, 2, self.slot(i, 2), 5),
            self.copy(i, 3, self.slot(i, 3), 4),
        )

    def direct(self, i):
        for copy in self.sent(i):
            copy.start()

    def relay(self, i):
        _, _, _, near_x, near_y, _ = place()
        part = self.part(i)
        to_y, to_x = self.passed(i)
        self.copy(i, 2, self.slot(i, 2)).wait_recv()
        self.buffers[i, 2, self.first] = self.buffers[i, 2, self.first] + part[self.first, lanes(near_y)]
        to_y.start()
        self.copy(i, 3, self.slot(i, 3)).wait_recv()
        self.buffers[i, 3, self.left] = self.buffers[i, 3, self.left] + part[self.second, lanes(near_x)]
        to_x.start()

    def total(self, i):
        _, h, _, _, _, _ = place()
        part = self.part(i)
        for k in (0, 5, 1, 4):
            self.copy(i, k, self.slot(i, k)).wait_recv()
        first = (
            part[self.first, lanes(h)] + self.buffers[i, 0, self.first] + self.buffers[i, 5, self.first]
        )
        second = part[self.second, lanes(h)] + self.buffers[i, 1, self.left] + self.buffers[i, 4, self.left]
        return jnp.concatenate([first, second], axis=0)

    def finish(self, i):
        for copy in self.sent(i) + self.passed(i):
            copy.wait_send()


def activation(values):
    scale = 0.7978845608028654
    square = values * values
    bent = jnp.tanh(scale * values * (1.0 + 0.044715 * square))
    half = 0.5 * (1.0 + bent)
    slope = half + 0.5 * values * (1.0 - bent * bent) * (scale * (1.0 + 0.134145 * square))
    return values * half, slope


def to_lanes(first, second, rows):
    lane = lax.broadcasted_iota(jnp.int32, (rows, 128), 1)
    both = jnp.where(lane == 0, first, jnp.where(lane == 1, second, 0.0))
    both = jnp.concatenate([both, jnp.zeros((LANES - rows, 128), F32)], axis=0)
    return jnp.transpose(both)[0:8]


def to_columns(block, rows):
    tall = jnp.concatenate([block, jnp.zeros((120, LANES), F32)], axis=0)
    turned = jnp.transpose(tall)[0:rows]
    return turned[:, 0:1], turned[:, 1:2]


class Reduce:
    SEMS = 12
    RING = 8
    LATE = 2

    def __init__(self, sems, total):
        self.sems, self.total = sems, total
        self.chunks = []
        self.clock = 0
        self.ready = 0

    def chunk(self, mine, theirs, got, result, result_other, room):
        self.chunks.append(
            dict(mine=mine, theirs=theirs, got=got, result=result, result_other=result_other, slot=room)
        )

    def add(self, partial, arrived, result, rows, ring):
        c = lax.axis_index("dp")
        half = partial.shape[0] // 2
        for r in range(half // rows):
            here = pl.ds(pl.multiple_of(c * half + r * rows, 8), rows)
            there = pl.ds(pl.multiple_of((1 - c) * half + r * rows, 8), rows)
            self.chunk(
                partial.at[here], partial.at[there], arrived.at[pl.ds(r * rows, rows)],
                result.at[here], result.at[there], ring.at[len(self.chunks) % self.RING, :, pl.ds(0, rows)],
            )
        return len(self.chunks)

    def add_columns(self, partial, arrived, result, rows, ring):
        c = lax.axis_index("dp")
        depth = partial.shape[0]
        half = depth // 2
        for j in range(partial.shape[1] // LANES):
            for r in range(half // rows):
                here = pl.multiple_of(c * half + r * rows, 8)
                there = pl.multiple_of((1 - c) * half + r * rows, 8)
                self.chunk(
                    partial.at[pl.ds(here, rows), lanes(j)], partial.at[pl.ds(there, rows), lanes(j)],
                    arrived.at[pl.ds(j * half + r * rows, rows)],
                    result.at[pl.ds(j * depth + here, rows)], result.at[pl.ds(j * depth + there, rows)],
                    ring.at[len(self.chunks) % self.RING],
                )
        return len(self.chunks)

    def side(self, k):
        z = lax.axis_index("seq")
        return z if k % 2 == 0 else 3 - z

    def device(self, k, y):
        return {"seq": y if k % 2 == 0 else 3 - y}

    def sem(self, k, n):
        return self.sems.at[k, n]

    def pair(self, k):
        chunk = self.chunks[k]
        c = lax.axis_index("dp")
        return remote(chunk["theirs"], chunk["got"], self.sem(k, 0), self.sem(k, 1), {"dp": 1 - c})

    def partial(self, k, into, y):
        chunk = self.chunks[k]
        return remote(
            chunk["mine"], chunk["slot"].at[into], self.sem(k, 2), self.sem(k, 3 + into), self.device(k, y)
        )

    def outcome(self, k, src, y, send):
        return remote(src, self.chunks[k]["result"], self.sem(k, send), self.sem(k, 5), self.device(k, y))

    def twin(self, k, src):
        c = lax.axis_index("dp")
        return remote(src, self.chunks[k]["result"], self.sem(k, 8), self.sem(k, 9), {"dp": 1 - c})

    def kept(self, k):
        chunk = self.chunks[k]
        return pltpu.make_async_copy(chunk["mine"], chunk["result"], self.sem(k, 10))

    def exchange(self, first, end):
        for k in range(first, end):
            self.pair(k).start()
        self.ready = end

    def combine(self, k):
        chunk, y = self.chunks[k], self.side(k)
        self.pair(k).wait_recv()
        chunk["mine"][...] = chunk["mine"][...] + chunk["got"][...]

        @pl.when(y == 0)
        def _():
            self.partial(k, 0, 1).start()

        @pl.when(y == 3)
        def _():
            self.partial(k, 0, 2).start()

    def middle(self, k):
        chunk, y = self.chunks[k], self.side(k)

        @pl.when(y == 2)
        def _():
            self.partial(k, 0, 3).wait_recv()
            chunk["mine"][...] = chunk["mine"][...] + chunk["slot"][0]
            self.partial(k, 1, 1).start()

    def root(self, k):
        chunk, y = self.chunks[k], self.side(k)

        @pl.when(y == 1)
        def _():
            self.partial(k, 0, 0).wait_recv()
            self.partial(k, 1, 2).wait_recv()
            chunk["mine"][...] = chunk["mine"][...] + chunk["slot"][0] + chunk["slot"][1]
            self.outcome(k, chunk["mine"], 2, 6).start()
            self.outcome(k, chunk["mine"], 0, 7).start()
            self.kept(k).start()
            self.twin(k, chunk["mine"]).start()

    def onward(self, k):
        chunk, y = self.chunks[k], self.side(k)

        @pl.when(y == 2)
        def _():
            self.outcome(k, chunk["result"], 1, 6).wait_recv()
            self.outcome(k, chunk["result"], 3, 6).start()
            self.twin(k, chunk["result"]).start()

    def leaf(self, k):
        chunk, y = self.chunks[k], self.side(k)

        @pl.when(y == 0)
        def _():
            self.outcome(k, chunk["result"], 1, 6).wait_recv()
            self.twin(k, chunk["result"]).start()

        @pl.when(y == 3)
        def _():
            self.outcome(k, chunk["result"], 2, 6).wait_recv()
            self.twin(k, chunk["result"]).start()

    def finish(self, k):
        chunk, y = self.chunks[k], self.side(k)
        c = lax.axis_index("dp")
        self.pair(k).wait_send()
        remote(
            chunk["result_other"], chunk["result_other"], self.sem(k, 8), self.sem(k, 9), {"dp": 1 - c}
        ).wait_recv()
        self.twin(k, chunk["result"]).wait_send()

        @pl.when(y == 0)
        def _():
            self.partial(k, 0, 1).wait_send()

        @pl.when(y == 3)
        def _():
            self.partial(k, 0, 2).wait_send()

        @pl.when(y == 2)
        def _():
            self.partial(k, 1, 1).wait_send()
            self.outcome(k, chunk["result"], 3, 6).wait_send()

        @pl.when(y == 1)
        def _():
            self.outcome(k, chunk["mine"], 2, 6).wait_send()
            self.outcome(k, chunk["mine"], 0, 7).wait_send()
            self.kept(k).wait()

    def tick(self):
        if self.clock >= self.ready and self.ready < self.total:
            return
        stages = (self.leaf, self.onward, self.root, self.middle, self.combine)
        for k, act in enumerate(stages):
            chunk = self.clock - self.LATE * (len(stages) - 1 - k)
            if 0 <= chunk < self.total:
                act(chunk)
        self.clock += 1

    def drain(self):
        while self.clock < self.total + 4 * self.LATE:
            self.tick()


CHUNK = 32
ROW_TILE = 16


def row_sums(total, value):
    return total + jnp.sum(value, axis=-1, keepdims=True)


def layer_kernel(
    dims,
    tok_in, mix_in, gains_in, wfull_in, up_in, bias_in, down_in, down_bias_in, grad_in,
    proj_in, den_in, prior_in, wout_in, wqkv_in,
    out_out, tok_grad_out, qkv_out, out_w_out, up_out, down_out, small_out,
    gains, bias, down_bias, grad, resid_grad, part_ffn, part, buf_norm, buf_tok, xhat_own, inv_own,
    d_down, d_up, d_small, got_ffn, got_out, got_qkv, got_small, state, state_in, ring, ring_q,
    grad_sem, norm_sem, back_sem, ffn_sem, tok_sem, state_sem, chunk_sem, load_sem, stage_sem, image_sem, store_sem,
):
    images, length, used, rows = dims
    width = grad.shape[2]
    hidden = up_in.shape[1]
    z, h, c, near_x, near_y, far = place()
    seq = lax.axis_size("seq")
    vmem = pltpu.VMEM
    tiles = width // LANES
    row_ok = lax.broadcasted_iota(jnp.int32, (rows, LANES), 0) < length

    small = (
        pltpu.make_async_copy(gains_in, gains, load_sem.at[0]),
        pltpu.make_async_copy(bias_in, bias, load_sem.at[1]),
        pltpu.make_async_copy(down_bias_in, down_bias, load_sem.at[2]),
    )

    grads = Gather(lambda i: grad.at[i, :, lanes(h)], grad, used, grad_sem)
    norm = Scatter(lambda i: part.at[i % 2], buf_norm, rows, norm_sem)
    back = Gather(lambda i: resid_grad.at[i, :, lanes(h)], resid_grad, used, back_sem)
    ffn = Scatter(lambda i: part_ffn.at[i], buf_norm, used, ffn_sem)
    toks = Scatter(lambda i: part.at[i % 2], buf_tok, rows, tok_sem)
    reduce = Reduce(chunk_sem, chunk_sem.shape[0])
    tick = reduce.tick
    stores = []

    def store(src, dst):
        copy = pltpu.make_async_copy(src, dst, store_sem.at[len(stores)])
        copy.start()
        stores.append(copy)

    def halves(source, high, low):
        split_rows(source, high, low, rows, ROW_TILE)

    def stats(i, weight, sums_with):
        first, second = [], []
        for s in row_blocks(rows):
            term = part[i % 2, s, :]
            first.append(jnp.sum(term * gains[weight, :], axis=-1, keepdims=True))
            second.append(jnp.sum(term * sums_with(s), axis=-1, keepdims=True))
        block = to_lanes(jnp.concatenate(first, axis=0), jnp.concatenate(second, axis=0), rows)
        for k in range(tiles):
            part[i % 2, rows - 8 : rows, lanes(k)] = block

    def norm_share(scatter, i, weight, hat, inv):
        both = scatter.total(i)
        mean, cross = to_columns(both[rows - 8 : rows], rows)
        own = jnp.where(row_ok, both, 0.0)
        scaled = own * gains[weight, lanes(h)]
        share = (scaled - mean * (1.0 / width) - hat * (cross * (1.0 / width))) * inv
        return share, own

    def resid_back(i):
        share, own = norm_share(norm, i, slice(1, 2), xhat_own[i], inv_own[i, :, 0:1])
        resid_grad[i, :, lanes(h)] = jnp.where(row_ok, grad[i, :, lanes(h)] + share, 0.0)
        for k, value in ((1, own * xhat_own[i]), (2, grad[i, :, lanes(h)])):
            d_small[8:9, lanes(k)] = d_small[8:9, lanes(k)] + jnp.sum(value, axis=0, keepdims=True)
        norm.finish(i)
        back.direct(i)

    def load_phase(raw):
        copies = [pltpu.make_async_copy(grad_in.at[i], raw.at[i], load_sem.at[3 + i]) for i in range(images)]
        for copy in copies + list(small):
            copy.start()
        blank = jnp.zeros((rows - used, LANES), F32)
        for i in range(images):
            for other in (near_x, near_y, far):
                grad[i, used:rows, lanes(other)] = blank
                resid_grad[i, used:rows, lanes(other)] = blank
        d_small[...] = jnp.zeros_like(d_small)
        for i in range(images):
            copies[i].wait()
            pad_rows(raw, grad, i, h)

    def ffn_phase(
        wo_h, wo_l, up_h, up_l, dn_h, dn_l, pair_h, pair_l, n_h, n_l, hid_h, hid_l, slope, ug_h, ug_l
    ):
        def weight_copy(k):
            source, stage, _, _ = weights[k]
            return pltpu.make_async_copy(source, stage, stage_sem.at[k])

        def take(k):
            _, stage, high, low = weights[k]
            weight_copy(k).wait()
            split_rows(stage, high, low, stage.shape[0], 64)

        weights = (
            (wfull_in, d_down, wo_h, wo_l),
            (up_in, d_up, up_h, up_l),
            (down_in, d_up, dn_h, dn_l),
        )

        def turned(source, target):
            def one(k, _):
                s = lanes(k)
                target[:, s] = source[s, :].T
                return 0

            lax.fori_loop(0, tiles, one, 0)

        def tok_copy(i):
            return pltpu.make_async_copy(tok_in.at[i], part.at[0], image_sem.at[0])

        def mix_copy(i):
            return pltpu.make_async_copy(mix_in.at[i], part.at[1], image_sem.at[1])

        def forward(i):
            mix_copy(i).wait()
            halves(part.at[1], pair_h, pair_l)
            if i + 1 < images:
                mix_copy(i + 1).start()
            if i == 0:
                take(0)
            tok_copy(i).wait()
            part[0] = part[0] + dot3((pair_h[...], pair_l[...]), (wo_h[...], wo_l[...]), "nn")
            part_ffn[i, :, lanes(h)] = part[0, :, lanes(h)]
            grads.forward(i)
            if i + 2 < images:
                grads.direct(i + 2)

            for s in row_blocks(rows):
                hat, inv = norm_parts(part[0, s, :])
                part[0, s, :] = hat
                inv_own[i, s, :] = jnp.broadcast_to(inv, (ROW_TILE, 128))
                n_h[i, s, :], n_l[i, s, :] = split(hat * gains[1:2, :])
            xhat_own[i] = part[0, :, lanes(h)]
            if i + 1 < images:
                tok_copy(i + 1).start()
            if i == 0:
                take(1)
                weight_copy(2).start()
            slope[i] = dot3((n_h[i], n_l[i]), (up_h[...], up_l[...]), "nn") + bias[0:1, :]
            for s in row_blocks(rows):
                act, by = activation(slope[i, s, :])
                hid_h[i, s, :], hid_l[i, s, :] = split(act)
                slope[i, s, :] = by
            grads.ready(i)
            halves(grad.at[i], pair_h, pair_l)

            term = dot3((hid_h[i], hid_l[i]), (pair_h[...], pair_l[...]), "tn")
            d_down[...] = term if i == 0 else d_down[...] + term

        def hidden_back(i):
            halves(grad.at[i], pair_h, pair_l)

            part[i % 2] = dot3((pair_h[...], pair_l[...]), (up_h[...], up_l[...]), "nn")
            total = jnp.zeros((1, hidden), F32)
            for s in row_blocks(rows):
                ug = part[i % 2, s, :] * slope[i, s, :]
                ug_h[s, :], ug_l[s, :] = split(ug)
                total = total + jnp.sum(ug, axis=0, keepdims=True)
            d_small[0:1, :] = d_small[0:1, :] + total

        def up_grad(i):
            term = dot3((n_h[i], n_l[i]), (ug_h[...], ug_l[...]), "tn")
            d_up[...] = term if i == 0 else d_up[...] + term

        def norm_back(i):
            part[i % 2] = dot3((ug_h[...], ug_l[...]), (wo_h[...], wo_l[...]), "nn")
            stats(i, slice(1, 2), lambda s: n_h[i, s, :].astype(F32) + n_l[i, s, :].astype(F32))
            norm.direct(i)

        def down(i):
            resid = part_ffn[i, :, lanes(h)]

            part_ffn[i] = dot3((hid_h[i], hid_l[i]), (dn_h[...], dn_l[...]), "nn")
            part_ffn[i, :, lanes(h)] = part_ffn[i, :, lanes(h)] + resid

        weight_copy(0).start()
        mix_copy(0).start()
        tok_copy(0).start()
        weight_copy(1).start()
        for copy in small:
            copy.wait()
        for i in range(images):
            forward(i)
            if i == 0:
                take(2)
        reduce.exchange(0, down_chunks)
        turned(up_h, wo_h)
        turned(up_l, wo_l)
        turned(dn_h, up_h)
        turned(dn_l, up_l)
        for i in range(images):
            hidden_back(i)
            tick()
            up_grad(i)
            if i == images - 1:
                reduce.exchange(down_chunks, up_chunks)
            tick()
            if i >= 1:
                norm.relay(i - 1)
            norm_back(i)
            tick()
            if i >= 1:
                resid_back(i - 1)
            if i >= 2:
                back.forward(i - 2)
        last = images - 1
        down(0)
        norm.relay(last)
        back.forward(last - 1)
        tick()
        down(1)
        tick()
        resid_back(last)
        down(2)
        tick()
        down(3)
        tick()
        back.forward(last)

    def attend_phase(
        wo_h, wo_l, wq_h, wq_l, tok, proj, den, prior, mixed, rg_h, rg_l, n_h, n_l, xhat, pg_h, pg_l,
        dnum, dden, later, hat_own, root_own, d_out, d_qkv, out_trim, tok_trim,
    ):
        def image_copies(i):
            return (
                pltpu.make_async_copy(mix_in.at[i, :, lanes(h)], mixed.at[i], load_sem.at[8 + 4 * i]),
                pltpu.make_async_copy(den_in.at[i], den.at[i], load_sem.at[9 + 4 * i]),
                pltpu.make_async_copy(proj_in.at[i], proj.at[i], load_sem.at[10 + 4 * i]),
                pltpu.make_async_copy(prior_in.at[i], prior.at[i], load_sem.at[11 + 4 * i]),
            )

        def tok_copy(i):
            return pltpu.make_async_copy(tok_in.at[i], tok.at[i % 2], image_sem.at[i % 2])

        weights = [pltpu.make_async_copy(wout_in, d_out, load_sem.at[0])]
        weights += [
            pltpu.make_async_copy(wqkv_in.at[pl.ds(j * width, width)], d_qkv.at[:, lanes(j)], load_sem.at[1 + j])
            for j in range(3)
        ]
        for copy in weights:
            copy.start()
        for i in range(images):
            for copy in image_copies(i):
                copy.start()
        tok_copy(0).start()
        tok_copy(1).start()
        out_chunks = reduce.add(d_out, got_out, out_w_out, CHUNK, ring)
        qkv_chunks = reduce.add_columns(d_qkv, got_qkv, qkv_out, ring_q.shape[2], ring_q)
        all_chunks = reduce.add(d_small, got_small, small_out, 8, ring)

        def state_copy(i, d, step):
            return remote(
                state.at[i], state_in.at[d - 1, i], state_sem.at[0, d - 1, i], state_sem.at[1, d - 1, i],
                {"seq": lax.rem(z + step + seq, seq)},
            )

        def first_half(i):
            back.ready(i)
            for copy in image_copies(i):
                copy.wait()
            halves(resid_grad.at[i], rg_h, rg_l)
            dm = dot3((rg_h[...], rg_l[...]), (wo_h[...], wo_l[...]), "nn")
            ones = jnp.where(diagonal_mask(), 1.0, 0.0).astype(BF)
            inverse = 1.0 / den[i]
            dnum[i] = dm * inverse
            dden[i] = -dot2(split(dm * mixed[i]), ones, "nn") * inverse
            query_feat = positive(proj[i, :, lanes(0)])
            state[i, 0:HEAD_DIM, :] = fold(dot3(split(query_feat), split(dnum[i]), "tn"))
            state[i, HEAD_DIM:, :] = jnp.broadcast_to(
                jnp.sum(query_feat * dden[i], axis=0, keepdims=True), (STATE - HEAD_DIM, LANES)
            )
            for d in range(1, seq):

                @pl.when(z >= d)
                def _():
                    state_copy(i, d, -d).start()

            term = dot3(split(mixed[i]), (rg_h[...], rg_l[...]), "tn")
            d_out[...] = term if i == 0 else d_out[...] + term

        def second_half(i):
            later[...] = jnp.zeros_like(later)
            for d in range(1, seq):

                @pl.when(z + d < seq)
                def _():
                    state_copy(i, d, d).wait_recv()
                    later[...] = later[...] + state_in[d - 1, i]

            query, key, value = (proj[i, :, lanes(k)] for k in range(3))
            query_feat = positive(query)
            key_feat = jnp.where(row_ok, positive(key), 0.0)
            query_pair, key_pair, value_pair = split(query_feat), split(key_feat), split(value)
            dden_i = dden[i]
            dnum_pair = split(dnum[i])
            prior_pair = split(unfold(prior[i, 0:HEAD_DIM, :]))
            later_pair = split(unfold(later[0:HEAD_DIM, :]))
            fq = dot3(dnum_pair, prior_pair, "nt") + dden_i * prior[i, HEAD_DIM : HEAD_DIM + 1, :]
            fk = dot3(value_pair, later_pair, "nt") + later[HEAD_DIM : HEAD_DIM + 1, :]
            fv = dot3(key_pair, later_pair, "nn")
            row = lax.broadcasted_iota(jnp.int32, (rows, rows), 0)
            col = lax.broadcasted_iota(jnp.int32, (rows, rows), 1)
            causal = col <= row
            for k, mask in enumerate(head_masks(rows)):
                key_h, query_h = pick(mask, key_pair), pick(mask, query_pair)
                scores = split(jnp.where(causal, dot3(query_pair, key_h, "nt"), 0.0))
                pull = dot3(dnum_pair, pick(mask, value_pair), "nt")
                pull = pull + dden_i[:, k * HEAD_DIM : k * HEAD_DIM + 1]
                pull = split(jnp.where(causal, pull, 0.0))
                fq = fq + dot3(pull, key_h, "nn")
                fk = fk + dot3(pull, query_h, "tn")
                fv = fv + dot3(scores, pick(mask, dnum_pair), "tn")
            slope = lambda v: jnp.where(v > 0, 1.0, jnp.exp(jnp.minimum(v, 0.0)))
            pg_h[:, lanes(0)], pg_l[:, lanes(0)] = split(fq * slope(query))
            pg_h[:, lanes(1)], pg_l[:, lanes(1)] = split(jnp.where(row_ok, fk * slope(key), 0.0))
            pg_h[:, lanes(2)], pg_l[:, lanes(2)] = split(fv)

        def weight_grads(i):
            tok_copy(i).wait()

            for s in row_blocks(rows):
                hat, inv = norm_parts(tok[i % 2, s, :])
                xhat[s, :] = hat
                root_own[i, s, :] = jnp.broadcast_to(inv, (ROW_TILE, 128))
                n_h[s, :], n_l[s, :] = split(hat * gains[0:1, :])
            hat_own[i] = xhat[:, lanes(h)]
            if i + 2 < images:
                tok_copy(i + 2).start()

            term = dot3((n_h[...], n_l[...]), (pg_h[...], pg_l[...]), "tn")
            d_qkv[...] = term if i == 0 else d_qkv[...] + term

        def norm_back(i):
            if i >= 2:
                toks.finish(i - 2)

            part[i % 2] = dot3((pg_h[...], pg_l[...]), (wq_h[...], wq_l[...]), "nn")
            stats(i, slice(0, 1), lambda s: xhat[s, :] * gains[0:1, :])
            toks.direct(i)

        def token_back(i):
            share, own = norm_share(toks, i, slice(0, 1), hat_own[i], root_own[i, :, 0:1])
            d_small[8:9, lanes(0)] = d_small[8:9, lanes(0)] + jnp.sum(own * hat_own[i], axis=0, keepdims=True)
            tok_trim[i] = (resid_grad[i, :, lanes(h)] + share)[0:length]
            store(tok_trim.at[i], tok_grad_out.at[i])

        def output(i):
            out_trim[i] = (ffn.total(i) + down_bias[0:1, :])[0:length]
            store(out_trim.at[i], out_out.at[i])

        for copy in weights:
            copy.wait()
        for k in range(tiles):
            wo_h[lanes(k), :], wo_l[lanes(k), :] = split(d_out[:, lanes(k)].T)

        def turn(k, _):
            for j in range(3):
                wq_h[lanes(j), lanes(k)], wq_l[lanes(j), lanes(k)] = split(d_qkv[lanes(k), lanes(j)].T)
            return 0

        lax.fori_loop(0, tiles, turn, 0)
        for i in range(images):
            first_half(i)
            tick()
        reduce.exchange(up_chunks, out_chunks)
        ffn.direct(0)
        ffn.direct(1)
        last = images - 1
        for i in range(images):
            second_half(i)
            tick()
            if i >= 1:
                toks.relay(i - 1)
            weight_grads(i)
            if i == last:
                reduce.exchange(out_chunks, qkv_chunks)
            if i < 2:
                ffn.relay(i)
                ffn.direct(i + 2)
            else:
                ffn.relay(i)
            tick()
            norm_back(i)
            if i >= 1:
                token_back(i - 1)
            if i >= 1:
                output(i - 1)
            tick()
        toks.relay(last)
        tick()
        output(last)
        tick()
        token_back(last)
        reduce.exchange(qkv_chunks, all_chunks)
        reduce.drain()
        for i in range(images):
            grads.finish(i)
            back.finish(i)
            ffn.finish(i)
            if i >= images - 2:
                toks.finish(i)
            for d in range(1, seq):

                @pl.when(z >= d)
                def _(i=i, d=d):
                    state_copy(i, d, -d).wait_send()

        for k in range(all_chunks):
            reduce.finish(k)
        for copy in stores:
            copy.wait()

    pl.run_scoped(load_phase, vmem((images, length, LANES), F32))
    enter(
        [{"head": near_x}, {"head": near_y}, {"dp": 1 - c}]
        + [{"seq": lax.rem(z + d, seq)} for d in range(1, seq)]
    )
    grads.direct(0)
    grads.direct(1)
    down_chunks = reduce.add(d_down, got_ffn.at[0], down_out, CHUNK, ring)
    up_chunks = reduce.add(d_up, got_ffn.at[1], up_out, CHUNK, ring)
    pair = lambda *s: [vmem(s, BF), vmem(s, BF)]
    pl.run_scoped(
        ffn_phase,
        *pair(width, width), *pair(width, hidden), *pair(hidden, width),
        *pair(rows, width), *pair(images, rows, width), *pair(images, rows, hidden),
        vmem((images, rows, hidden), F32), *pair(rows, hidden),
    )
    pl.run_scoped(
        attend_phase,
        *pair(width, LANES), *pair(3 * LANES, width), vmem((2, rows, width), F32),
        vmem((images, rows, 3 * LANES), F32), vmem((images, rows, LANES), F32), vmem((images, STATE, LANES), F32),
        vmem((images, rows, LANES), F32), *pair(rows, width), *pair(rows, width), vmem((rows, width), F32),
        *pair(rows, 3 * LANES), vmem((images, rows, LANES), F32), vmem((images, rows, LANES), F32),
        vmem((STATE, LANES), F32), vmem((images, rows, LANES), F32), vmem((images, rows, 128), F32),
        vmem((LANES, width), F32), vmem((width, 3 * LANES), F32),
        vmem((images, length, LANES), F32), vmem((images, length, LANES), F32),
    )


def layer_call(tok, mix, gains, wfull, up_weight, up_bias, down_weight, down_bias, grads, proj, den, prior, wout, wqkv):
    images, length, _ = grads.shape
    rows, width = tok.shape[1:]
    hidden = up_weight.shape[1]
    used = round_up(length, 8)
    seq = lax.axis_size("seq")
    any_spec = pl.BlockSpec(memory_space=pl.ANY)
    shape = lambda *s: jax.ShapeDtypeStruct(s, F32)
    vmem, dma = pltpu.VMEM, pltpu.SemaphoreType.DMA
    half = round_up(rows // 2, 8)
    chunk_q = 128
    chunks = 2 * (hidden // 2 // CHUNK) + LANES // 2 // CHUNK + 3 * width // 2 // chunk_q + 1
    return pl.pallas_call(
        functools.partial(layer_kernel, (images, length, used, rows)),
        out_shape=(
            shape(images, length, LANES),
            shape(images, length, LANES),
            shape(3 * width, LANES),
            shape(LANES, width),
            shape(width, hidden),
            shape(hidden, width),
            shape(16, width),
        ),
        in_specs=[any_spec] * 14,
        out_specs=(any_spec,) * 7,
        scratch_shapes=[
            vmem((8, width), F32), vmem((8, hidden), F32), vmem((8, LANES), F32),
            vmem((images, rows, width), F32), vmem((images, rows, width), F32), vmem((images, rows, width), F32),
            vmem((2, rows, width), F32), vmem((images, 6, half, LANES), F32), vmem((images, 6, half, LANES), F32),
            vmem((images, rows, LANES), F32), vmem((images, rows, 128), F32),
            vmem((hidden, width), F32), vmem((width, hidden), F32), vmem((16, width), F32),
            vmem((2, hidden // 2, width), F32), vmem((LANES // 2, width), F32), vmem((3 * width // 2, LANES), F32),
            vmem((8, width), F32), vmem((images, STATE, LANES), F32), vmem((seq - 1, images, STATE, LANES), F32),
            vmem((Reduce.RING, 2, CHUNK, width), F32), vmem((Reduce.RING, 2, chunk_q, LANES), F32),
            dma((images, Gather.SEMS)), dma((images, Scatter.SEMS)), dma((images, Gather.SEMS)),
            dma((images, Scatter.SEMS)), dma((images, Scatter.SEMS)), dma((2, seq - 1, images)),
            dma((chunks, Reduce.SEMS)), dma((8 + 4 * images,)), dma((3,)), dma((2,)), dma((2 * images,)),
        ],
        compiler_params=pltpu.CompilerParams(
            collective_id=1, has_side_effects=True, vmem_limit_bytes=64 * 1024 * 1024
        ),
    )(tok, mix, gains, wfull, up_weight, up_bias, down_weight, down_bias, grads, proj, den, prior, wout, wqkv)


def fast_device(
    tokens,
    gain_attn,
    qkv_weight,
    out_weight,
    gain_ffn,
    up_weight,
    up_bias,
    down_weight,
    down_bias,
    out_grad,
):
    model_width, kinds, local_width = qkv_weight.shape

    def wide(*vectors):
        blank = jnp.zeros((8 - len(vectors), vectors[0].shape[0]), jnp.float32)
        return jnp.concatenate([v[None] for v in vectors] + [blank])

    proj_weight = jnp.transpose(qkv_weight, (1, 0, 2)).reshape(kinds * model_width, local_width)
    tok, gains, proj, den, prior, mix, wfull = attend_call(
        tokens, wide(gain_attn, gain_ffn), proj_weight, out_weight
    )
    output, tok_grad, d_qkv, d_out, d_up, d_down, small = layer_call(
        tok, mix, gains, wfull.reshape(model_width, model_width), up_weight, wide(up_bias), down_weight,
        wide(down_bias), out_grad, proj, den, prior, out_weight, proj_weight,
    )
    return (
        output,
        tok_grad,
        small[8, 0:LANES],
        jnp.transpose(d_qkv.reshape(kinds, model_width, local_width), (1, 0, 2)),
        d_out,
        small[8, LANES : 2 * LANES],
        d_up,
        small[0],
        d_down,
        small[8, 2 * LANES : 3 * LANES],
    )


def device_function(mesh):
    if (mesh.shape["seq"], mesh.shape["head"], mesh.shape["dp"]) == (4, 4, 2):
        return fast_device
    return per_device


def solution(mesh):
    return jax.shard_map(
        device_function(mesh),
        mesh=mesh,
        in_specs=(
            P("dp", "seq", "head"),
            P("head"),
            P(None, None, "head"),
            P("head", None),
            P("head"),
            P(None, "head"),
            P("head"),
            P("head", None),
            P("head"),
            P("dp", "seq", "head"),
        ),
        out_specs=(
            P("dp", "seq", "head"),
            P("dp", "seq", "head"),
            P("head"),
            P(None, None, "head"),
            P("head", None),
            P("head"),
            P(None, "head"),
            P("head"),
            P("head", None),
            P("head"),
        ),
        check_vma=False,
    )
```

```python
import functools

import jax
import jax.numpy as jnp
from jax import lax
from jax.experimental import pallas as pl
from jax.experimental.pallas import tpu as pltpu
from jax.sharding import PartitionSpec as P

HEAD_DIM = 64


highest = lax.Precision.HIGH
norm_eps = 1e-05


def entering(part, axis, combine, identity, reverse):
    count = lax.axis_size(axis)
    place = lax.axis_index(axis)
    ahead = count - 1 - place if reverse else place
    gathered = jax.tree.map(lambda a: lax.all_gather(a, axis), part)
    state = jax.tree.map(lambda a, e: jnp.zeros_like(a) + jnp.asarray(e, a.dtype), part, identity)

    def one(turn, state):
        source = count - 1 - turn if reverse else turn
        return combine(
            state, jax.tree.map(lambda a: lax.dynamic_index_in_dim(a, source, 0, False), gathered)
        )

    return lax.fori_loop(0, ahead, one, state)


def feature(values_in):
    return jax.nn.elu(values_in) + 1.0


def layer_norm(values_in, gain):
    row_mean = jnp.mean(values_in, axis=-1, keepdims=True)
    centred = values_in - row_mean
    row_var = jnp.mean(centred * centred, axis=-1, keepdims=True)
    return centred * lax.rsqrt(row_var + norm_eps) * gain


def norm_back(partial_grad, rows_full, gain_full, gain_share):
    local_width = gain_share.shape[0]
    model_width = gain_full.shape[0]
    row_mean = jnp.mean(rows_full, axis=-1, keepdims=True)
    centred = rows_full - row_mean
    row_inv = lax.rsqrt(jnp.mean(centred * centred, axis=-1, keepdims=True) + norm_eps)
    scaled = partial_grad * gain_full
    sums = lax.psum(
        jnp.stack(
            [jnp.sum(scaled, axis=-1), jnp.sum(scaled * (centred * row_inv), axis=-1)]
        ),
        "head",
    )
    means = (sums / model_width)[:, :, None]
    share = lax.psum_scatter(partial_grad, "head", scatter_dimension=1, tiled=True)
    start = lax.axis_index("head") * local_width
    xhat = lax.dynamic_slice_in_dim(centred, start, local_width, 1) * row_inv
    back = (share * gain_share - means[0] - xhat * means[1]) * row_inv
    return back, jnp.sum(share * xhat, axis=0)


def mlp_act(values_in):
    return jax.nn.gelu(values_in, approximate=True)


def block_attend(query_proj, key_proj, value_proj, prior_state, prior_total):
    query_feat = feature(query_proj)
    key_feat = feature(key_proj)
    length_now = query_proj.shape[1]
    scores = jnp.einsum("gihe,gjhe->ghij", query_feat, key_feat, precision=highest)
    row_index = lax.broadcasted_iota(jnp.int32, (length_now, length_now), 0)
    col_index = lax.broadcasted_iota(jnp.int32, (length_now, length_now), 1)
    scores = jnp.where(col_index <= row_index, scores, jnp.float32(0.0))
    numerator = jnp.einsum("ghij,gjhe->gihe", scores, value_proj, precision=highest)
    numerator = numerator + jnp.einsum(
        "gihe,ghef->gihf", query_feat, prior_state, precision=highest
    )
    denominator = jnp.sum(scores, axis=-1) + jnp.einsum(
        "gihe,ghe->ghi", query_feat, prior_total, precision=highest
    )
    return numerator / jnp.transpose(denominator, (0, 2, 1))[..., None]


def block_state(key_proj, value_proj):
    key_feat = feature(key_proj)
    kv_sum = jnp.einsum("gihe,gihf->ghef", key_feat, value_proj, precision=highest)
    return (kv_sum, jnp.sum(key_feat, axis=1))


def add_pair(earlier, later):
    return (earlier[0] + later[0], earlier[1] + later[1])


def per_device(
    tokens,
    gain_attn,
    qkv_weight,
    out_weight,
    gain_ffn,
    up_weight,
    up_bias,
    down_weight,
    down_bias,
    out_grad,
):
    image_count, block_len, local_width = tokens.shape
    row_count = image_count * block_len
    model_width = qkv_weight.shape[0]
    heads_local = local_width // HEAD_DIM
    column_start = lax.axis_index("head") * local_width
    full_tokens, gain_first, gain_second = (
        lax.all_gather(tokens, "head", axis=2, tiled=True),
        lax.all_gather(gain_attn, "head", axis=0, tiled=True),
        lax.all_gather(gain_ffn, "head", axis=0, tiled=True),
    )
    token_rows = full_tokens.reshape(row_count, model_width)
    normed_one = layer_norm(token_rows, gain_first)
    proj_weight = qkv_weight.reshape(model_width, 3 * local_width)
    projected = jnp.dot(normed_one, proj_weight, precision=highest)
    parts_view = projected.reshape(image_count, block_len, 3, heads_local, HEAD_DIM)
    query_proj = parts_view[:, :, 0]
    key_proj = parts_view[:, :, 1]
    value_proj = parts_view[:, :, 2]
    (own_state, own_total), pull_state = jax.vjp(block_state, key_proj, value_proj)
    zero_pair = (jnp.zeros_like(own_state), jnp.zeros_like(own_total))
    prior_state, prior_total = entering((own_state, own_total), "seq", add_pair, zero_pair, False)
    mixed, pull_attend = jax.vjp(
        block_attend, query_proj, key_proj, value_proj, prior_state, prior_total
    )
    mixed_rows = mixed.reshape(row_count, local_width)
    branch_out = jnp.dot(mixed_rows, out_weight, precision=highest)
    token_share = tokens.reshape(row_count, local_width)
    resid_share = token_share + lax.psum_scatter(
        branch_out, "head", scatter_dimension=1, tiled=True
    )
    resid_full = lax.all_gather(resid_share, "head", axis=1, tiled=True)
    normed_two = layer_norm(resid_full, gain_second)
    up_proj = jnp.dot(normed_two, up_weight, precision=highest) + up_bias
    hidden, pull_act = jax.vjp(mlp_act, up_proj)
    down_proj = jnp.dot(hidden, down_weight, precision=highest)
    ffn_share = lax.psum_scatter(down_proj, "head", scatter_dimension=1, tiled=True)
    output = (resid_share + ffn_share + down_bias).reshape(tokens.shape)
    grad_share = out_grad.reshape(row_count, local_width)
    grad_full = lax.all_gather(grad_share, "head", axis=1, tiled=True)
    down_bias_grad = jnp.sum(grad_share, axis=0)
    down_weight_grad = jnp.dot(hidden.T, grad_full, precision=highest)
    hidden_grad = jnp.dot(grad_full, down_weight.T, precision=highest)
    (up_grad,) = pull_act(hidden_grad)
    up_bias_grad = jnp.sum(up_grad, axis=0)
    up_weight_grad = jnp.dot(normed_two.T, up_grad, precision=highest)
    ffn_grads = lax.psum((up_weight_grad, down_weight_grad), ("seq", "dp"))
    resid_back, gain_ffn_share = norm_back(
        jnp.dot(up_grad, up_weight.T, precision=highest), resid_full, gain_second, gain_ffn
    )
    resid_grad_share = grad_share + resid_back
    resid_grad = lax.all_gather(resid_grad_share, "head", axis=1, tiled=True)
    out_weight_grad = jnp.dot(mixed_rows.T, resid_grad, precision=highest)
    mixed_grad = jnp.dot(resid_grad, out_weight.T, precision=highest).reshape(mixed.shape)
    query_grad, key_grad, value_grad, state_grad, total_grad = pull_attend(mixed_grad)
    later_state, later_total = entering((state_grad, total_grad), "seq", add_pair, zero_pair, True)
    key_extra, value_extra = pull_state((later_state, later_total))
    key_grad = key_grad + key_extra
    value_grad = value_grad + value_extra
    proj_grad = jnp.stack([query_grad, key_grad, value_grad], axis=2).reshape(
        row_count, 3 * local_width
    )
    qkv_weight_grad = jnp.dot(normed_one.T, proj_grad, precision=highest).reshape(qkv_weight.shape)
    token_back, gain_attn_share = norm_back(
        jnp.dot(proj_grad, proj_weight.T, precision=highest), token_rows, gain_first, gain_attn
    )
    tokens_grad = (resid_grad_share + token_back).reshape(tokens.shape)
    summed_grads = lax.psum(
        (
            gain_attn_share,
            qkv_weight_grad,
            out_weight_grad,
            gain_ffn_share,
            up_bias_grad,
            down_bias_grad,
        ),
        ("seq", "dp"),
    )
    return (
        output,
        tokens_grad,
        summed_grads[0],
        summed_grads[1],
        summed_grads[2],
        summed_grads[3],
        ffn_grads[0],
        summed_grads[4],
        ffn_grads[1],
        summed_grads[5],
    )


MESH = pl.DeviceIdType.MESH
BF = jnp.bfloat16
F32 = jnp.float32
LANES = 256
DIMS = {
    "nn": (((1,), (0,)), ((), ())),
    "nt": (((1,), (1,)), ((), ())),
    "tn": (((0,), (0,)), ((), ())),
}


def round_up(value, step):
    return -(-value // step) * step


def padded(length):
    return round_up(round_up(length, 8) + 8, 16)


def row_blocks(rows):
    return [slice(r, r + 16) for r in range(0, rows, 16)]


def pad_rows(raw, slots, i, h):
    length, rows = raw.shape[1], slots.shape[1]
    slots[i, 0:length, lanes(h)] = raw[i]
    slots[i, length:rows, lanes(h)] = jnp.zeros((rows - length, LANES), F32)


def dot(left, right, kind):
    return lax.dot_general(left, right, DIMS[kind], preferred_element_type=F32)


def split(values):
    high = values.astype(BF)
    return high, (values - high.astype(F32)).astype(BF)


def dot3(left, right, kind):
    return (
        dot(left[0], right[0], kind) + dot(left[0], right[1], kind) + dot(left[1], right[0], kind)
    )


def dot2(left, right, kind):
    return dot(left[0], right, kind) + dot(left[1], right, kind)


def lanes(index):
    if isinstance(index, int):
        return pl.ds(index * LANES, LANES)
    return pl.ds(pl.multiple_of(index * LANES, LANES), LANES)


def place():
    z, h, c = lax.axis_index("seq"), lax.axis_index("head"), lax.axis_index("dp")
    near_x = h + 1 - 2 * lax.rem(h, 2)
    near_y = lax.rem(h + 2, 4)
    return z, h, c, near_x, near_y, 3 - h


def remote(src, dst, send, recv, device):
    return pltpu.make_async_remote_copy(
        src_ref=src, dst_ref=dst, send_sem=send, recv_sem=recv, device_id=device, device_id_type=MESH
    )


def enter(targets):
    barrier = pltpu.get_barrier_semaphore()
    for device in targets:
        pl.semaphore_signal(barrier, inc=1, device_id=device, device_id_type=MESH)
    pl.semaphore_wait(barrier, len(targets))


class Gather:
    SEMS = 8

    def __init__(self, own, slots, rows, sems):
        self.own, self.slots, self.sems = own, slots, sems
        self.half = round_up(rows // 2, 8)
        self.rows = rows

    def copies(self, i):
        _, h, _, near_x, near_y, _ = place()
        slots, sems = self.slots, self.sems
        first, second = pl.ds(0, self.half), pl.ds(self.half, self.rows - self.half)
        every = pl.ds(0, self.rows)

        def one(src, dst, place_in, device):
            return remote(src, dst, sems.at[i, place_in], sems.at[i, 4 + place_in], {"head": device})

        own = self.own(i)
        return (
            one(own.at[every], slots.at[i, every, lanes(h)], 0, near_x),
            one(own.at[every], slots.at[i, every, lanes(h)], 1, near_y),
            one(slots.at[i, first, lanes(near_x)], slots.at[i, first, lanes(near_x)], 2, near_y),
            one(slots.at[i, second, lanes(near_y)], slots.at[i, second, lanes(near_y)], 3, near_x),
        )

    def arrivals(self, i):
        _, h, _, near_x, near_y, far = place()
        slots, sems = self.slots, self.sems
        first, second = pl.ds(0, self.half), pl.ds(self.half, self.rows - self.half)
        every = pl.ds(0, self.rows)

        def one(dst, place_in, device):
            return remote(dst, dst, sems.at[i, place_in], sems.at[i, 4 + place_in], {"head": device})

        return (
            one(slots.at[i, every, lanes(near_x)], 0, near_x),
            one(slots.at[i, every, lanes(near_y)], 1, near_y),
            one(slots.at[i, first, lanes(far)], 2, near_y),
            one(slots.at[i, second, lanes(far)], 3, near_x),
        )

    def direct(self, i):
        x, y, _, _ = self.copies(i)
        x.start()
        y.start()

    def forward(self, i):
        x, y, _, _ = self.arrivals(i)
        x.wait_recv()
        y.wait_recv()
        _, _, to_y, to_x = self.copies(i)
        to_y.start()
        to_x.start()

    def ready(self, i):
        _, _, x, y = self.arrivals(i)
        x.wait_recv()
        y.wait_recv()

    def finish(self, i):
        for copy in self.copies(i):
            copy.wait_send()


def head_masks(rows):
    head = lax.broadcasted_iota(jnp.int32, (rows, LANES), 1) // HEAD_DIM
    return [head == k for k in range(LANES // HEAD_DIM)]


def diagonal_mask():
    rows = lax.broadcasted_iota(jnp.int32, (LANES, LANES), 0) // HEAD_DIM
    cols = lax.broadcasted_iota(jnp.int32, (LANES, LANES), 1) // HEAD_DIM
    return rows == cols


def pick(mask, pair):
    zero = jnp.zeros((), BF)
    return jnp.where(mask, pair[0], zero), jnp.where(mask, pair[1], zero)


def fold(square):
    square = jnp.where(diagonal_mask(), square, 0.0)
    return (
        square[0:HEAD_DIM]
        + square[HEAD_DIM : 2 * HEAD_DIM]
        + square[2 * HEAD_DIM : 3 * HEAD_DIM]
        + square[3 * HEAD_DIM :]
    )


def unfold(wide):
    return jnp.where(diagonal_mask(), jnp.concatenate([wide] * 4, axis=0), 0.0)


def positive(values):
    return jnp.where(values > 0, values + 1.0, jnp.exp(jnp.minimum(values, 0.0)))


def norm_parts(rows):
    row_mean = jnp.mean(rows, axis=-1, keepdims=True)
    centred = rows - row_mean
    row_inv = lax.rsqrt(jnp.mean(centred * centred, axis=-1, keepdims=True) + norm_eps)
    return centred * row_inv, row_inv


def split_rows(source, high, low, rows, step):
    def one(r, _):
        s = pl.ds(pl.multiple_of(r * step, step), step)
        high[s, :], low[s, :] = split(source[s, :])
        return 0

    lax.fori_loop(0, rows // step, one, 0)


STATE = HEAD_DIM + 8


def attend_kernel(
    dims,
    tok_in, attn_in, ffn_in, wqkv_in, wout_in,
    tok_out, gains_out, proj_out, den_out, prior_out, mix_out, wout_out,
    raw, tok, mix, gains, proj, den, prior, state, state_in, wstage, w_h, w_l, n_h, n_l, wout,
    tok_sem, mix_sem, gain_sem, state_sem, out_sem, mate_sem, pair_sem, load_sem, store_sem,
):
    images, length, used, rows = dims
    width = tok.shape[2]
    z, h, c, near_x, near_y, far = place()
    seq = lax.axis_size("seq")
    out_rows = wout_in.shape[0] // 4

    loads = [
        pltpu.make_async_copy(tok_in.at[i], raw.at[i], load_sem.at[i]) for i in range(images)
    ]
    loads += [
        pltpu.make_async_copy(wqkv_in.at[pl.ds(j * width, width)], wstage.at[:, lanes(j)], load_sem.at[images + j])
        for j in range(3)
    ]
    for copy in loads:
        copy.start()

    gains[:, lanes(h)] = jnp.zeros((8, LANES), F32)
    gains[0:1, lanes(h)] = attn_in[...]
    gains[1:2, lanes(h)] = ffn_in[...]
    blank = jnp.zeros((rows - used, LANES), F32)
    for i in range(images):
        for other in (near_x, near_y, far):
            tok[i, used:rows, lanes(other)] = blank
    for i in range(images):
        loads[i].wait()
        pad_rows(raw, tok, i, h)

    enter(
        [{"head": near_x}, {"head": near_y}, {"head": far}, {"dp": 1 - c}]
        + [{"seq": lax.rem(z + d, seq)} for d in range(1, seq)]
    )
    tokens = Gather(lambda i: tok.at[i, :, lanes(h)], tok, used, tok_sem)
    mixes = Gather(lambda i: mix.at[i, :, lanes(h)], mix, used, mix_sem)
    tokens.direct(0)
    gain_copies = [
        remote(gains.at[:, lanes(h)], gains.at[:, lanes(h)], gain_sem.at[k], gain_sem.at[3 + k], {"head": other})
        for k, other in enumerate((near_x, near_y, far))
    ]
    for copy in gain_copies:
        copy.start()
    tokens.direct(1)
    for copy in loads[images:]:
        copy.wait()
    split_rows(wstage, w_h, w_l, wstage.shape[0], 64)
    for k, other in enumerate((near_x, near_y, far)):
        remote(
            gains.at[:, lanes(other)], gains.at[:, lanes(other)], gain_sem.at[k], gain_sem.at[3 + k],
            {"head": other},
        ).wait_recv()
    row_ok = lax.broadcasted_iota(jnp.int32, (rows, LANES), 0) < length

    def project(i):

        for s in row_blocks(rows):
            n_h[s, :], n_l[s, :] = split(norm_parts(tok[i, s, :])[0] * gains[0:1, :])
        proj[i] = dot3((n_h[...], n_l[...]), (w_h[...], w_l[...]), "nn")
        key_feat = jnp.where(row_ok, positive(proj[i, :, lanes(1)]), 0.0)
        state[i, 0:HEAD_DIM, :] = fold(dot3(split(key_feat), split(proj[i, :, lanes(2)]), "tn"))
        state[i, HEAD_DIM:, :] = jnp.broadcast_to(
            jnp.sum(key_feat, axis=0, keepdims=True), (STATE - HEAD_DIM, LANES)
        )
        for d in range(1, seq):

            @pl.when(z + d < seq)
            def _():
                state_copy(i, d, d).start()

    def state_copy(i, d, step):
        return remote(
            state.at[i], state_in.at[d - 1, i], state_sem.at[0, d - 1, i], state_sem.at[1, d - 1, i],
            {"seq": lax.rem(z + step + seq, seq)},
        )

    def attend(i):
        prior[i] = jnp.zeros((STATE, LANES), F32)
        for d in range(1, seq):

            @pl.when(z >= d)
            def _():
                state_copy(i, d, -d).wait_recv()
                prior[i] = prior[i] + state_in[d - 1, i]

        query_feat = positive(proj[i, :, lanes(0)])
        key_feat = jnp.where(row_ok, positive(proj[i, :, lanes(1)]), 0.0)
        query_pair, key_pair = split(query_feat), split(key_feat)
        value_pair = split(proj[i, :, lanes(2)])
        total = prior[i, HEAD_DIM : HEAD_DIM + 1, :]
        ones = jnp.where(diagonal_mask(), 1.0, 0.0).astype(BF)
        num = dot3(query_pair, split(unfold(prior[i, 0:HEAD_DIM, :])), "nn")
        below = dot2(split(query_feat * total), ones, "nn")
        row = lax.broadcasted_iota(jnp.int32, (rows, rows), 0)
        col = lax.broadcasted_iota(jnp.int32, (rows, rows), 1)
        for mask in head_masks(rows):
            scores = dot3(query_pair, pick(mask, key_pair), "nt")
            score_pair = split(jnp.where(col <= row, scores, 0.0))
            num = num + dot3(score_pair, pick(mask, value_pair), "nn")
            below = below + dot2(score_pair, jnp.where(mask, 1.0, 0.0).astype(BF), "nn")
        den[i] = below
        mix[i, :, lanes(h)] = jnp.where(row_ok, num / below, 0.0)
        blank_rows = jnp.zeros((rows - used, LANES), F32)
        for other in (near_x, near_y, far):
            mix[i, used:rows, lanes(other)] = blank_rows

    mate = z + 1 - 2 * lax.rem(z, 2)

    def quarter(plane, core):
        return pl.ds(pl.multiple_of((2 * lax.rem(plane, 2) + core) * out_rows, out_rows), out_rows)

    own_rows = quarter(z, c)
    out_copies = [
        remote(
            wout_in.at[own_rows], wout.at[h, own_rows], out_sem.at[0, k], out_sem.at[1, k], {"head": other}
        )
        for k, other in enumerate((near_x, near_y, far))
    ]
    out_own = pltpu.make_async_copy(wout_in, wout.at[h], load_sem.at[images + 4])

    def out_arrival(k, other):
        return remote(
            wout.at[other, own_rows], wout.at[other, own_rows], out_sem.at[0, k], out_sem.at[1, k],
            {"head": other},
        )

    def mate_copy(k, other, plane):
        part = wout.at[other, quarter(plane, c)]
        return remote(part, part, mate_sem.at[0, k], mate_sem.at[1, k], {"seq": mate})

    def pair_copy(k, other, plane, core, late):
        part = wout.at[other, quarter(plane, core)]
        return remote(part, part, pair_sem.at[0, late, k], pair_sem.at[1, late, k], {"dp": 1 - c})

    peers = tuple(enumerate((near_x, near_y, far)))
    stores = []

    def store(src, dst):
        copy = pltpu.make_async_copy(src, dst, store_sem.at[len(stores)])
        copy.start()
        stores.append(copy)

    for t in range(images + 2):
        if t < images:
            tokens.forward(t)
            if t + 2 < images:
                tokens.direct(t + 2)
            elif t == images - 1:
                for copy in out_copies:
                    copy.start()
                out_own.start()
        if 1 <= t <= images:
            tokens.ready(t - 1)
            project(t - 1)
            store(tok.at[t - 1], tok_out.at[t - 1])
            store(proj.at[t - 1], proj_out.at[t - 1])
        if t == images + 1:
            for k, other in peers:
                out_arrival(k, other).wait_recv()
                mate_copy(k, other, z).start()
                pair_copy(k, other, z, c, 0).start()
        if t >= 2:
            attend(t - 2)
            mixes.direct(t - 2)
            store(den.at[t - 2], den_out.at[t - 2])
            store(prior.at[t - 2], prior_out.at[t - 2])
    store(gains, gains_out)
    out_own.wait()
    for i in range(images - 1):
        mixes.forward(i)
    for k, other in peers:
        mate_copy(k, other, mate).wait_recv()
        pair_copy(k, other, mate, c, 1).start()
    mixes.forward(images - 1)
    for k, other in peers:
        pair_copy(k, other, z, 1 - c, 0).wait_recv()
        pair_copy(k, other, mate, 1 - c, 1).wait_recv()
    store(wout, wout_out)
    for i in range(images):
        mixes.ready(i)
        store(mix.at[i], mix_out.at[i])
    for i in range(images):
        tokens.finish(i)
        mixes.finish(i)
        for d in range(1, seq):

            @pl.when(z + d < seq)
            def _(i=i, d=d):
                state_copy(i, d, d).wait_send()

    for copy in gain_copies + out_copies:
        copy.wait_send()
    for k, other in peers:
        mate_copy(k, other, z).wait_send()
        pair_copy(k, other, z, c, 0).wait_send()
        pair_copy(k, other, mate, c, 1).wait_send()
    for copy in stores:
        copy.wait()


def attend_call(tokens, gain_attn, gain_ffn, wqkv, wout):
    images, length, _ = tokens.shape
    used = round_up(length, 8)
    rows = padded(length)
    width = wqkv.shape[0] // 3
    heads_n = width // LANES
    dma = pltpu.SemaphoreType.DMA
    seq = lax.axis_size("seq")
    any_spec = pl.BlockSpec(memory_space=pl.ANY)
    vmem_spec = pl.BlockSpec(memory_space=pltpu.VMEM)
    shape = lambda *s: jax.ShapeDtypeStruct(s, F32)
    return pl.pallas_call(
        functools.partial(attend_kernel, (images, length, used, rows)),
        out_shape=(
            shape(images, rows, width),
            shape(8, width),
            shape(images, rows, 3 * LANES),
            shape(images, rows, LANES),
            shape(images, STATE, LANES),
            shape(images, rows, width),
            shape(heads_n, LANES, width),
        ),
        in_specs=[any_spec, vmem_spec, vmem_spec, any_spec, any_spec],
        out_specs=(any_spec,) * 7,
        scratch_shapes=[
            pltpu.VMEM((images, length, LANES), F32),
            pltpu.VMEM((images, rows, width), F32),
            pltpu.VMEM((images, rows, width), F32),
            pltpu.VMEM((8, width), F32),
            pltpu.VMEM((images, rows, 3 * LANES), F32),
            pltpu.VMEM((images, rows, LANES), F32),
            pltpu.VMEM((images, STATE, LANES), F32),
            pltpu.VMEM((images, STATE, LANES), F32),
            pltpu.VMEM((seq - 1, images, STATE, LANES), F32),
            pltpu.VMEM((width, 3 * LANES), F32),
            pltpu.VMEM((width, 3 * LANES), BF),
            pltpu.VMEM((width, 3 * LANES), BF),
            pltpu.VMEM((rows, width), BF),
            pltpu.VMEM((rows, width), BF),
            pltpu.VMEM((heads_n, LANES, width), F32),
            dma((images, Gather.SEMS)),
            dma((images, Gather.SEMS)),
            dma((6,)),
            dma((2, seq - 1, images)),
            dma((2, 3)),
            dma((2, 3)),
            dma((2, 2, 3)),
            dma((images + 5,)),
            dma((5 * images + 4,)),
        ],
        compiler_params=pltpu.CompilerParams(
            collective_id=0, has_side_effects=True, vmem_limit_bytes=VMEM_BYTES
        ),
    )(tokens, gain_attn, gain_ffn, wqkv, wout)


VMEM_BYTES = 60 * 1024 * 1024
class Scatter:
    SEMS = 12

    def __init__(self, part, buffers, rows, sems):
        self.part, self.buffers, self.sems = part, buffers, sems
        self.half = round_up(rows // 2, 8)
        self.rows = rows
        self.first, self.second = pl.ds(0, self.half), pl.ds(self.half, rows - self.half)
        self.left = pl.ds(0, rows - self.half)

    def slot(self, i, k):
        rows = self.first if k in (0, 2, 5) else self.left
        return self.buffers.at[i, k, rows]

    def copy(self, i, k, src, into=None):
        _, _, _, near_x, near_y, _ = place()
        into = k if into is None else into
        device = near_x if into in (0, 2, 4) else near_y
        return remote(
            src, self.slot(i, into), self.sems.at[i, into], self.sems.at[i, 6 + into], {"head": device}
        )

    def sent(self, i):
        _, _, _, near_x, near_y, far = place()
        part = self.part(i)
        return (
            self.copy(i, 2, part.at[self.first, lanes(far)]),
            self.copy(i, 3, part.at[self.second, lanes(far)]),
            self.copy(i, 0, part.at[self.first, lanes(near_x)]),
            self.copy(i, 1, part.at[self.second, lanes(near_y)]),
        )

    def passed(self, i):
        return (
            self.copy(i, 2, self.slot(i, 2), 5),
            self.copy(i, 3, self.slot(i, 3), 4),
        )

    def direct(self, i):
        for copy in self.sent(i):
            copy.start()

    def relay(self, i):
        _, _, _, near_x, near_y, _ = place()
        part = self.part(i)
        to_y, to_x = self.passed(i)
        self.copy(i, 2, self.slot(i, 2)).wait_recv()
        self.buffers[i, 2, self.first] = self.buffers[i, 2, self.first] + part[self.first, lanes(near_y)]
        to_y.start()
        self.copy(i, 3, self.slot(i, 3)).wait_recv()
        self.buffers[i, 3, self.left] = self.buffers[i, 3, self.left] + part[self.second, lanes(near_x)]
        to_x.start()

    def total(self, i):
        _, h, _, _, _, _ = place()
        part = self.part(i)
        for k in (0, 5, 1, 4):
            self.copy(i, k, self.slot(i, k)).wait_recv()
        first = (
            part[self.first, lanes(h)] + self.buffers[i, 0, self.first] + self.buffers[i, 5, self.first]
        )
        second = part[self.second, lanes(h)] + self.buffers[i, 1, self.left] + self.buffers[i, 4, self.left]
        return jnp.concatenate([first, second], axis=0)

    def finish(self, i):
        for copy in self.sent(i) + self.passed(i):
            copy.wait_send()


def activation(values):
    scale = 0.7978845608028654
    square = values * values
    bent = jnp.tanh(scale * values * (1.0 + 0.044715 * square))
    half = 0.5 * (1.0 + bent)
    slope = half + 0.5 * values * (1.0 - bent * bent) * (scale * (1.0 + 0.134145 * square))
    return values * half, slope


def to_lanes(first, second, rows):
    lane = lax.broadcasted_iota(jnp.int32, (rows, 128), 1)
    both = jnp.where(lane == 0, first, jnp.where(lane == 1, second, 0.0))
    both = jnp.concatenate([both, jnp.zeros((LANES - rows, 128), F32)], axis=0)
    return jnp.transpose(both)[0:8]


def to_columns(block, rows):
    tall = jnp.concatenate([block, jnp.zeros((120, LANES), F32)], axis=0)
    turned = jnp.transpose(tall)[0:rows]
    return turned[:, 0:1], turned[:, 1:2]


class Reduce:
    SEMS = 12
    RING = 12
    LATE = 3

    def __init__(self, sems, total):
        self.sems, self.total = sems, total
        self.chunks = []
        self.clock = 0
        self.ready = 0

    def chunk(self, mine, theirs, got, result, result_other, room):
        self.chunks.append(
            dict(mine=mine, theirs=theirs, got=got, result=result, result_other=result_other, slot=room)
        )

    def add(self, partial, arrived, result, rows, ring, columns):
        c = lax.axis_index("dp")
        half = partial.shape[0] // 2
        for j in columns:
            for r in range(half // rows):
                here = pl.ds(pl.multiple_of(c * half + r * rows, 8), rows)
                there = pl.ds(pl.multiple_of((1 - c) * half + r * rows, 8), rows)
                self.chunk(
                    partial.at[here, lanes(j)], partial.at[there, lanes(j)],
                    arrived.at[pl.ds(r * rows, rows), lanes(j)], result.at[here, lanes(j)], result.at[there, lanes(j)],
                    ring.at[len(self.chunks) % self.RING, :, pl.ds(0, rows)],
                )
        return len(self.chunks)

    def add_columns(self, partial, arrived, result, rows, ring):
        c = lax.axis_index("dp")
        depth = partial.shape[0]
        half = depth // 2
        for j in range(partial.shape[1] // LANES):
            for r in range(half // rows):
                here = pl.multiple_of(c * half + r * rows, 8)
                there = pl.multiple_of((1 - c) * half + r * rows, 8)
                self.chunk(
                    partial.at[pl.ds(here, rows), lanes(j)], partial.at[pl.ds(there, rows), lanes(j)],
                    arrived.at[pl.ds(j * half + r * rows, rows)],
                    result.at[pl.ds(j * depth + here, rows)], result.at[pl.ds(j * depth + there, rows)],
                    ring.at[len(self.chunks) % self.RING],
                )
        return len(self.chunks)

    def side(self, k):
        z = lax.axis_index("seq")
        return z if k % 2 == 0 else 3 - z

    def device(self, k, y):
        return {"seq": y if k % 2 == 0 else 3 - y}

    def sem(self, k, n):
        return self.sems.at[k, n]

    def pair(self, k):
        chunk = self.chunks[k]
        c = lax.axis_index("dp")
        return remote(chunk["theirs"], chunk["got"], self.sem(k, 0), self.sem(k, 1), {"dp": 1 - c})

    def partial(self, k, into, y):
        chunk = self.chunks[k]
        return remote(
            chunk["mine"], chunk["slot"].at[into], self.sem(k, 2), self.sem(k, 3 + into), self.device(k, y)
        )

    def outcome(self, k, src, y, send):
        return remote(src, self.chunks[k]["result"], self.sem(k, send), self.sem(k, 5), self.device(k, y))

    def twin(self, k, src):
        c = lax.axis_index("dp")
        return remote(src, self.chunks[k]["result"], self.sem(k, 8), self.sem(k, 9), {"dp": 1 - c})

    def kept(self, k):
        chunk = self.chunks[k]
        return pltpu.make_async_copy(chunk["mine"], chunk["result"], self.sem(k, 10))

    def exchange(self, first, end):
        for k in range(first, end):
            self.pair(k).start()
        self.ready = end

    def combine(self, k):
        chunk, y = self.chunks[k], self.side(k)
        self.pair(k).wait_recv()
        chunk["mine"][...] = chunk["mine"][...] + chunk["got"][...]

        @pl.when(y == 0)
        def _():
            self.partial(k, 0, 1).start()

        @pl.when(y == 3)
        def _():
            self.partial(k, 0, 2).start()

    def middle(self, k):
        chunk, y = self.chunks[k], self.side(k)

        @pl.when(y == 2)
        def _():
            self.partial(k, 0, 3).wait_recv()
            chunk["mine"][...] = chunk["mine"][...] + chunk["slot"][0]
            self.partial(k, 1, 1).start()

    def root(self, k):
        chunk, y = self.chunks[k], self.side(k)

        @pl.when(y == 1)
        def _():
            self.partial(k, 0, 0).wait_recv()
            self.partial(k, 1, 2).wait_recv()
            chunk["mine"][...] = chunk["mine"][...] + chunk["slot"][0] + chunk["slot"][1]
            self.outcome(k, chunk["mine"], 2, 6).start()
            self.outcome(k, chunk["mine"], 0, 7).start()
            self.kept(k).start()
            self.twin(k, chunk["mine"]).start()

    def onward(self, k):
        chunk, y = self.chunks[k], self.side(k)

        @pl.when(y == 2)
        def _():
            self.outcome(k, chunk["result"], 1, 6).wait_recv()
            self.outcome(k, chunk["result"], 3, 6).start()
            self.twin(k, chunk["result"]).start()

    def leaf(self, k):
        chunk, y = self.chunks[k], self.side(k)

        @pl.when(y == 0)
        def _():
            self.outcome(k, chunk["result"], 1, 6).wait_recv()
            self.twin(k, chunk["result"]).start()

        @pl.when(y == 3)
        def _():
            self.outcome(k, chunk["result"], 2, 6).wait_recv()
            self.twin(k, chunk["result"]).start()

    def finish(self, k):
        chunk, y = self.chunks[k], self.side(k)
        c = lax.axis_index("dp")
        self.pair(k).wait_send()
        remote(
            chunk["result_other"], chunk["result_other"], self.sem(k, 8), self.sem(k, 9), {"dp": 1 - c}
        ).wait_recv()
        self.twin(k, chunk["result"]).wait_send()

        @pl.when(y == 0)
        def _():
            self.partial(k, 0, 1).wait_send()

        @pl.when(y == 3)
        def _():
            self.partial(k, 0, 2).wait_send()

        @pl.when(y == 2)
        def _():
            self.partial(k, 1, 1).wait_send()
            self.outcome(k, chunk["result"], 3, 6).wait_send()

        @pl.when(y == 1)
        def _():
            self.outcome(k, chunk["mine"], 2, 6).wait_send()
            self.outcome(k, chunk["mine"], 0, 7).wait_send()
            self.kept(k).wait()

    def tick(self):
        if self.clock >= self.ready and self.ready < self.total:
            return
        stages = (self.leaf, self.onward, self.root, self.middle, self.combine)
        for k, act in enumerate(stages):
            chunk = self.clock - self.LATE * (len(stages) - 1 - k)
            if 0 <= chunk < self.total:
                act(chunk)
        self.clock += 1

    def drain(self):
        while self.clock < self.total + 4 * self.LATE:
            self.tick()


CHUNK = 128
ROW_TILE = 16


def row_sums(total, value):
    return total + jnp.sum(value, axis=-1, keepdims=True)


def layer_kernel(
    dims,
    tok_in, mix_in, gains_in, wfull_in, up_in, bias, down_in, down_bias, grad_in,
    proj_in, den_in, prior_in, wout_in, wqkv_in,
    out_out, tok_grad_out, qkv_out, out_w_out, up_out, down_out, small_out,
    gains, grad, resid_grad, part_ffn, part, buf_norm, buf_tok, xhat_own, inv_own,
    d_down, d_up, d_small, got_ffn, got_out, got_qkv, got_small, state, state_in, ring,
    grad_sem, norm_sem, back_sem, ffn_sem, tok_sem, state_sem, chunk_sem, load_sem, stage_sem, image_sem, store_sem,
):
    images, length, used, rows = dims
    width = grad.shape[2]
    hidden = up_in.shape[1]
    z, h, c, near_x, near_y, far = place()
    seq = lax.axis_size("seq")
    vmem = pltpu.VMEM
    tiles = width // LANES
    row_ok = lax.broadcasted_iota(jnp.int32, (rows, LANES), 0) < length

    small = (pltpu.make_async_copy(gains_in, gains, load_sem.at[0]),)

    grads = Gather(lambda i: grad.at[i, :, lanes(h)], grad, used, grad_sem)
    norm = Scatter(lambda i: part.at[i % 2], buf_norm, rows, norm_sem)
    back = Gather(lambda i: resid_grad.at[i, :, lanes(h)], resid_grad, used, back_sem)
    ffn = Scatter(lambda i: part_ffn.at[i], buf_norm, used, ffn_sem)
    toks = Scatter(lambda i: part.at[i % 2], buf_tok, rows, tok_sem)
    reduce = Reduce(chunk_sem, chunk_sem.shape[0])
    tick = reduce.tick
    stores = []

    def store(src, dst):
        copy = pltpu.make_async_copy(src, dst, store_sem.at[len(stores)])
        copy.start()
        stores.append(copy)

    def halves(source, high, low):
        split_rows(source, high, low, rows, ROW_TILE)

    def stats(i, weight, sums_with):
        first, second = [], []
        for s in row_blocks(rows):
            term = part[i % 2, s, :]
            first.append(jnp.sum(term * gains[weight, :], axis=-1, keepdims=True))
            second.append(jnp.sum(term * sums_with(s), axis=-1, keepdims=True))
        block = to_lanes(jnp.concatenate(first, axis=0), jnp.concatenate(second, axis=0), rows)
        for k in range(tiles):
            part[i % 2, rows - 8 : rows, lanes(k)] = block

    def norm_share(scatter, i, weight, hat, inv):
        both = scatter.total(i)
        mean, cross = to_columns(both[rows - 8 : rows], rows)
        own = jnp.where(row_ok, both, 0.0)
        scaled = own * gains[weight, lanes(h)]
        share = (scaled - mean * (1.0 / width) - hat * (cross * (1.0 / width))) * inv
        return share, own

    def resid_back(i):
        share, own = norm_share(norm, i, slice(1, 2), xhat_own[i], inv_own[i, :, 0:1])
        resid_grad[i, :, lanes(h)] = jnp.where(row_ok, grad[i, :, lanes(h)] + share, 0.0)
        for k, value in ((1, own * xhat_own[i]), (2, grad[i, :, lanes(h)])):
            d_small[8:9, lanes(k)] = d_small[8:9, lanes(k)] + jnp.sum(value, axis=0, keepdims=True)
        norm.finish(i)
        back.direct(i)

    def load_phase(raw):
        copies = [pltpu.make_async_copy(grad_in.at[i], raw.at[i], load_sem.at[3 + i]) for i in range(images)]
        for copy in copies + list(small):
            copy.start()
        blank = jnp.zeros((rows - used, LANES), F32)
        for i in range(images):
            for other in (near_x, near_y, far):
                grad[i, used:rows, lanes(other)] = blank
                resid_grad[i, used:rows, lanes(other)] = blank
        d_small[...] = jnp.zeros_like(d_small)
        for i in range(images):
            copies[i].wait()
            pad_rows(raw, grad, i, h)

    def ffn_phase(
        wo_h, wo_l, up_h, up_l, dn_h, dn_l, pair_h, pair_l, n_h, n_l, hid_h, hid_l, slope, ug_h, ug_l
    ):
        def weight_copy(k):
            source, stage, _, _ = weights[k]
            return pltpu.make_async_copy(source, stage, stage_sem.at[k])

        def take(k):
            _, stage, high, low = weights[k]
            weight_copy(k).wait()
            split_rows(stage, high, low, stage.shape[0], 64)

        weights = (
            (wfull_in, d_down, wo_h, wo_l),
            (up_in, d_up, up_h, up_l),
            (down_in, d_up, dn_h, dn_l),
        )

        def turned(source, target):
            def one(k, _):
                s = lanes(k)
                target[:, s] = source[s, :].T
                return 0

            lax.fori_loop(0, tiles, one, 0)

        def tok_copy(i):
            return pltpu.make_async_copy(tok_in.at[i], part.at[0], image_sem.at[0])

        def mix_copy(i):
            return pltpu.make_async_copy(mix_in.at[i], part.at[1], image_sem.at[1])

        def forward(i):
            mix_copy(i).wait()
            halves(part.at[1], pair_h, pair_l)
            if i + 1 < images:
                mix_copy(i + 1).start()
            if i == 0:
                take(0)
            tok_copy(i).wait()
            part[0] = part[0] + dot3((pair_h[...], pair_l[...]), (wo_h[...], wo_l[...]), "nn")
            part_ffn[i, :, lanes(h)] = part[0, :, lanes(h)]
            grads.forward(i)
            if i + 2 < images:
                grads.direct(i + 2)

            for s in row_blocks(rows):
                hat, inv = norm_parts(part[0, s, :])
                part[0, s, :] = hat
                inv_own[i, s, :] = jnp.broadcast_to(inv, (ROW_TILE, 128))
                n_h[i, s, :], n_l[i, s, :] = split(hat * gains[1:2, :])
            xhat_own[i] = part[0, :, lanes(h)]
            if i + 1 < images:
                tok_copy(i + 1).start()
            if i == 0:
                take(1)
                weight_copy(2).start()
            slope[i] = dot3((n_h[i], n_l[i]), (up_h[...], up_l[...]), "nn") + bias[0:1, :]
            for s in row_blocks(rows):
                act, by = activation(slope[i, s, :])
                hid_h[i, s, :], hid_l[i, s, :] = split(act)
                slope[i, s, :] = by
            grads.ready(i)
            halves(grad.at[i], pair_h, pair_l)

            term = dot3((hid_h[i], hid_l[i]), (pair_h[...], pair_l[...]), "tn")
            d_down[...] = term if i == 0 else d_down[...] + term

        def hidden_back(i):
            halves(grad.at[i], pair_h, pair_l)

            part[i % 2] = dot3((pair_h[...], pair_l[...]), (up_h[...], up_l[...]), "nn")
            total = jnp.zeros((1, hidden), F32)
            for s in row_blocks(rows):
                ug = part[i % 2, s, :] * slope[i, s, :]
                ug_h[s, :], ug_l[s, :] = split(ug)
                total = total + jnp.sum(ug, axis=0, keepdims=True)
            d_small[0:1, :] = d_small[0:1, :] + total

        def up_grad(i):
            term = dot3((n_h[i], n_l[i]), (ug_h[...], ug_l[...]), "tn")
            d_up[...] = term if i == 0 else d_up[...] + term

        def norm_back(i):
            part[i % 2] = dot3((ug_h[...], ug_l[...]), (wo_h[...], wo_l[...]), "nn")
            stats(i, slice(1, 2), lambda s: n_h[i, s, :].astype(F32) + n_l[i, s, :].astype(F32))
            norm.direct(i)

        def down(i):
            resid = part_ffn[i, :, lanes(h)]

            part_ffn[i] = dot3((hid_h[i], hid_l[i]), (dn_h[...], dn_l[...]), "nn")
            part_ffn[i, :, lanes(h)] = part_ffn[i, :, lanes(h)] + resid

        weight_copy(0).start()
        mix_copy(0).start()
        tok_copy(0).start()
        weight_copy(1).start()
        for copy in small:
            copy.wait()
        for i in range(images):
            forward(i)
            if i == 0:
                take(2)
        reduce.exchange(0, down_chunks)
        turned(up_h, wo_h)
        turned(up_l, wo_l)
        turned(dn_h, up_h)
        turned(dn_l, up_l)
        for i in range(images):
            hidden_back(i)
            tick()
            up_grad(i)
            if i == images - 1:
                reduce.exchange(down_chunks, up_chunks)
            tick()
            if i >= 1:
                norm.relay(i - 1)
            norm_back(i)
            tick()
            if i >= 2:
                back.forward(i - 2)
                tick()
            if i >= 1:
                resid_back(i - 1)
                tick()
        last = images - 1
        down(0)
        tick()
        norm.relay(last)
        down(1)
        tick()
        back.forward(last - 1)
        down(2)
        tick()
        resid_back(last)
        down(3)
        tick()
        back.forward(last)

    def attend_phase(
        wo_h, wo_l, wq_h, wq_l, tok, proj, den, prior, mixed, rg_h, rg_l, n_h, n_l, xhat, pg_h, pg_l,
        dnum, dden, later, hat_own, root_own, d_out, d_qkv, out_trim, tok_trim,
    ):
        def image_copies(i):
            return (
                pltpu.make_async_copy(mix_in.at[i, :, lanes(h)], mixed.at[i], load_sem.at[8 + 4 * i]),
                pltpu.make_async_copy(den_in.at[i], den.at[i], load_sem.at[9 + 4 * i]),
                pltpu.make_async_copy(proj_in.at[i], proj.at[i], load_sem.at[10 + 4 * i]),
                pltpu.make_async_copy(prior_in.at[i], prior.at[i], load_sem.at[11 + 4 * i]),
            )

        def tok_copy(i):
            return pltpu.make_async_copy(tok_in.at[i], tok.at[i % 2], image_sem.at[i % 2])

        weights = [pltpu.make_async_copy(wout_in, d_out, load_sem.at[0])]
        weights += [
            pltpu.make_async_copy(wqkv_in.at[pl.ds(j * width, width)], d_qkv.at[:, lanes(j)], load_sem.at[1 + j])
            for j in range(3)
        ]
        for copy in weights:
            copy.start()
        for i in range(images):
            for copy in image_copies(i):
                copy.start()
        tok_copy(0).start()
        tok_copy(1).start()
        reduce.add(d_out, got_out, out_w_out, CHUNK, ring, range(tiles))
        out_chunks = reduce.add(d_small, got_small, small_out, 8, ring, range(1, tiles))
        qkv_chunks = reduce.add_columns(d_qkv, got_qkv, qkv_out, CHUNK, ring)
        all_chunks = reduce.add(d_small, got_small, small_out, 8, ring, range(1))

        def state_copy(i, d, step):
            return remote(
                state.at[i], state_in.at[d - 1, i], state_sem.at[0, d - 1, i], state_sem.at[1, d - 1, i],
                {"seq": lax.rem(z + step + seq, seq)},
            )

        def first_half(i):
            back.ready(i)
            for copy in image_copies(i):
                copy.wait()
            halves(resid_grad.at[i], rg_h, rg_l)
            dm = dot3((rg_h[...], rg_l[...]), (wo_h[...], wo_l[...]), "nn")
            ones = jnp.where(diagonal_mask(), 1.0, 0.0).astype(BF)
            inverse = 1.0 / den[i]
            dnum[i] = dm * inverse
            dden[i] = -dot2(split(dm * mixed[i]), ones, "nn") * inverse
            query_feat = positive(proj[i, :, lanes(0)])
            state[i, 0:HEAD_DIM, :] = fold(dot3(split(query_feat), split(dnum[i]), "tn"))
            state[i, HEAD_DIM:, :] = jnp.broadcast_to(
                jnp.sum(query_feat * dden[i], axis=0, keepdims=True), (STATE - HEAD_DIM, LANES)
            )
            for d in range(1, seq):

                @pl.when(z >= d)
                def _():
                    state_copy(i, d, -d).start()

            term = dot3(split(mixed[i]), (rg_h[...], rg_l[...]), "tn")
            d_out[...] = term if i == 0 else d_out[...] + term

        def second_half(i):
            later[...] = jnp.zeros_like(later)
            for d in range(1, seq):

                @pl.when(z + d < seq)
                def _():
                    state_copy(i, d, d).wait_recv()
                    later[...] = later[...] + state_in[d - 1, i]

            query, key, value = (proj[i, :, lanes(k)] for k in range(3))
            query_feat = positive(query)
            key_feat = jnp.where(row_ok, positive(key), 0.0)
            query_pair, key_pair, value_pair = split(query_feat), split(key_feat), split(value)
            dden_i = dden[i]
            dnum_pair = split(dnum[i])
            prior_pair = split(unfold(prior[i, 0:HEAD_DIM, :]))
            later_pair = split(unfold(later[0:HEAD_DIM, :]))
            fq = dot3(dnum_pair, prior_pair, "nt") + dden_i * prior[i, HEAD_DIM : HEAD_DIM + 1, :]
            fk = dot3(value_pair, later_pair, "nt") + later[HEAD_DIM : HEAD_DIM + 1, :]
            fv = dot3(key_pair, later_pair, "nn")
            row = lax.broadcasted_iota(jnp.int32, (rows, rows), 0)
            col = lax.broadcasted_iota(jnp.int32, (rows, rows), 1)
            causal = col <= row
            for k, mask in enumerate(head_masks(rows)):
                key_h, query_h = pick(mask, key_pair), pick(mask, query_pair)
                scores = split(jnp.where(causal, dot3(query_pair, key_h, "nt"), 0.0))
                pull = dot3(dnum_pair, pick(mask, value_pair), "nt")
                pull = pull + dden_i[:, k * HEAD_DIM : k * HEAD_DIM + 1]
                pull = split(jnp.where(causal, pull, 0.0))
                fq = fq + dot3(pull, key_h, "nn")
                fk = fk + dot3(pull, query_h, "tn")
                fv = fv + dot3(scores, pick(mask, dnum_pair), "tn")
            slope = lambda v: jnp.where(v > 0, 1.0, jnp.exp(jnp.minimum(v, 0.0)))
            pg_h[:, lanes(0)], pg_l[:, lanes(0)] = split(fq * slope(query))
            pg_h[:, lanes(1)], pg_l[:, lanes(1)] = split(jnp.where(row_ok, fk * slope(key), 0.0))
            pg_h[:, lanes(2)], pg_l[:, lanes(2)] = split(fv)

        def weight_grads(i):
            tok_copy(i).wait()

            for s in row_blocks(rows):
                hat, inv = norm_parts(tok[i % 2, s, :])
                xhat[s, :] = hat
                root_own[i, s, :] = jnp.broadcast_to(inv, (ROW_TILE, 128))
                n_h[s, :], n_l[s, :] = split(hat * gains[0:1, :])
            hat_own[i] = xhat[:, lanes(h)]
            if i + 2 < images:
                tok_copy(i + 2).start()

            term = dot3((n_h[...], n_l[...]), (pg_h[...], pg_l[...]), "tn")
            d_qkv[...] = term if i == 0 else d_qkv[...] + term

        def norm_back(i):
            if i >= 2:
                toks.finish(i - 2)

            part[i % 2] = dot3((pg_h[...], pg_l[...]), (wq_h[...], wq_l[...]), "nn")
            stats(i, slice(0, 1), lambda s: xhat[s, :] * gains[0:1, :])
            toks.direct(i)

        def token_back(i):
            share, own = norm_share(toks, i, slice(0, 1), hat_own[i], root_own[i, :, 0:1])
            d_small[8:9, lanes(0)] = d_small[8:9, lanes(0)] + jnp.sum(own * hat_own[i], axis=0, keepdims=True)
            tok_trim[i] = (resid_grad[i, :, lanes(h)] + share)[0:length]
            store(tok_trim.at[i], tok_grad_out.at[i])

        def output(i):
            out_trim[i] = (ffn.total(i) + down_bias[0:1, :])[0:length]
            store(out_trim.at[i], out_out.at[i])

        for copy in weights:
            copy.wait()
        for k in range(tiles):
            wo_h[lanes(k), :], wo_l[lanes(k), :] = split(d_out[:, lanes(k)].T)

        def turn(k, _):
            for j in range(3):
                wq_h[lanes(j), lanes(k)], wq_l[lanes(j), lanes(k)] = split(d_qkv[lanes(k), lanes(j)].T)
            return 0

        lax.fori_loop(0, tiles, turn, 0)
        for i in range(images):
            first_half(i)
            tick()
        reduce.exchange(up_chunks, out_chunks)
        ffn.direct(0)
        ffn.direct(1)
        last = images - 1
        for i in range(images):
            second_half(i)
            tick()
            if i >= 1:
                toks.relay(i - 1)
            weight_grads(i)
            if i == last:
                reduce.exchange(out_chunks, qkv_chunks)
            tick()
            ffn.relay(i)
            if i < 2:
                ffn.direct(i + 2)
            norm_back(i)
            tick()
            if i >= 1:
                token_back(i - 1)
                tick()
                output(i - 1)
        tick()
        toks.relay(last)
        tick()
        output(last)
        tick()
        token_back(last)
        reduce.exchange(qkv_chunks, all_chunks)
        reduce.drain()
        for i in range(images):
            grads.finish(i)
            back.finish(i)
            ffn.finish(i)
            if i >= images - 2:
                toks.finish(i)
            for d in range(1, seq):

                @pl.when(z >= d)
                def _(i=i, d=d):
                    state_copy(i, d, -d).wait_send()

        for k in range(all_chunks):
            reduce.finish(k)
        for copy in stores:
            copy.wait()

    pl.run_scoped(load_phase, vmem((images, length, LANES), F32))
    enter(
        [{"head": near_x}, {"head": near_y}, {"dp": 1 - c}]
        + [{"seq": lax.rem(z + d, seq)} for d in range(1, seq)]
    )
    grads.direct(0)
    grads.direct(1)
    down_chunks = reduce.add(d_down, got_ffn.at[0], down_out, CHUNK, ring, range(tiles))
    up_chunks = reduce.add(d_up, got_ffn.at[1], up_out, CHUNK, ring, range(hidden // LANES))
    pair = lambda *s: [vmem(s, BF), vmem(s, BF)]
    pl.run_scoped(
        ffn_phase,
        *pair(width, width), *pair(width, hidden), *pair(hidden, width),
        *pair(rows, width), *pair(images, rows, width), *pair(images, rows, hidden),
        vmem((images, rows, hidden), F32), *pair(rows, hidden),
    )
    pl.run_scoped(
        attend_phase,
        *pair(width, LANES), *pair(3 * LANES, width), vmem((2, rows, width), F32),
        vmem((images, rows, 3 * LANES), F32), vmem((images, rows, LANES), F32), vmem((images, STATE, LANES), F32),
        vmem((images, rows, LANES), F32), *pair(rows, width), *pair(rows, width), vmem((rows, width), F32),
        *pair(rows, 3 * LANES), vmem((images, rows, LANES), F32), vmem((images, rows, LANES), F32),
        vmem((STATE, LANES), F32), vmem((images, rows, LANES), F32), vmem((images, rows, 128), F32),
        vmem((LANES, width), F32), vmem((width, 3 * LANES), F32),
        vmem((images, length, LANES), F32), vmem((images, length, LANES), F32),
    )


def layer_call(tok, mix, gains, wfull, up_weight, up_bias, down_weight, down_bias, grads, proj, den, prior, wout, wqkv):
    images, length, _ = grads.shape
    rows, width = tok.shape[1:]
    hidden = up_weight.shape[1]
    used = round_up(length, 8)
    seq = lax.axis_size("seq")
    any_spec = pl.BlockSpec(memory_space=pl.ANY)
    vmem_spec = pl.BlockSpec(memory_space=pltpu.VMEM)
    shape = lambda *s: jax.ShapeDtypeStruct(s, F32)
    vmem, dma = pltpu.VMEM, pltpu.SemaphoreType.DMA
    half = round_up(rows // 2, 8)
    chunks = (2 * (hidden // 2 // CHUNK) + LANES // 2 // CHUNK + 1) * (width // LANES) + 3 * (width // 2 // CHUNK)
    return pl.pallas_call(
        functools.partial(layer_kernel, (images, length, used, rows)),
        out_shape=(
            shape(images, length, LANES),
            shape(images, length, LANES),
            shape(3 * width, LANES),
            shape(LANES, width),
            shape(width, hidden),
            shape(hidden, width),
            shape(16, width),
        ),
        in_specs=[any_spec] * 5 + [vmem_spec, any_spec, vmem_spec] + [any_spec] * 6,
        out_specs=(any_spec,) * 7,
        scratch_shapes=[
            vmem((8, width), F32),
            vmem((images, rows, width), F32), vmem((images, rows, width), F32), vmem((images, rows, width), F32),
            vmem((2, rows, width), F32), vmem((images, 6, half, LANES), F32), vmem((images, 6, half, LANES), F32),
            vmem((images, rows, LANES), F32), vmem((images, rows, 128), F32),
            vmem((hidden, width), F32), vmem((width, hidden), F32), vmem((16, width), F32),
            vmem((2, hidden // 2, width), F32), vmem((LANES // 2, width), F32), vmem((3 * width // 2, LANES), F32),
            vmem((8, width), F32), vmem((images, STATE, LANES), F32), vmem((seq - 1, images, STATE, LANES), F32),
            vmem((Reduce.RING, 2, CHUNK, LANES), F32),
            dma((images, Gather.SEMS)), dma((images, Scatter.SEMS)), dma((images, Gather.SEMS)),
            dma((images, Scatter.SEMS)), dma((images, Scatter.SEMS)), dma((2, seq - 1, images)),
            dma((chunks, Reduce.SEMS)), dma((8 + 4 * images,)), dma((3,)), dma((2,)), dma((2 * images,)),
        ],
        compiler_params=pltpu.CompilerParams(
            collective_id=1, has_side_effects=True, vmem_limit_bytes=64 * 1024 * 1024
        ),
    )(tok, mix, gains, wfull, up_weight, up_bias, down_weight, down_bias, grads, proj, den, prior, wout, wqkv)


def fast_device(
    tokens,
    gain_attn,
    qkv_weight,
    out_weight,
    gain_ffn,
    up_weight,
    up_bias,
    down_weight,
    down_bias,
    out_grad,
):
    model_width, kinds, local_width = qkv_weight.shape

    proj_weight = jnp.transpose(qkv_weight, (1, 0, 2)).reshape(kinds * model_width, local_width)
    tok, gains, proj, den, prior, mix, wfull = attend_call(
        tokens, gain_attn[None], gain_ffn[None], proj_weight, out_weight
    )
    output, tok_grad, d_qkv, d_out, d_up, d_down, small = layer_call(
        tok, mix, gains, wfull.reshape(model_width, model_width), up_weight, up_bias[None], down_weight,
        down_bias[None], out_grad, proj, den, prior, out_weight, proj_weight,
    )
    return (
        output,
        tok_grad,
        small[8, 0:LANES],
        jnp.transpose(d_qkv.reshape(kinds, model_width, local_width), (1, 0, 2)),
        d_out,
        small[8, LANES : 2 * LANES],
        d_up,
        small[0],
        d_down,
        small[8, 2 * LANES : 3 * LANES],
    )


def device_function(mesh):
    if (mesh.shape["seq"], mesh.shape["head"], mesh.shape["dp"]) == (4, 4, 2):
        return fast_device
    return per_device


def solution(mesh):
    return jax.shard_map(
        device_function(mesh),
        mesh=mesh,
        in_specs=(
            P("dp", "seq", "head"),
            P("head"),
            P(None, None, "head"),
            P("head", None),
            P("head"),
            P(None, "head"),
            P("head"),
            P("head", None),
            P("head"),
            P("dp", "seq", "head"),
        ),
        out_specs=(
            P("dp", "seq", "head"),
            P("dp", "seq", "head"),
            P("head"),
            P(None, None, "head"),
            P("head", None),
            P("head"),
            P(None, "head"),
            P("head"),
            P("head", None),
            P("head"),
        ),
        check_vma=False,
    )
```

```python
import functools

import jax
import jax.numpy as jnp
from jax import lax
from jax.experimental import pallas as pl
from jax.experimental.pallas import tpu as pltpu
from jax.sharding import PartitionSpec as P

HEAD_DIM = 64


highest = lax.Precision.HIGH
norm_eps = 1e-05


def entering(part, axis, combine, identity, reverse):
    count = lax.axis_size(axis)
    place = lax.axis_index(axis)
    ahead = count - 1 - place if reverse else place
    gathered = jax.tree.map(lambda a: lax.all_gather(a, axis), part)
    state = jax.tree.map(lambda a, e: jnp.zeros_like(a) + jnp.asarray(e, a.dtype), part, identity)

    def one(turn, state):
        source = count - 1 - turn if reverse else turn
        return combine(
            state, jax.tree.map(lambda a: lax.dynamic_index_in_dim(a, source, 0, False), gathered)
        )

    return lax.fori_loop(0, ahead, one, state)


def feature(values_in):
    return jax.nn.elu(values_in) + 1.0


def layer_norm(values_in, gain):
    row_mean = jnp.mean(values_in, axis=-1, keepdims=True)
    centred = values_in - row_mean
    row_var = jnp.mean(centred * centred, axis=-1, keepdims=True)
    return centred * lax.rsqrt(row_var + norm_eps) * gain


def norm_back(partial_grad, rows_full, gain_full, gain_share):
    local_width = gain_share.shape[0]
    model_width = gain_full.shape[0]
    row_mean = jnp.mean(rows_full, axis=-1, keepdims=True)
    centred = rows_full - row_mean
    row_inv = lax.rsqrt(jnp.mean(centred * centred, axis=-1, keepdims=True) + norm_eps)
    scaled = partial_grad * gain_full
    sums = lax.psum(
        jnp.stack(
            [jnp.sum(scaled, axis=-1), jnp.sum(scaled * (centred * row_inv), axis=-1)]
        ),
        "head",
    )
    means = (sums / model_width)[:, :, None]
    share = lax.psum_scatter(partial_grad, "head", scatter_dimension=1, tiled=True)
    start = lax.axis_index("head") * local_width
    xhat = lax.dynamic_slice_in_dim(centred, start, local_width, 1) * row_inv
    back = (share * gain_share - means[0] - xhat * means[1]) * row_inv
    return back, jnp.sum(share * xhat, axis=0)


def mlp_act(values_in):
    return jax.nn.gelu(values_in, approximate=True)


def block_attend(query_proj, key_proj, value_proj, prior_state, prior_total):
    query_feat = feature(query_proj)
    key_feat = feature(key_proj)
    length_now = query_proj.shape[1]
    scores = jnp.einsum("gihe,gjhe->ghij", query_feat, key_feat, precision=highest)
    row_index = lax.broadcasted_iota(jnp.int32, (length_now, length_now), 0)
    col_index = lax.broadcasted_iota(jnp.int32, (length_now, length_now), 1)
    scores = jnp.where(col_index <= row_index, scores, jnp.float32(0.0))
    numerator = jnp.einsum("ghij,gjhe->gihe", scores, value_proj, precision=highest)
    numerator = numerator + jnp.einsum(
        "gihe,ghef->gihf", query_feat, prior_state, precision=highest
    )
    denominator = jnp.sum(scores, axis=-1) + jnp.einsum(
        "gihe,ghe->ghi", query_feat, prior_total, precision=highest
    )
    return numerator / jnp.transpose(denominator, (0, 2, 1))[..., None]


def block_state(key_proj, value_proj):
    key_feat = feature(key_proj)
    kv_sum = jnp.einsum("gihe,gihf->ghef", key_feat, value_proj, precision=highest)
    return (kv_sum, jnp.sum(key_feat, axis=1))


def add_pair(earlier, later):
    return (earlier[0] + later[0], earlier[1] + later[1])


def per_device(
    tokens,
    gain_attn,
    qkv_weight,
    out_weight,
    gain_ffn,
    up_weight,
    up_bias,
    down_weight,
    down_bias,
    out_grad,
):
    image_count, block_len, local_width = tokens.shape
    row_count = image_count * block_len
    model_width = qkv_weight.shape[0]
    heads_local = local_width // HEAD_DIM
    column_start = lax.axis_index("head") * local_width
    full_tokens, gain_first, gain_second = (
        lax.all_gather(tokens, "head", axis=2, tiled=True),
        lax.all_gather(gain_attn, "head", axis=0, tiled=True),
        lax.all_gather(gain_ffn, "head", axis=0, tiled=True),
    )
    token_rows = full_tokens.reshape(row_count, model_width)
    normed_one = layer_norm(token_rows, gain_first)
    proj_weight = qkv_weight.reshape(model_width, 3 * local_width)
    projected = jnp.dot(normed_one, proj_weight, precision=highest)
    parts_view = projected.reshape(image_count, block_len, 3, heads_local, HEAD_DIM)
    query_proj = parts_view[:, :, 0]
    key_proj = parts_view[:, :, 1]
    value_proj = parts_view[:, :, 2]
    (own_state, own_total), pull_state = jax.vjp(block_state, key_proj, value_proj)
    zero_pair = (jnp.zeros_like(own_state), jnp.zeros_like(own_total))
    prior_state, prior_total = entering((own_state, own_total), "seq", add_pair, zero_pair, False)
    mixed, pull_attend = jax.vjp(
        block_attend, query_proj, key_proj, value_proj, prior_state, prior_total
    )
    mixed_rows = mixed.reshape(row_count, local_width)
    branch_out = jnp.dot(mixed_rows, out_weight, precision=highest)
    token_share = tokens.reshape(row_count, local_width)
    resid_share = token_share + lax.psum_scatter(
        branch_out, "head", scatter_dimension=1, tiled=True
    )
    resid_full = lax.all_gather(resid_share, "head", axis=1, tiled=True)
    normed_two = layer_norm(resid_full, gain_second)
    up_proj = jnp.dot(normed_two, up_weight, precision=highest) + up_bias
    hidden, pull_act = jax.vjp(mlp_act, up_proj)
    down_proj = jnp.dot(hidden, down_weight, precision=highest)
    ffn_share = lax.psum_scatter(down_proj, "head", scatter_dimension=1, tiled=True)
    output = (resid_share + ffn_share + down_bias).reshape(tokens.shape)
    grad_share = out_grad.reshape(row_count, local_width)
    grad_full = lax.all_gather(grad_share, "head", axis=1, tiled=True)
    down_bias_grad = jnp.sum(grad_share, axis=0)
    down_weight_grad = jnp.dot(hidden.T, grad_full, precision=highest)
    hidden_grad = jnp.dot(grad_full, down_weight.T, precision=highest)
    (up_grad,) = pull_act(hidden_grad)
    up_bias_grad = jnp.sum(up_grad, axis=0)
    up_weight_grad = jnp.dot(normed_two.T, up_grad, precision=highest)
    ffn_grads = lax.psum((up_weight_grad, down_weight_grad), ("seq", "dp"))
    resid_back, gain_ffn_share = norm_back(
        jnp.dot(up_grad, up_weight.T, precision=highest), resid_full, gain_second, gain_ffn
    )
    resid_grad_share = grad_share + resid_back
    resid_grad = lax.all_gather(resid_grad_share, "head", axis=1, tiled=True)
    out_weight_grad = jnp.dot(mixed_rows.T, resid_grad, precision=highest)
    mixed_grad = jnp.dot(resid_grad, out_weight.T, precision=highest).reshape(mixed.shape)
    query_grad, key_grad, value_grad, state_grad, total_grad = pull_attend(mixed_grad)
    later_state, later_total = entering((state_grad, total_grad), "seq", add_pair, zero_pair, True)
    key_extra, value_extra = pull_state((later_state, later_total))
    key_grad = key_grad + key_extra
    value_grad = value_grad + value_extra
    proj_grad = jnp.stack([query_grad, key_grad, value_grad], axis=2).reshape(
        row_count, 3 * local_width
    )
    qkv_weight_grad = jnp.dot(normed_one.T, proj_grad, precision=highest).reshape(qkv_weight.shape)
    token_back, gain_attn_share = norm_back(
        jnp.dot(proj_grad, proj_weight.T, precision=highest), token_rows, gain_first, gain_attn
    )
    tokens_grad = (resid_grad_share + token_back).reshape(tokens.shape)
    summed_grads = lax.psum(
        (
            gain_attn_share,
            qkv_weight_grad,
            out_weight_grad,
            gain_ffn_share,
            up_bias_grad,
            down_bias_grad,
        ),
        ("seq", "dp"),
    )
    return (
        output,
        tokens_grad,
        summed_grads[0],
        summed_grads[1],
        summed_grads[2],
        summed_grads[3],
        ffn_grads[0],
        summed_grads[4],
        ffn_grads[1],
        summed_grads[5],
    )


MESH = pl.DeviceIdType.MESH
BF = jnp.bfloat16
F32 = jnp.float32
LANES = 256
DIMS = {
    "nn": (((1,), (0,)), ((), ())),
    "nt": (((1,), (1,)), ((), ())),
    "tn": (((0,), (0,)), ((), ())),
}


def round_up(value, step):
    return -(-value // step) * step


def padded(length):
    return round_up(round_up(length, 8) + 8, 16)


def row_blocks(rows):
    return [slice(r, r + 16) for r in range(0, rows, 16)]


def pad_rows(raw, slots, i, h):
    length, rows = raw.shape[1], slots.shape[1]
    slots[i, 0:length, lanes(h)] = raw[i]
    slots[i, length:rows, lanes(h)] = jnp.zeros((rows - length, LANES), F32)


def dot(left, right, kind):
    return lax.dot_general(left, right, DIMS[kind], preferred_element_type=F32)


def split(values):
    high = values.astype(BF)
    return high, (values - high.astype(F32)).astype(BF)


def dot3(left, right, kind):
    return (
        dot(left[0], right[0], kind) + dot(left[0], right[1], kind) + dot(left[1], right[0], kind)
    )


def dot2(left, right, kind):
    return dot(left[0], right, kind) + dot(left[1], right, kind)


def lanes(index):
    if isinstance(index, int):
        return pl.ds(index * LANES, LANES)
    return pl.ds(pl.multiple_of(index * LANES, LANES), LANES)


def place():
    z, h, c = lax.axis_index("seq"), lax.axis_index("head"), lax.axis_index("dp")
    near_x = h + 1 - 2 * lax.rem(h, 2)
    near_y = lax.rem(h + 2, 4)
    return z, h, c, near_x, near_y, 3 - h


def remote(src, dst, send, recv, device):
    return pltpu.make_async_remote_copy(
        src_ref=src, dst_ref=dst, send_sem=send, recv_sem=recv, device_id=device, device_id_type=MESH
    )


def greet(targets):
    barrier = pltpu.get_barrier_semaphore()
    for device in targets:
        pl.semaphore_signal(barrier, inc=1, device_id=device, device_id_type=MESH)


def meet(targets):
    pl.semaphore_wait(pltpu.get_barrier_semaphore(), len(targets))


class Gather:
    SEMS = 8

    def __init__(self, own, slots, rows, sems):
        self.own, self.slots, self.sems = own, slots, sems
        self.half = round_up(rows // 2, 8)
        self.rows = rows

    def copies(self, i):
        _, h, _, near_x, near_y, _ = place()
        slots, sems = self.slots, self.sems
        first, second = pl.ds(0, self.half), pl.ds(self.half, self.rows - self.half)
        every = pl.ds(0, self.rows)

        def one(src, dst, place_in, device):
            return remote(src, dst, sems.at[i, place_in], sems.at[i, 4 + place_in], {"head": device})

        own = self.own(i)
        return (
            one(own.at[every], slots.at[i, every, lanes(h)], 0, near_x),
            one(own.at[every], slots.at[i, every, lanes(h)], 1, near_y),
            one(slots.at[i, first, lanes(near_x)], slots.at[i, first, lanes(near_x)], 2, near_y),
            one(slots.at[i, second, lanes(near_y)], slots.at[i, second, lanes(near_y)], 3, near_x),
        )

    def arrivals(self, i):
        _, h, _, near_x, near_y, far = place()
        slots, sems = self.slots, self.sems
        first, second = pl.ds(0, self.half), pl.ds(self.half, self.rows - self.half)
        every = pl.ds(0, self.rows)

        def one(dst, place_in, device):
            return remote(dst, dst, sems.at[i, place_in], sems.at[i, 4 + place_in], {"head": device})

        return (
            one(slots.at[i, every, lanes(near_x)], 0, near_x),
            one(slots.at[i, every, lanes(near_y)], 1, near_y),
            one(slots.at[i, first, lanes(far)], 2, near_y),
            one(slots.at[i, second, lanes(far)], 3, near_x),
        )

    def direct(self, i):
        x, y, _, _ = self.copies(i)
        x.start()
        y.start()

    def forward(self, i):
        x, y, _, _ = self.arrivals(i)
        x.wait_recv()
        y.wait_recv()
        _, _, to_y, to_x = self.copies(i)
        to_y.start()
        to_x.start()

    def ready(self, i):
        _, _, x, y = self.arrivals(i)
        x.wait_recv()
        y.wait_recv()

    def finish(self, i):
        for copy in self.copies(i):
            copy.wait_send()


def head_masks(rows):
    head = lax.broadcasted_iota(jnp.int32, (rows, LANES), 1) // HEAD_DIM
    return [head == k for k in range(LANES // HEAD_DIM)]


def diagonal_mask():
    rows = lax.broadcasted_iota(jnp.int32, (LANES, LANES), 0) // HEAD_DIM
    cols = lax.broadcasted_iota(jnp.int32, (LANES, LANES), 1) // HEAD_DIM
    return rows == cols


def pick(mask, pair):
    zero = jnp.zeros((), BF)
    return jnp.where(mask, pair[0], zero), jnp.where(mask, pair[1], zero)


def fold(square):
    square = jnp.where(diagonal_mask(), square, 0.0)
    return (
        square[0:HEAD_DIM]
        + square[HEAD_DIM : 2 * HEAD_DIM]
        + square[2 * HEAD_DIM : 3 * HEAD_DIM]
        + square[3 * HEAD_DIM :]
    )


def unfold(wide):
    return jnp.where(diagonal_mask(), jnp.concatenate([wide] * 4, axis=0), 0.0)


def positive(values):
    return jnp.where(values > 0, values + 1.0, jnp.exp(jnp.minimum(values, 0.0)))


def norm_parts(rows):
    row_mean = jnp.mean(rows, axis=-1, keepdims=True)
    centred = rows - row_mean
    row_inv = lax.rsqrt(jnp.mean(centred * centred, axis=-1, keepdims=True) + norm_eps)
    return centred * row_inv, row_inv


def split_rows(source, high, low, rows, step):
    def one(r, _):
        s = pl.ds(pl.multiple_of(r * step, step), step)
        high[s, :], low[s, :] = split(source[s, :])
        return 0

    lax.fori_loop(0, rows // step, one, 0)


STATE = HEAD_DIM + 8


def attend_kernel(
    dims,
    tok_in, attn_in, ffn_in, wqkv_in, wout_in,
    tok_out, gains_out, proj_out, den_out, prior_out, mix_out, wout_out,
    raw, tok, mix, gains, proj, den, prior, state, state_in, wstage, w_h, w_l, n_h, n_l, wout,
    tok_sem, mix_sem, gain_sem, state_sem, out_sem, mate_sem, pair_sem, load_sem, store_sem,
):
    images, length, used, rows = dims
    width = tok.shape[2]
    z, h, c, near_x, near_y, far = place()
    seq = lax.axis_size("seq")
    out_rows = wout_in.shape[0] // 4

    friends = [{"head": near_x}, {"head": near_y}, {"head": far}, {"dp": 1 - c}]
    friends += [{"seq": lax.rem(z + d, seq)} for d in range(1, seq)]
    greet(friends)
    loads = [pltpu.make_async_copy(tok_in.at[i], raw.at[i], load_sem.at[i]) for i in range(images)]
    loads += [
        pltpu.make_async_copy(wqkv_in.at[pl.ds(j * width, width)], wstage.at[:, lanes(j)], load_sem.at[images + j])
        for j in range(3)
    ]
    for copy in loads:
        copy.start()

    gains[:, lanes(h)] = jnp.zeros((8, LANES), F32)
    gains[0:1, lanes(h)] = attn_in[...]
    gains[1:2, lanes(h)] = ffn_in[...]
    blank = jnp.zeros((rows - used, LANES), F32)
    for i in range(images):
        for other in (near_x, near_y, far):
            tok[i, used:rows, lanes(other)] = blank
    for i in range(images):
        loads[i].wait()
        pad_rows(raw, tok, i, h)

    meet(friends)
    tokens = Gather(lambda i: tok.at[i, :, lanes(h)], tok, used, tok_sem)
    mixes = Gather(lambda i: mix.at[i, :, lanes(h)], mix, used, mix_sem)
    tokens.direct(0)
    gain_copies = [
        remote(gains.at[:, lanes(h)], gains.at[:, lanes(h)], gain_sem.at[k], gain_sem.at[3 + k], {"head": other})
        for k, other in enumerate((near_x, near_y, far))
    ]
    for copy in gain_copies:
        copy.start()
    tokens.direct(1)
    for copy in loads[images:]:
        copy.wait()
    split_rows(wstage, w_h, w_l, wstage.shape[0], 64)
    for k, other in enumerate((near_x, near_y, far)):
        remote(
            gains.at[:, lanes(other)], gains.at[:, lanes(other)], gain_sem.at[k], gain_sem.at[3 + k],
            {"head": other},
        ).wait_recv()
    row_ok = lax.broadcasted_iota(jnp.int32, (rows, LANES), 0) < length

    def project(i):

        for s in row_blocks(rows):
            n_h[s, :], n_l[s, :] = split(norm_parts(tok[i, s, :])[0] * gains[0:1, :])
        proj[i] = dot3((n_h[...], n_l[...]), (w_h[...], w_l[...]), "nn")
        key_feat = jnp.where(row_ok, positive(proj[i, :, lanes(1)]), 0.0)
        state[i, 0:HEAD_DIM, :] = fold(dot3(split(key_feat), split(proj[i, :, lanes(2)]), "tn"))
        state[i, HEAD_DIM:, :] = jnp.broadcast_to(
            jnp.sum(key_feat, axis=0, keepdims=True), (STATE - HEAD_DIM, LANES)
        )
        for d in range(1, seq):

            @pl.when(z + d < seq)
            def _():
                state_copy(i, d, d).start()

    def state_copy(i, d, step):
        return remote(
            state.at[i], state_in.at[d - 1, i], state_sem.at[0, d - 1, i], state_sem.at[1, d - 1, i],
            {"seq": lax.rem(z + step + seq, seq)},
        )

    def attend(i):
        prior[i] = jnp.zeros((STATE, LANES), F32)
        for d in range(1, seq):

            @pl.when(z >= d)
            def _():
                state_copy(i, d, -d).wait_recv()
                prior[i] = prior[i] + state_in[d - 1, i]

        query_feat = positive(proj[i, :, lanes(0)])
        key_feat = jnp.where(row_ok, positive(proj[i, :, lanes(1)]), 0.0)
        query_pair, key_pair = split(query_feat), split(key_feat)
        value_pair = split(proj[i, :, lanes(2)])
        total = prior[i, HEAD_DIM : HEAD_DIM + 1, :]
        ones = jnp.where(diagonal_mask(), 1.0, 0.0).astype(BF)
        num = dot3(query_pair, split(unfold(prior[i, 0:HEAD_DIM, :])), "nn")
        below = dot2(split(query_feat * total), ones, "nn")
        row = lax.broadcasted_iota(jnp.int32, (rows, rows), 0)
        col = lax.broadcasted_iota(jnp.int32, (rows, rows), 1)
        for mask in head_masks(rows):
            scores = dot3(query_pair, pick(mask, key_pair), "nt")
            score_pair = split(jnp.where(col <= row, scores, 0.0))
            num = num + dot3(score_pair, pick(mask, value_pair), "nn")
            below = below + dot2(score_pair, jnp.where(mask, 1.0, 0.0).astype(BF), "nn")
        den[i] = below
        mix[i, :, lanes(h)] = jnp.where(row_ok, num / below, 0.0)
        blank_rows = jnp.zeros((rows - used, LANES), F32)
        for other in (near_x, near_y, far):
            mix[i, used:rows, lanes(other)] = blank_rows

    mate = z + 1 - 2 * lax.rem(z, 2)

    def quarter(plane, core):
        return pl.ds(pl.multiple_of((2 * lax.rem(plane, 2) + core) * out_rows, out_rows), out_rows)

    own_rows = quarter(z, c)
    out_copies = [
        remote(
            wout_in.at[own_rows], wout.at[h, own_rows], out_sem.at[0, k], out_sem.at[1, k], {"head": other}
        )
        for k, other in enumerate((near_x, near_y, far))
    ]
    out_own = pltpu.make_async_copy(wout_in, wout.at[h], load_sem.at[images + 4])

    def out_arrival(k, other):
        return remote(
            wout.at[other, own_rows], wout.at[other, own_rows], out_sem.at[0, k], out_sem.at[1, k],
            {"head": other},
        )

    def mate_copy(k, other, plane):
        part = wout.at[other, quarter(plane, c)]
        return remote(part, part, mate_sem.at[0, k], mate_sem.at[1, k], {"seq": mate})

    def pair_copy(k, other, plane, core, late):
        part = wout.at[other, quarter(plane, core)]
        return remote(part, part, pair_sem.at[0, late, k], pair_sem.at[1, late, k], {"dp": 1 - c})

    peers = tuple(enumerate((near_x, near_y, far)))
    stores = []

    def store(src, dst):
        copy = pltpu.make_async_copy(src, dst, store_sem.at[len(stores)])
        copy.start()
        stores.append(copy)

    for t in range(images + 2):
        if t < images:
            tokens.forward(t)
            if t + 2 < images:
                tokens.direct(t + 2)
            elif t == images - 1:
                for copy in out_copies:
                    copy.start()
                out_own.start()
        if 1 <= t <= images:
            tokens.ready(t - 1)
            project(t - 1)
            store(tok.at[t - 1], tok_out.at[t - 1])
            store(proj.at[t - 1], proj_out.at[t - 1])
        if t == images + 1:
            for k, other in peers:
                out_arrival(k, other).wait_recv()
                mate_copy(k, other, z).start()
                pair_copy(k, other, z, c, 0).start()
        if t >= 2:
            attend(t - 2)
            mixes.direct(t - 2)
            store(den.at[t - 2], den_out.at[t - 2])
            store(prior.at[t - 2], prior_out.at[t - 2])
    store(gains, gains_out)
    out_own.wait()
    for i in range(images - 1):
        mixes.forward(i)
    for k, other in peers:
        mate_copy(k, other, mate).wait_recv()
        pair_copy(k, other, mate, c, 1).start()
    mixes.forward(images - 1)
    for k, other in peers:
        pair_copy(k, other, z, 1 - c, 0).wait_recv()
        pair_copy(k, other, mate, 1 - c, 1).wait_recv()
    store(wout, wout_out)
    for i in range(images):
        mixes.ready(i)
        store(mix.at[i], mix_out.at[i])
    for i in range(images):
        tokens.finish(i)
        mixes.finish(i)
        for d in range(1, seq):

            @pl.when(z + d < seq)
            def _(i=i, d=d):
                state_copy(i, d, d).wait_send()

    for copy in gain_copies + out_copies:
        copy.wait_send()
    for k, other in peers:
        mate_copy(k, other, z).wait_send()
        pair_copy(k, other, z, c, 0).wait_send()
        pair_copy(k, other, mate, c, 1).wait_send()
    for copy in stores:
        copy.wait()


def attend_call(tokens, gain_attn, gain_ffn, wqkv, wout):
    images, length, _ = tokens.shape
    used = round_up(length, 8)
    rows = padded(length)
    width = wqkv.shape[0] // 3
    heads_n = width // LANES
    dma = pltpu.SemaphoreType.DMA
    seq = lax.axis_size("seq")
    any_spec = pl.BlockSpec(memory_space=pl.ANY)
    vmem_spec = pl.BlockSpec(memory_space=pltpu.VMEM)
    shape = lambda *s: jax.ShapeDtypeStruct(s, F32)
    return pl.pallas_call(
        functools.partial(attend_kernel, (images, length, used, rows)),
        out_shape=(
            shape(images, rows, width),
            shape(8, width),
            shape(images, rows, 3 * LANES),
            shape(images, rows, LANES),
            shape(images, STATE, LANES),
            shape(images, rows, width),
            shape(heads_n, LANES, width),
        ),
        in_specs=[any_spec, vmem_spec, vmem_spec, any_spec, any_spec],
        out_specs=(any_spec,) * 7,
        scratch_shapes=[
            pltpu.VMEM((images, length, LANES), F32),
            pltpu.VMEM((images, rows, width), F32),
            pltpu.VMEM((images, rows, width), F32),
            pltpu.VMEM((8, width), F32),
            pltpu.VMEM((images, rows, 3 * LANES), F32),
            pltpu.VMEM((images, rows, LANES), F32),
            pltpu.VMEM((images, STATE, LANES), F32),
            pltpu.VMEM((images, STATE, LANES), F32),
            pltpu.VMEM((seq - 1, images, STATE, LANES), F32),
            pltpu.VMEM((width, 3 * LANES), F32),
            pltpu.VMEM((width, 3 * LANES), BF),
            pltpu.VMEM((width, 3 * LANES), BF),
            pltpu.VMEM((rows, width), BF),
            pltpu.VMEM((rows, width), BF),
            pltpu.VMEM((heads_n, LANES, width), F32),
            dma((images, Gather.SEMS)),
            dma((images, Gather.SEMS)),
            dma((6,)),
            dma((2, seq - 1, images)),
            dma((2, 3)),
            dma((2, 3)),
            dma((2, 2, 3)),
            dma((images + 5,)),
            dma((5 * images + 4,)),
        ],
        compiler_params=pltpu.CompilerParams(
            collective_id=0, has_side_effects=True, vmem_limit_bytes=VMEM_BYTES
        ),
    )(tokens, gain_attn, gain_ffn, wqkv, wout)


VMEM_BYTES = 60 * 1024 * 1024
class Scatter:
    SEMS = 12

    def __init__(self, part, buffers, rows, sems):
        self.part, self.buffers, self.sems = part, buffers, sems
        self.half = round_up(rows // 2, 8)
        self.rows = rows
        self.first, self.second = pl.ds(0, self.half), pl.ds(self.half, rows - self.half)
        self.left = pl.ds(0, rows - self.half)

    def slot(self, i, k):
        rows = self.first if k in (0, 2, 5) else self.left
        return self.buffers.at[i, k, rows]

    def copy(self, i, k, src, into=None):
        _, _, _, near_x, near_y, _ = place()
        into = k if into is None else into
        device = near_x if into in (0, 2, 4) else near_y
        return remote(
            src, self.slot(i, into), self.sems.at[i, into], self.sems.at[i, 6 + into], {"head": device}
        )

    def sent(self, i):
        _, _, _, near_x, near_y, far = place()
        part = self.part(i)
        return (
            self.copy(i, 2, part.at[self.first, lanes(far)]),
            self.copy(i, 3, part.at[self.second, lanes(far)]),
            self.copy(i, 0, part.at[self.first, lanes(near_x)]),
            self.copy(i, 1, part.at[self.second, lanes(near_y)]),
        )

    def passed(self, i):
        return (
            self.copy(i, 2, self.slot(i, 2), 5),
            self.copy(i, 3, self.slot(i, 3), 4),
        )

    def direct(self, i):
        for copy in self.sent(i):
            copy.start()

    def relay(self, i):
        _, _, _, near_x, near_y, _ = place()
        part = self.part(i)
        to_y, to_x = self.passed(i)
        self.copy(i, 2, self.slot(i, 2)).wait_recv()
        self.buffers[i, 2, self.first] = self.buffers[i, 2, self.first] + part[self.first, lanes(near_y)]
        to_y.start()
        self.copy(i, 3, self.slot(i, 3)).wait_recv()
        self.buffers[i, 3, self.left] = self.buffers[i, 3, self.left] + part[self.second, lanes(near_x)]
        to_x.start()

    def total(self, i):
        _, h, _, _, _, _ = place()
        part = self.part(i)
        for k in (0, 5, 1, 4):
            self.copy(i, k, self.slot(i, k)).wait_recv()
        first = (
            part[self.first, lanes(h)] + self.buffers[i, 0, self.first] + self.buffers[i, 5, self.first]
        )
        second = part[self.second, lanes(h)] + self.buffers[i, 1, self.left] + self.buffers[i, 4, self.left]
        return jnp.concatenate([first, second], axis=0)

    def finish(self, i):
        for copy in self.sent(i) + self.passed(i):
            copy.wait_send()


def activation(values):
    scale = 0.7978845608028654
    square = values * values
    bent = jnp.tanh(scale * values * (1.0 + 0.044715 * square))
    half = 0.5 * (1.0 + bent)
    slope = half + 0.5 * values * (1.0 - bent * bent) * (scale * (1.0 + 0.134145 * square))
    return values * half, slope


def to_lanes(first, second, rows):
    lane = lax.broadcasted_iota(jnp.int32, (rows, 128), 1)
    both = jnp.where(lane == 0, first, jnp.where(lane == 1, second, 0.0))
    both = jnp.concatenate([both, jnp.zeros((LANES - rows, 128), F32)], axis=0)
    return jnp.transpose(both)[0:8]


def to_columns(block, rows):
    tall = jnp.concatenate([block, jnp.zeros((120, LANES), F32)], axis=0)
    turned = jnp.transpose(tall)[0:rows]
    return turned[:, 0:1], turned[:, 1:2]


class Reduce:
    SEMS = 4
    RING_SEMS = 7
    RING = 12
    LATE = (12, 9, 6, 3, 0)

    def __init__(self, sems, ring_sems):
        self.sems, self.ring_sems, self.total = sems, ring_sems, sems.shape[0]
        self.chunks = []
        self.clock = 0
        self.ready = 0

    def chunk(self, mine, theirs, got, result, result_other, room):
        self.chunks.append(
            dict(mine=mine, theirs=theirs, got=got, result=result, result_other=result_other, slot=room)
        )

    def add(self, partial, arrived, result, rows, ring, columns):
        c = lax.axis_index("dp")
        half = partial.shape[0] // 2
        for j in columns:
            for r in range(half // rows):
                here = pl.ds(pl.multiple_of(c * half + r * rows, 8), rows)
                there = pl.ds(pl.multiple_of((1 - c) * half + r * rows, 8), rows)
                self.chunk(
                    partial.at[here, lanes(j)], partial.at[there, lanes(j)],
                    arrived.at[pl.ds(r * rows, rows), lanes(j)], result.at[here, lanes(j)], result.at[there, lanes(j)],
                    ring.at[len(self.chunks) % self.RING, :, pl.ds(0, rows)],
                )
        return len(self.chunks)

    def add_columns(self, partial, arrived, result, rows, ring):
        c = lax.axis_index("dp")
        depth = partial.shape[0]
        half = depth // 2
        blocks = partial.shape[1] // LANES
        for j in range(blocks):
            rows = rows // 2 if j == blocks - 1 else rows
            for r in range(half // rows):
                here = pl.multiple_of(c * half + r * rows, 8)
                there = pl.multiple_of((1 - c) * half + r * rows, 8)
                self.chunk(
                    partial.at[pl.ds(here, rows), lanes(j)], partial.at[pl.ds(there, rows), lanes(j)],
                    arrived.at[pl.ds(j * half + r * rows, rows)],
                    result.at[pl.ds(j * depth + here, rows)], result.at[pl.ds(j * depth + there, rows)],
                    ring.at[len(self.chunks) % self.RING, :, pl.ds(0, rows)],
                )
        return len(self.chunks)

    def side(self, k):
        z = lax.axis_index("seq")
        return z if k % 2 == 0 else 3 - z

    def device(self, k, y):
        return {"seq": y if k % 2 == 0 else 3 - y}

    def sem(self, k, n):
        return self.sems.at[k, n] if n < self.SEMS else self.ring_sems.at[k % self.RING, n - self.SEMS]

    def pair(self, k):
        chunk = self.chunks[k]
        c = lax.axis_index("dp")
        return remote(chunk["theirs"], chunk["got"], self.sem(k, 0), self.sem(k, 1), {"dp": 1 - c})

    def partial(self, k, into, y):
        chunk = self.chunks[k]
        return remote(
            chunk["mine"], chunk["slot"].at[into], self.sem(k, 4), self.sem(k, 5 + into), self.device(k, y)
        )

    def outcome(self, k, src, y, send):
        return remote(src, self.chunks[k]["result"], self.sem(k, send), self.sem(k, 7), self.device(k, y))

    def twin(self, k, src):
        c = lax.axis_index("dp")
        return remote(src, self.chunks[k]["result"], self.sem(k, 2), self.sem(k, 3), {"dp": 1 - c})

    def kept(self, k):
        chunk = self.chunks[k]
        return pltpu.make_async_copy(chunk["mine"], chunk["result"], self.sem(k, 10))

    def exchange(self, first, end):
        for k in range(first, end):
            self.pair(k).start()
        self.ready = end

    def combine(self, k):
        chunk, y = self.chunks[k], self.side(k)
        self.pair(k).wait_recv()
        chunk["mine"][...] = chunk["mine"][...] + chunk["got"][...]

        @pl.when(y == 0)
        def _():
            self.partial(k, 0, 1).start()

        @pl.when(y == 3)
        def _():
            self.partial(k, 0, 2).start()

    def middle(self, k):
        chunk, y = self.chunks[k], self.side(k)

        @pl.when(y == 2)
        def _():
            self.partial(k, 0, 3).wait_recv()
            chunk["mine"][...] = chunk["mine"][...] + chunk["slot"][0]
            self.partial(k, 1, 1).start()

    def root(self, k):
        chunk, y = self.chunks[k], self.side(k)

        @pl.when(y == 1)
        def _():
            self.partial(k, 0, 0).wait_recv()
            self.partial(k, 1, 2).wait_recv()
            chunk["mine"][...] = chunk["mine"][...] + chunk["slot"][0] + chunk["slot"][1]
            self.outcome(k, chunk["mine"], 2, 8).start()
            self.outcome(k, chunk["mine"], 0, 9).start()
            self.kept(k).start()
            self.twin(k, chunk["mine"]).start()

    def onward(self, k):
        chunk, y = self.chunks[k], self.side(k)

        @pl.when(y == 2)
        def _():
            self.outcome(k, chunk["result"], 1, 8).wait_recv()
            self.outcome(k, chunk["result"], 3, 8).start()
            self.twin(k, chunk["result"]).start()

    def leaf(self, k):
        chunk, y = self.chunks[k], self.side(k)

        @pl.when(y == 0)
        def _():
            self.outcome(k, chunk["result"], 1, 8).wait_recv()
            self.twin(k, chunk["result"]).start()

        @pl.when(y == 3)
        def _():
            self.outcome(k, chunk["result"], 2, 8).wait_recv()
            self.twin(k, chunk["result"]).start()

    def settle(self, k):
        chunk, y = self.chunks[k], self.side(k)

        @pl.when(y == 0)
        def _():
            self.partial(k, 0, 1).wait_send()

        @pl.when(y == 3)
        def _():
            self.partial(k, 0, 2).wait_send()

        @pl.when(y == 2)
        def _():
            self.partial(k, 1, 1).wait_send()
            self.outcome(k, chunk["result"], 3, 8).wait_send()

        @pl.when(y == 1)
        def _():
            self.outcome(k, chunk["mine"], 2, 8).wait_send()
            self.outcome(k, chunk["mine"], 0, 9).wait_send()
            self.kept(k).wait()

    def finish(self, k):
        chunk = self.chunks[k]
        c = lax.axis_index("dp")
        if k + self.RING >= self.total:
            self.settle(k)
        self.pair(k).wait_send()
        remote(
            chunk["result_other"], chunk["result_other"], self.sem(k, 2), self.sem(k, 3), {"dp": 1 - c}
        ).wait_recv()
        self.twin(k, chunk["result"]).wait_send()

    def tick(self, times=1):
        for _ in range(times):
            self.step()

    def step(self):
        if self.clock >= self.ready and self.ready < self.total:
            return
        stages = (self.leaf, self.onward, self.root, self.middle, self.combine)
        for late, act in zip(self.LATE, stages):
            chunk = self.clock - late
            if late == 0 and self.RING <= chunk < self.total:
                self.settle(chunk - self.RING)
            if 0 <= chunk < self.total:
                act(chunk)
        self.clock += 1

    def drain(self):
        while self.clock < self.total + self.LATE[0]:
            self.step()


CHUNK = 128
ROW_TILE = 16


def row_sums(total, value):
    return total + jnp.sum(value, axis=-1, keepdims=True)


def layer_kernel(
    dims,
    tok_in, mix_in, gains_in, wfull_in, up_in, bias, down_in, down_bias, grad_in,
    proj_in, den_in, prior_in, wout_in, wqkv_in,
    out_out, tok_grad_out, qkv_out, out_w_out, up_out, down_out, small_out,
    gains, grad, resid_grad, part_ffn, part, buf_norm, buf_tok, xhat_own, inv_own,
    d_down, d_up, d_small, got_ffn, got_out, got_qkv, got_small, state, state_in, ring, slope, proj, prior, turned_h, turned_l, d_out,
    grad_sem, norm_sem, back_sem, ffn_sem, tok_sem, state_sem, chunk_sem, ring_sem, load_sem, stage_sem, image_sem, store_sem,
):
    images, length, used, rows = dims
    width = grad.shape[2]
    hidden = up_in.shape[1]
    z, h, c, near_x, near_y, far = place()
    seq = lax.axis_size("seq")
    vmem = pltpu.VMEM
    tiles = width // LANES
    row_ok = lax.broadcasted_iota(jnp.int32, (rows, LANES), 0) < length

    small = (pltpu.make_async_copy(gains_in, gains, load_sem.at[0]),)

    grads = Gather(lambda i: grad.at[i, :, lanes(h)], grad, used, grad_sem)
    norm = Scatter(lambda i: part.at[i % 2], buf_norm, rows, norm_sem)
    back = Gather(lambda i: resid_grad.at[i, :, lanes(h)], resid_grad, used, back_sem)
    ffn = Scatter(lambda i: part_ffn.at[i], buf_norm, used, ffn_sem)
    toks = Scatter(lambda i: part.at[i % 2], buf_tok, rows, tok_sem)
    reduce = Reduce(chunk_sem, ring_sem)
    tick = reduce.tick
    stores = []

    def store(src, dst):
        copy = pltpu.make_async_copy(src, dst, store_sem.at[len(stores)])
        copy.start()
        stores.append(copy)

    def halves(source, high, low):
        split_rows(source, high, low, rows, ROW_TILE)

    def stats(i, weight, sums_with):
        first, second = [], []
        for s in row_blocks(rows):
            term = part[i % 2, s, :]
            first.append(jnp.sum(term * gains[weight, :], axis=-1, keepdims=True))
            second.append(jnp.sum(term * sums_with(s), axis=-1, keepdims=True))
        block = to_lanes(jnp.concatenate(first, axis=0), jnp.concatenate(second, axis=0), rows)
        for k in range(tiles):
            part[i % 2, rows - 8 : rows, lanes(k)] = block

    def norm_share(scatter, i, weight, hat, inv):
        both = scatter.total(i)
        mean, cross = to_columns(both[rows - 8 : rows], rows)
        own = jnp.where(row_ok, both, 0.0)
        scaled = own * gains[weight, lanes(h)]
        share = (scaled - mean * (1.0 / width) - hat * (cross * (1.0 / width))) * inv
        return share, own

    def resid_back(i):
        share, own = norm_share(norm, i, slice(1, 2), xhat_own[i], inv_own[i, :, 0:1])
        resid_grad[i, :, lanes(h)] = jnp.where(row_ok, grad[i, :, lanes(h)] + share, 0.0)
        for k, value in ((1, own * xhat_own[i]), (2, grad[i, :, lanes(h)])):
            d_small[8:9, lanes(k)] = d_small[8:9, lanes(k)] + jnp.sum(value, axis=0, keepdims=True)
        norm.finish(i)
        back.direct(i)
        grads.finish(i)
        for copy in image_copies(i):
            copy.start()

    dden_at, den_at, mixed_at, dnum_at = lanes(0), lanes(1), lanes(2), lanes(3)

    def image_copies(i):
        return (
            pltpu.make_async_copy(mix_in.at[i, :, lanes(h)], grad.at[i, :, mixed_at], load_sem.at[8 + 4 * i]),
            pltpu.make_async_copy(den_in.at[i], grad.at[i, :, den_at], load_sem.at[9 + 4 * i]),
        )

    def proj_copies(i):
        return (
            pltpu.make_async_copy(proj_in.at[i], proj.at[i], load_sem.at[10 + 4 * i]),
            pltpu.make_async_copy(prior_in.at[i], prior.at[i], load_sem.at[11 + 4 * i]),
        )

    def state_copy(i, step):
        return remote(
            state.at[i], state_in.at[i], state_sem.at[0, i], state_sem.at[1, i],
            {"seq": lax.rem(z + step + seq, seq)},
        )

    def hop(i, step):
        @pl.when(z == seq - 1 - step)
        def _():
            state_copy(i, 1).wait_recv()
            if step < seq - 1:
                state[i] = state[i] + state_in[i]
                state_copy(i, -1).start()

    def first_half(i, rg_h, rg_l):
        back.ready(i)
        for copy in image_copies(i):
            copy.wait()
        halves(resid_grad.at[i], rg_h, rg_l)
        dm = dot3((rg_h[...], rg_l[...]), (turned_h[...], turned_l[...]), "nn")
        ones = jnp.where(diagonal_mask(), 1.0, 0.0).astype(BF)
        inverse = 1.0 / grad[i, :, den_at]
        slope[i, :, dnum_at] = dm * inverse
        grad[i, :, dden_at] = -dot2(split(dm * grad[i, :, mixed_at]), ones, "nn") * inverse
        query_feat = positive(proj[i, :, lanes(0)])
        state[i, 0:HEAD_DIM, :] = fold(dot3(split(query_feat), split(slope[i, :, dnum_at]), "tn"))
        state[i, HEAD_DIM:, :] = jnp.broadcast_to(
            jnp.sum(query_feat * grad[i, :, dden_at], axis=0, keepdims=True), (STATE - HEAD_DIM, LANES)
        )
        @pl.when(z == seq - 1)
        def _():
            state_in[i] = jnp.zeros((STATE, LANES), F32)
            state_copy(i, -1).start()

        term = dot3(split(grad[i, :, mixed_at]), (rg_h[...], rg_l[...]), "tn")
        d_out[...] = term if i == 0 else d_out[...] + term

    def within(i):
        query_feat = positive(proj[i, :, lanes(0)])
        key_feat = jnp.where(row_ok, positive(proj[i, :, lanes(1)]), 0.0)
        query_pair, key_pair, value_pair = split(query_feat), split(key_feat), split(proj[i, :, lanes(2)])
        dden_i = grad[i, :, dden_at]
        dnum_pair = split(slope[i, :, dnum_at])
        prior_pair = split(unfold(prior[i, 0:HEAD_DIM, :]))
        fq = dot3(dnum_pair, prior_pair, "nt") + dden_i * prior[i, HEAD_DIM : HEAD_DIM + 1, :]
        fk = jnp.zeros((rows, LANES), F32)
        fv = jnp.zeros((rows, LANES), F32)
        row = lax.broadcasted_iota(jnp.int32, (rows, rows), 0)
        col = lax.broadcasted_iota(jnp.int32, (rows, rows), 1)
        causal = col <= row
        for k, mask in enumerate(head_masks(rows)):
            key_h, query_h = pick(mask, key_pair), pick(mask, query_pair)
            scores = split(jnp.where(causal, dot3(query_pair, key_h, "nt"), 0.0))
            pull = dot3(dnum_pair, pick(mask, value_pair), "nt")
            pull = pull + dden_i[:, k * HEAD_DIM : k * HEAD_DIM + 1]
            pull = split(jnp.where(causal, pull, 0.0))
            fq = fq + dot3(pull, key_h, "nn")
            fk = fk + dot3(pull, query_h, "tn")
            fv = fv + dot3(scores, pick(mask, dnum_pair), "tn")
        slope[i, :, lanes(0)] = fq
        slope[i, :, lanes(1)] = fk
        slope[i, :, lanes(2)] = fv

    def load_phase(raw):
        copies = [pltpu.make_async_copy(grad_in.at[i], raw.at[i], load_sem.at[3 + i]) for i in range(images)]
        for copy in copies + list(small):
            copy.start()
        start_loads()
        blank = jnp.zeros((rows - used, LANES), F32)
        for i in range(images):
            for other in (near_x, near_y, far):
                grad[i, used:rows, lanes(other)] = blank
                resid_grad[i, used:rows, lanes(other)] = blank
        d_small[...] = jnp.zeros_like(d_small)
        for i in range(images):
            copies[i].wait()
            pad_rows(raw, grad, i, h)

    def ffn_phase(
        wo_h, wo_l, up_h, up_l, pair_h, pair_l, n_h, n_l, hid_h, hid_l, ug_h, ug_l
    ):
        rooms = ((d_down, wo_h, wo_l), (d_up, up_h, up_l))

        def take(k):
            room, high, low = rooms[k]
            weight_loads[k].wait()
            split_rows(room, high, low, room.shape[0], 64)

        def turned(source, target):
            def one(k, _):
                s = lanes(k)
                target[:, s] = source[s, :].T
                return 0

            lax.fori_loop(0, tiles, one, 0)

        tok_copy, mix_copy = image_loads

        def forward(i):
            mix_copy(i).wait()
            halves(part.at[1], pair_h, pair_l)
            if i + 1 < images:
                mix_copy(i + 1).start()
            if i == 0:
                take(0)
            tok_copy(i).wait()
            part[0] = part[0] + dot3((pair_h[...], pair_l[...]), (wo_h[...], wo_l[...]), "nn")
            part_ffn[i, :, lanes(h)] = part[0, :, lanes(h)]
            grads.forward(i)
            if i + 2 < images:
                grads.direct(i + 2)

            for s in row_blocks(rows):
                hat, inv = norm_parts(part[0, s, :])
                part[0, s, :] = hat
                inv_own[i, s, :] = jnp.broadcast_to(inv, (ROW_TILE, 128))
                n_h[i, s, :], n_l[i, s, :] = split(hat * gains[1:2, :])
            xhat_own[i] = part[0, :, lanes(h)]
            if i + 1 < images:
                tok_copy(i + 1).start()
            if i == 0:
                take(1)
                weight_loads[2].start()
            slope[i] = dot3((n_h[i], n_l[i]), (up_h[...], up_l[...]), "nn") + bias[0:1, :]
            for s in row_blocks(rows):
                act, by = activation(slope[i, s, :])
                hid_h[i, s, :], hid_l[i, s, :] = split(act)
                slope[i, s, :] = by
            grads.ready(i)
            halves(grad.at[i], pair_h, pair_l)

            term = dot3((hid_h[i], hid_l[i]), (pair_h[...], pair_l[...]), "tn")
            d_down[...] = term if i == 0 else d_down[...] + term

        def hidden_back(i):
            halves(grad.at[i], pair_h, pair_l)

            part[i % 2] = dot3((pair_h[...], pair_l[...]), (up_h[...], up_l[...]), "nn")
            total = jnp.zeros((1, hidden), F32)
            for s in row_blocks(rows):
                ug = part[i % 2, s, :] * slope[i, s, :]
                ug_h[s, :], ug_l[s, :] = split(ug)
                total = total + jnp.sum(ug, axis=0, keepdims=True)
            d_small[0:1, :] = d_small[0:1, :] + total

        def up_grad(i):
            term = dot3((n_h[i], n_l[i]), (ug_h[...], ug_l[...]), "tn")
            d_up[...] = term if i == 0 else d_up[...] + term

        def norm_back(i):
            part[i % 2] = dot3((ug_h[...], ug_l[...]), (wo_h[...], wo_l[...]), "nn")
            stats(i, slice(1, 2), lambda s: n_h[i, s, :].astype(F32) + n_l[i, s, :].astype(F32))
            norm.direct(i)

        def down(i):
            resid = part_ffn[i, :, lanes(h)]

            part_ffn[i] = dot3((hid_h[i], hid_l[i]), (up_h[...], up_l[...]), "nt")
            part_ffn[i, :, lanes(h)] = part_ffn[i, :, lanes(h)] + resid

        for copy in small:
            copy.wait()
        for i in range(images):
            forward(i)
        reduce.exchange(0, down_chunks)
        turned(up_h, wo_h)
        turned(up_l, wo_l)
        tick()
        weight_loads[2].wait()

        def turn_down(k, _):
            s = lanes(k)
            up_h[:, s], up_l[:, s] = split(d_up[s, :].T)
            return 0

        lax.fori_loop(0, hidden // LANES, turn_down, 0)
        out_load.wait()
        for k in range(tiles):
            turned_h[lanes(k), :], turned_l[lanes(k), :] = split(d_out[:, lanes(k)].T)
        last = images - 1
        for i in range(images):
            hidden_back(i)
            tick()
            up_grad(i)
            if i == last:
                reduce.exchange(down_chunks, up_chunks)
            tick()
            if i >= 1:
                norm.relay(i - 1)
            norm_back(i)
            tick()
            if i >= 2:
                back.forward(i - 2)
                tick()
            if i >= 1:
                resid_back(i - 1)
                tick()
        for i in range(images):
            for copy in proj_copies(i):
                copy.wait()
        first_half(0, pair_h, pair_l)
        tick()
        norm.relay(last)
        back.forward(last - 1)
        down(0)
        tick()
        within(0)
        tick()
        resid_back(last)
        first_half(1, pair_h, pair_l)
        tick()
        hop(0, 1)
        down(1)
        tick()
        back.forward(last)
        within(1)
        tick()
        first_half(2, pair_h, pair_l)
        tick()
        hop(0, 2)
        hop(1, 1)
        down(2)
        tick()
        within(2)
        tick()
        hop(2, 1)
        down(3)
        tick()
        hop(0, 3)
        hop(1, 2)
        first_half(3, pair_h, pair_l)
        reduce.exchange(up_chunks, out_chunks)
        ffn.direct(0)
        ffn.direct(1)
        tick()
        hop(2, 2)
        within(3)
        tick()
        hop(1, 3)
        hop(3, 1)

    def attend_phase(
        wq_h, wq_l, tok, n_h, n_l, xhat, pg_h, pg_l, hat_own, root_own, d_qkv, out_trim, tok_trim,
    ):
        def tok_copy(i):
            return pltpu.make_async_copy(tok_in.at[i], tok.at[i % 2], image_sem.at[i % 2])

        weights = [
            pltpu.make_async_copy(wqkv_in.at[pl.ds(j * width, width)], d_qkv.at[:, lanes(j)], load_sem.at[1 + j])
            for j in range(3)
        ]
        for copy in weights:
            copy.start()
        tok_copy(0).start()
        tok_copy(1).start()
        qkv_chunks = reduce.add_columns(d_qkv, got_qkv, qkv_out, CHUNK, ring)
        all_chunks = reduce.add(d_small, got_small, small_out, 8, ring, range(1))

        def across(i):
            later_pair = split(unfold(state_in[i, 0:HEAD_DIM, :]))
            query, key, value = (proj[i, :, lanes(k)] for k in range(3))
            key_pair = split(jnp.where(row_ok, positive(key), 0.0))
            fk = slope[i, :, lanes(1)] + dot3(split(value), later_pair, "nt")
            fk = fk + state_in[i, HEAD_DIM : HEAD_DIM + 1, :]
            fv = slope[i, :, lanes(2)] + dot3(key_pair, later_pair, "nn")
            bend = lambda v: jnp.where(v > 0, 1.0, jnp.exp(jnp.minimum(v, 0.0)))
            pg_h[i, :, lanes(0)], pg_l[i, :, lanes(0)] = split(slope[i, :, lanes(0)] * bend(query))
            pg_h[i, :, lanes(1)], pg_l[i, :, lanes(1)] = split(jnp.where(row_ok, fk * bend(key), 0.0))
            pg_h[i, :, lanes(2)], pg_l[i, :, lanes(2)] = split(fv)

        def weight_grads(i):
            tok_copy(i).wait()

            for s in row_blocks(rows):
                hat, inv = norm_parts(tok[i % 2, s, :])
                xhat[s, :] = hat
                root_own[i, s, :] = jnp.broadcast_to(inv, (ROW_TILE, 128))
                n_h[i, s, :], n_l[i, s, :] = split(hat * gains[0:1, :])
            hat_own[i] = xhat[:, lanes(h)]
            if i + 2 < images:
                tok_copy(i + 2).start()

            term = dot3((n_h[i], n_l[i]), (pg_h[i], pg_l[i]), "tn")
            d_qkv[...] = term if i == 0 else d_qkv[...] + term

        def norm_back(i):
            if i >= 2:
                toks.finish(i - 2)

            part[i % 2] = dot3((pg_h[i], pg_l[i]), (wq_h[...], wq_l[...]), "nn")
            stats(i, slice(0, 1), lambda s: n_h[i, s, :].astype(F32) + n_l[i, s, :].astype(F32))
            toks.direct(i)

        def token_back(i):
            share, own = norm_share(toks, i, slice(0, 1), hat_own[i], root_own[i, :, 0:1])
            d_small[8:9, lanes(0)] = d_small[8:9, lanes(0)] + jnp.sum(own * hat_own[i], axis=0, keepdims=True)
            tok_trim[i] = (resid_grad[i, :, lanes(h)] + share)[0:length]
            store(tok_trim.at[i], tok_grad_out.at[i])

        def output(i):
            out_trim[i] = (ffn.total(i) + down_bias[0:1, :])[0:length]
            store(out_trim.at[i], out_out.at[i])

        tick()
        tick()
        for copy in weights:
            copy.wait()
        def turn(k, _):
            for j in range(3):
                wq_h[lanes(j), lanes(k)], wq_l[lanes(j), lanes(k)] = split(d_qkv[lanes(k), lanes(j)].T)
            return 0

        lax.fori_loop(0, tiles, turn, 0)
        tick()
        last = images - 1

        across(0)
        weight_grads(0)
        tick()
        hop(2, 3)
        hop(3, 2)
        ffn.relay(0)
        ffn.direct(2)
        across(1)
        weight_grads(1)
        tick()
        ffn.relay(1)
        ffn.direct(3)
        across(2)
        weight_grads(2)
        tick()
        tick()
        hop(3, 3)
        across(3)
        weight_grads(3)
        reduce.exchange(out_chunks, qkv_chunks)
        norm_back(0)
        tick()
        norm_back(1)
        tick()
        ffn.relay(2)
        output(0)
        toks.relay(0)
        tick()
        ffn.relay(3)
        output(1)
        token_back(0)
        norm_back(2)
        tick()
        toks.relay(1)
        tick()
        token_back(1)
        norm_back(3)
        tick()
        output(2)
        toks.relay(2)
        tick()
        output(3)
        token_back(2)
        toks.relay(3)
        tick()
        token_back(3)
        reduce.exchange(qkv_chunks, all_chunks)
        reduce.drain()
        for i in range(images):
            back.finish(i)
            ffn.finish(i)
            if i >= images - 2:
                toks.finish(i)

            @pl.when(z > 0)
            def _(i=i):
                state_copy(i, -1).wait_send()

        for k in range(all_chunks):
            reduce.finish(k)
        for copy in stores:
            copy.wait()

    weight_loads = [
        pltpu.make_async_copy(source, room, stage_sem.at[k])
        for k, (source, room) in enumerate(((wfull_in, d_down), (up_in, d_up), (down_in, d_up)))
    ]
    image_loads = (
        lambda i: pltpu.make_async_copy(tok_in.at[i], part.at[0], image_sem.at[0]),
        lambda i: pltpu.make_async_copy(mix_in.at[i], part.at[1], image_sem.at[1]),
    )
    out_load = pltpu.make_async_copy(wout_in, d_out, load_sem.at[1])

    def start_loads():
        weight_loads[0].start()
        for load in image_loads:
            load(0).start()
        weight_loads[1].start()
        out_load.start()
        for i in range(images):
            for copy in proj_copies(i):
                copy.start()

    friends = [{"head": near_x}, {"head": near_y}, {"dp": 1 - c}]
    friends += [{"seq": lax.rem(z + d, seq)} for d in range(1, seq)]
    greet(friends)
    pl.run_scoped(load_phase, vmem((images, length, LANES), F32))
    meet(friends)
    grads.direct(0)
    grads.direct(1)
    down_chunks = reduce.add(d_down, got_ffn.at[0], down_out, CHUNK, ring, range(tiles))
    up_chunks = reduce.add(d_up, got_ffn.at[1], up_out, CHUNK, ring, range(hidden // LANES))
    reduce.add(d_out, got_out, out_w_out, CHUNK, ring, range(tiles))
    out_chunks = reduce.add(d_small, got_small, small_out, 8, ring, range(1, tiles))
    pair = lambda *s: [vmem(s, BF), vmem(s, BF)]
    pl.run_scoped(
        ffn_phase,
        *pair(width, width), *pair(width, hidden),
        *pair(rows, width), *pair(images, rows, width), *pair(images, rows, hidden), *pair(rows, hidden),
    )
    pl.run_scoped(
        attend_phase,
        *pair(3 * LANES, width), vmem((2, rows, width), F32), *pair(images, rows, width), vmem((rows, width), F32),
        *pair(images, rows, 3 * LANES), vmem((images, rows, LANES), F32), vmem((images, rows, 128), F32),
        vmem((width, 3 * LANES), F32), vmem((images, length, LANES), F32), vmem((images, length, LANES), F32),
    )


def layer_call(tok, mix, gains, wfull, up_weight, up_bias, down_weight, down_bias, grads, proj, den, prior, wout, wqkv):
    images, length, _ = grads.shape
    rows, width = tok.shape[1:]
    hidden = up_weight.shape[1]
    used = round_up(length, 8)
    seq = lax.axis_size("seq")
    any_spec = pl.BlockSpec(memory_space=pl.ANY)
    vmem_spec = pl.BlockSpec(memory_space=pltpu.VMEM)
    shape = lambda *s: jax.ShapeDtypeStruct(s, F32)
    vmem, dma = pltpu.VMEM, pltpu.SemaphoreType.DMA
    half = round_up(rows // 2, 8)
    chunks = (2 * (hidden // 2 // CHUNK) + LANES // 2 // CHUNK + 1) * (width // LANES) + 4 * (width // 2 // CHUNK)
    return pl.pallas_call(
        functools.partial(layer_kernel, (images, length, used, rows)),
        out_shape=(
            shape(images, length, LANES),
            shape(images, length, LANES),
            shape(3 * width, LANES),
            shape(LANES, width),
            shape(width, hidden),
            shape(hidden, width),
            shape(16, width),
        ),
        in_specs=[any_spec] * 5 + [vmem_spec, any_spec, vmem_spec] + [any_spec] * 6,
        out_specs=(any_spec,) * 7,
        scratch_shapes=[
            vmem((8, width), F32),
            vmem((images, rows, width), F32), vmem((images, rows, width), F32), vmem((images, rows, width), F32),
            vmem((2, rows, width), F32), vmem((images, 6, half, LANES), F32), vmem((images, 6, half, LANES), F32),
            vmem((images, rows, LANES), F32), vmem((images, rows, 128), F32),
            vmem((hidden, width), F32), vmem((width, hidden), F32), vmem((16, width), F32),
            vmem((2, hidden // 2, width), F32), vmem((LANES // 2, width), F32), vmem((3 * width // 2, LANES), F32),
            vmem((8, width), F32), vmem((images, STATE, LANES), F32), vmem((images, STATE, LANES), F32),
            vmem((Reduce.RING, 2, CHUNK, LANES), F32),
            vmem((images, rows, hidden), F32), vmem((images, rows, 3 * LANES), F32), vmem((images, STATE, LANES), F32),
            vmem((width, LANES), BF), vmem((width, LANES), BF), vmem((LANES, width), F32),
            dma((images, Gather.SEMS)), dma((images, Scatter.SEMS)), dma((images, Gather.SEMS)),
            dma((images, Scatter.SEMS)), dma((images, Scatter.SEMS)), dma((2, images)),
            dma((chunks, Reduce.SEMS)), dma((Reduce.RING, Reduce.RING_SEMS)), dma((8 + 4 * images,)), dma((3,)), dma((2,)), dma((2 * images,)),
        ],
        compiler_params=pltpu.CompilerParams(
            collective_id=1, has_side_effects=True, vmem_limit_bytes=64 * 1024 * 1024
        ),
    )(tok, mix, gains, wfull, up_weight, up_bias, down_weight, down_bias, grads, proj, den, prior, wout, wqkv)


def fast_device(
    tokens,
    gain_attn,
    qkv_weight,
    out_weight,
    gain_ffn,
    up_weight,
    up_bias,
    down_weight,
    down_bias,
    out_grad,
):
    model_width, kinds, local_width = qkv_weight.shape
    if (tokens.shape[0], local_width, up_weight.shape[1]) != (4, LANES, model_width):
        return per_device(
            tokens, gain_attn, qkv_weight, out_weight, gain_ffn, up_weight, up_bias, down_weight, down_bias, out_grad
        )

    proj_weight = jnp.transpose(qkv_weight, (1, 0, 2)).reshape(kinds * model_width, local_width)
    tok, gains, proj, den, prior, mix, wfull = attend_call(
        tokens, gain_attn[None], gain_ffn[None], proj_weight, out_weight
    )
    output, tok_grad, d_qkv, d_out, d_up, d_down, small = layer_call(
        tok, mix, gains, wfull.reshape(model_width, model_width), up_weight, up_bias[None], down_weight,
        down_bias[None], out_grad, proj, den, prior, out_weight, proj_weight,
    )
    return (
        output,
        tok_grad,
        small[8, 0:LANES],
        jnp.transpose(d_qkv.reshape(kinds, model_width, local_width), (1, 0, 2)),
        d_out,
        small[8, LANES : 2 * LANES],
        d_up,
        small[0],
        d_down,
        small[8, 2 * LANES : 3 * LANES],
    )


def device_function(mesh):
    if (mesh.shape["seq"], mesh.shape["head"], mesh.shape["dp"]) == (4, 4, 2):
        return fast_device
    return per_device


def solution(mesh):
    return jax.shard_map(
        device_function(mesh),
        mesh=mesh,
        in_specs=(
            P("dp", "seq", "head"),
            P("head"),
            P(None, None, "head"),
            P("head", None),
            P("head"),
            P(None, "head"),
            P("head"),
            P("head", None),
            P("head"),
            P("dp", "seq", "head"),
        ),
        out_specs=(
            P("dp", "seq", "head"),
            P("dp", "seq", "head"),
            P("head"),
            P(None, None, "head"),
            P("head", None),
            P("head"),
            P(None, "head"),
            P("head"),
            P("head", None),
            P("head"),
        ),
        check_vma=False,
    )
```

```python
import functools

import jax
import jax.numpy as jnp
from jax import lax
from jax.experimental import pallas as pl
from jax.experimental.pallas import tpu as pltpu
from jax.sharding import PartitionSpec as P

HEAD_DIM = 64


highest = lax.Precision.HIGH
norm_eps = 1e-05


def entering(part, axis, combine, identity, reverse):
    count = lax.axis_size(axis)
    place = lax.axis_index(axis)
    ahead = count - 1 - place if reverse else place
    gathered = jax.tree.map(lambda a: lax.all_gather(a, axis), part)
    state = jax.tree.map(lambda a, e: jnp.zeros_like(a) + jnp.asarray(e, a.dtype), part, identity)

    def one(turn, state):
        source = count - 1 - turn if reverse else turn
        return combine(
            state, jax.tree.map(lambda a: lax.dynamic_index_in_dim(a, source, 0, False), gathered)
        )

    return lax.fori_loop(0, ahead, one, state)


def feature(values_in):
    return jax.nn.elu(values_in) + 1.0


def layer_norm(values_in, gain):
    row_mean = jnp.mean(values_in, axis=-1, keepdims=True)
    centred = values_in - row_mean
    row_var = jnp.mean(centred * centred, axis=-1, keepdims=True)
    return centred * lax.rsqrt(row_var + norm_eps) * gain


def norm_back(partial_grad, rows_full, gain_full, gain_share):
    local_width = gain_share.shape[0]
    model_width = gain_full.shape[0]
    row_mean = jnp.mean(rows_full, axis=-1, keepdims=True)
    centred = rows_full - row_mean
    row_inv = lax.rsqrt(jnp.mean(centred * centred, axis=-1, keepdims=True) + norm_eps)
    scaled = partial_grad * gain_full
    sums = lax.psum(
        jnp.stack(
            [jnp.sum(scaled, axis=-1), jnp.sum(scaled * (centred * row_inv), axis=-1)]
        ),
        "head",
    )
    means = (sums / model_width)[:, :, None]
    share = lax.psum_scatter(partial_grad, "head", scatter_dimension=1, tiled=True)
    start = lax.axis_index("head") * local_width
    xhat = lax.dynamic_slice_in_dim(centred, start, local_width, 1) * row_inv
    back = (share * gain_share - means[0] - xhat * means[1]) * row_inv
    return back, jnp.sum(share * xhat, axis=0)


def mlp_act(values_in):
    return jax.nn.gelu(values_in, approximate=True)


def block_attend(query_proj, key_proj, value_proj, prior_state, prior_total):
    query_feat = feature(query_proj)
    key_feat = feature(key_proj)
    length_now = query_proj.shape[1]
    scores = jnp.einsum("gihe,gjhe->ghij", query_feat, key_feat, precision=highest)
    row_index = lax.broadcasted_iota(jnp.int32, (length_now, length_now), 0)
    col_index = lax.broadcasted_iota(jnp.int32, (length_now, length_now), 1)
    scores = jnp.where(col_index <= row_index, scores, jnp.float32(0.0))
    numerator = jnp.einsum("ghij,gjhe->gihe", scores, value_proj, precision=highest)
    numerator = numerator + jnp.einsum(
        "gihe,ghef->gihf", query_feat, prior_state, precision=highest
    )
    denominator = jnp.sum(scores, axis=-1) + jnp.einsum(
        "gihe,ghe->ghi", query_feat, prior_total, precision=highest
    )
    return numerator / jnp.transpose(denominator, (0, 2, 1))[..., None]


def block_state(key_proj, value_proj):
    key_feat = feature(key_proj)
    kv_sum = jnp.einsum("gihe,gihf->ghef", key_feat, value_proj, precision=highest)
    return (kv_sum, jnp.sum(key_feat, axis=1))


def add_pair(earlier, later):
    return (earlier[0] + later[0], earlier[1] + later[1])


def per_device(
    tokens,
    gain_attn,
    qkv_weight,
    out_weight,
    gain_ffn,
    up_weight,
    up_bias,
    down_weight,
    down_bias,
    out_grad,
):
    image_count, block_len, local_width = tokens.shape
    row_count = image_count * block_len
    model_width = qkv_weight.shape[0]
    heads_local = local_width // HEAD_DIM
    column_start = lax.axis_index("head") * local_width
    full_tokens, gain_first, gain_second = (
        lax.all_gather(tokens, "head", axis=2, tiled=True),
        lax.all_gather(gain_attn, "head", axis=0, tiled=True),
        lax.all_gather(gain_ffn, "head", axis=0, tiled=True),
    )
    token_rows = full_tokens.reshape(row_count, model_width)
    normed_one = layer_norm(token_rows, gain_first)
    proj_weight = qkv_weight.reshape(model_width, 3 * local_width)
    projected = jnp.dot(normed_one, proj_weight, precision=highest)
    parts_view = projected.reshape(image_count, block_len, 3, heads_local, HEAD_DIM)
    query_proj = parts_view[:, :, 0]
    key_proj = parts_view[:, :, 1]
    value_proj = parts_view[:, :, 2]
    (own_state, own_total), pull_state = jax.vjp(block_state, key_proj, value_proj)
    zero_pair = (jnp.zeros_like(own_state), jnp.zeros_like(own_total))
    prior_state, prior_total = entering((own_state, own_total), "seq", add_pair, zero_pair, False)
    mixed, pull_attend = jax.vjp(
        block_attend, query_proj, key_proj, value_proj, prior_state, prior_total
    )
    mixed_rows = mixed.reshape(row_count, local_width)
    branch_out = jnp.dot(mixed_rows, out_weight, precision=highest)
    token_share = tokens.reshape(row_count, local_width)
    resid_share = token_share + lax.psum_scatter(
        branch_out, "head", scatter_dimension=1, tiled=True
    )
    resid_full = lax.all_gather(resid_share, "head", axis=1, tiled=True)
    normed_two = layer_norm(resid_full, gain_second)
    up_proj = jnp.dot(normed_two, up_weight, precision=highest) + up_bias
    hidden, pull_act = jax.vjp(mlp_act, up_proj)
    down_proj = jnp.dot(hidden, down_weight, precision=highest)
    ffn_share = lax.psum_scatter(down_proj, "head", scatter_dimension=1, tiled=True)
    output = (resid_share + ffn_share + down_bias).reshape(tokens.shape)
    grad_share = out_grad.reshape(row_count, local_width)
    grad_full = lax.all_gather(grad_share, "head", axis=1, tiled=True)
    down_bias_grad = jnp.sum(grad_share, axis=0)
    down_weight_grad = jnp.dot(hidden.T, grad_full, precision=highest)
    hidden_grad = jnp.dot(grad_full, down_weight.T, precision=highest)
    (up_grad,) = pull_act(hidden_grad)
    up_bias_grad = jnp.sum(up_grad, axis=0)
    up_weight_grad = jnp.dot(normed_two.T, up_grad, precision=highest)
    ffn_grads = lax.psum((up_weight_grad, down_weight_grad), ("seq", "dp"))
    resid_back, gain_ffn_share = norm_back(
        jnp.dot(up_grad, up_weight.T, precision=highest), resid_full, gain_second, gain_ffn
    )
    resid_grad_share = grad_share + resid_back
    resid_grad = lax.all_gather(resid_grad_share, "head", axis=1, tiled=True)
    out_weight_grad = jnp.dot(mixed_rows.T, resid_grad, precision=highest)
    mixed_grad = jnp.dot(resid_grad, out_weight.T, precision=highest).reshape(mixed.shape)
    query_grad, key_grad, value_grad, state_grad, total_grad = pull_attend(mixed_grad)
    later_state, later_total = entering((state_grad, total_grad), "seq", add_pair, zero_pair, True)
    key_extra, value_extra = pull_state((later_state, later_total))
    key_grad = key_grad + key_extra
    value_grad = value_grad + value_extra
    proj_grad = jnp.stack([query_grad, key_grad, value_grad], axis=2).reshape(
        row_count, 3 * local_width
    )
    qkv_weight_grad = jnp.dot(normed_one.T, proj_grad, precision=highest).reshape(qkv_weight.shape)
    token_back, gain_attn_share = norm_back(
        jnp.dot(proj_grad, proj_weight.T, precision=highest), token_rows, gain_first, gain_attn
    )
    tokens_grad = (resid_grad_share + token_back).reshape(tokens.shape)
    summed_grads = lax.psum(
        (
            gain_attn_share,
            qkv_weight_grad,
            out_weight_grad,
            gain_ffn_share,
            up_bias_grad,
            down_bias_grad,
        ),
        ("seq", "dp"),
    )
    return (
        output,
        tokens_grad,
        summed_grads[0],
        summed_grads[1],
        summed_grads[2],
        summed_grads[3],
        ffn_grads[0],
        summed_grads[4],
        ffn_grads[1],
        summed_grads[5],
    )


MESH = pl.DeviceIdType.MESH
BF = jnp.bfloat16
F32 = jnp.float32
LANES = 256
DIMS = {
    "nn": (((1,), (0,)), ((), ())),
    "nt": (((1,), (1,)), ((), ())),
    "tn": (((0,), (0,)), ((), ())),
}


def round_up(value, step):
    return -(-value // step) * step


def padded(length):
    return round_up(round_up(length, 8) + 8, 16)


def row_blocks(rows):
    return [slice(r, r + 16) for r in range(0, rows, 16)]


def pad_rows(raw, slots, i, h):
    length, rows = raw.shape[1], slots.shape[1]
    slots[i, 0:length, lanes(h)] = raw[i]
    slots[i, length:rows, lanes(h)] = jnp.zeros((rows - length, LANES), F32)


def dot(left, right, kind):
    return lax.dot_general(left, right, DIMS[kind], preferred_element_type=F32)


def split(values):
    high = values.astype(BF)
    return high, (values - high.astype(F32)).astype(BF)


def dot3(left, right, kind):
    return (
        dot(left[0], right[0], kind) + dot(left[0], right[1], kind) + dot(left[1], right[0], kind)
    )


def dot2(left, right, kind):
    return dot(left[0], right, kind) + dot(left[1], right, kind)


def lanes(index):
    if isinstance(index, int):
        return pl.ds(index * LANES, LANES)
    return pl.ds(pl.multiple_of(index * LANES, LANES), LANES)


def place():
    z, h, c = lax.axis_index("seq"), lax.axis_index("head"), lax.axis_index("dp")
    near_x = h + 1 - 2 * lax.rem(h, 2)
    near_y = lax.rem(h + 2, 4)
    return z, h, c, near_x, near_y, 3 - h


def remote(src, dst, send, recv, device):
    return pltpu.make_async_remote_copy(
        src_ref=src, dst_ref=dst, send_sem=send, recv_sem=recv, device_id=device, device_id_type=MESH
    )


def greet(targets):
    barrier = pltpu.get_barrier_semaphore()
    for device in targets:
        pl.semaphore_signal(barrier, inc=1, device_id=device, device_id_type=MESH)


def meet(targets):
    pl.semaphore_wait(pltpu.get_barrier_semaphore(), len(targets))


class Gather:
    SEMS = 8

    def __init__(self, own, slots, rows, sems):
        self.own, self.slots, self.sems = own, slots, sems
        self.half = round_up(rows // 2, 8)
        self.rows = rows

    def copies(self, i):
        _, h, _, near_x, near_y, _ = place()
        slots, sems = self.slots, self.sems
        first, second = pl.ds(0, self.half), pl.ds(self.half, self.rows - self.half)
        every = pl.ds(0, self.rows)

        def one(src, dst, place_in, device):
            return remote(src, dst, sems.at[i, place_in], sems.at[i, 4 + place_in], {"head": device})

        own = self.own(i)
        return (
            one(own.at[every], slots.at[i, every, lanes(h)], 0, near_x),
            one(own.at[every], slots.at[i, every, lanes(h)], 1, near_y),
            one(slots.at[i, first, lanes(near_x)], slots.at[i, first, lanes(near_x)], 2, near_y),
            one(slots.at[i, second, lanes(near_y)], slots.at[i, second, lanes(near_y)], 3, near_x),
        )

    def arrivals(self, i):
        _, h, _, near_x, near_y, far = place()
        slots, sems = self.slots, self.sems
        first, second = pl.ds(0, self.half), pl.ds(self.half, self.rows - self.half)
        every = pl.ds(0, self.rows)

        def one(dst, place_in, device):
            return remote(dst, dst, sems.at[i, place_in], sems.at[i, 4 + place_in], {"head": device})

        return (
            one(slots.at[i, every, lanes(near_x)], 0, near_x),
            one(slots.at[i, every, lanes(near_y)], 1, near_y),
            one(slots.at[i, first, lanes(far)], 2, near_y),
            one(slots.at[i, second, lanes(far)], 3, near_x),
        )

    def direct(self, i):
        x, y, _, _ = self.copies(i)
        x.start()
        y.start()

    def forward(self, i):
        x, y, _, _ = self.arrivals(i)
        x.wait_recv()
        y.wait_recv()
        _, _, to_y, to_x = self.copies(i)
        to_y.start()
        to_x.start()

    def ready(self, i):
        _, _, x, y = self.arrivals(i)
        x.wait_recv()
        y.wait_recv()

    def finish(self, i):
        for copy in self.copies(i):
            copy.wait_send()


def head_masks(rows):
    head = lax.broadcasted_iota(jnp.int32, (rows, LANES), 1) // HEAD_DIM
    return [head == k for k in range(LANES // HEAD_DIM)]


def diagonal_mask():
    rows = lax.broadcasted_iota(jnp.int32, (LANES, LANES), 0) // HEAD_DIM
    cols = lax.broadcasted_iota(jnp.int32, (LANES, LANES), 1) // HEAD_DIM
    return rows == cols


def pick(mask, pair):
    zero = jnp.zeros((), BF)
    return jnp.where(mask, pair[0], zero), jnp.where(mask, pair[1], zero)


def fold(square):
    square = jnp.where(diagonal_mask(), square, 0.0)
    return (
        square[0:HEAD_DIM]
        + square[HEAD_DIM : 2 * HEAD_DIM]
        + square[2 * HEAD_DIM : 3 * HEAD_DIM]
        + square[3 * HEAD_DIM :]
    )


def unfold(wide):
    return jnp.where(diagonal_mask(), jnp.concatenate([wide] * 4, axis=0), 0.0)


def positive(values):
    return jnp.where(values > 0, values + 1.0, jnp.exp(jnp.minimum(values, 0.0)))


def norm_parts(rows):
    row_mean = jnp.mean(rows, axis=-1, keepdims=True)
    centred = rows - row_mean
    row_inv = lax.rsqrt(jnp.mean(centred * centred, axis=-1, keepdims=True) + norm_eps)
    return centred * row_inv, row_inv


def split_rows(source, high, low, rows, step):
    def one(r, _):
        s = pl.ds(pl.multiple_of(r * step, step), step)
        high[s, :], low[s, :] = split(source[s, :])
        return 0

    lax.fori_loop(0, rows // step, one, 0)


STATE = HEAD_DIM + 8


def attend_kernel(
    dims,
    tok_in, attn_in, ffn_in, wqkv_in, wout_in,
    tok_out, gains_out, proj_out, den_out, prior_out, mix_out, wout_out,
    raw, tok, mix, gains, proj, den, prior, state, state_in, wstage, w_h, w_l, n_h, n_l, wout,
    tok_sem, mix_sem, gain_sem, state_sem, out_sem, mate_sem, pair_sem, load_sem, store_sem,
):
    images, length, used, rows = dims
    width = tok.shape[2]
    z, h, c, near_x, near_y, far = place()
    seq = lax.axis_size("seq")
    out_rows = wout_in.shape[0] // 4

    friends = [{"head": near_x}, {"head": near_y}, {"head": far}, {"dp": 1 - c}]
    friends += [{"seq": lax.rem(z + d, seq)} for d in range(1, seq)]
    greet(friends)
    loads = [pltpu.make_async_copy(tok_in.at[i], raw.at[i], load_sem.at[i]) for i in range(images)]
    loads += [
        pltpu.make_async_copy(wqkv_in.at[pl.ds(j * width, width)], wstage.at[:, lanes(j)], load_sem.at[images + j])
        for j in range(3)
    ]
    for copy in loads:
        copy.start()

    gains[:, lanes(h)] = jnp.zeros((8, LANES), F32)
    gains[0:1, lanes(h)] = attn_in[...]
    gains[1:2, lanes(h)] = ffn_in[...]
    blank = jnp.zeros((rows - used, LANES), F32)
    for i in range(images):
        for other in (near_x, near_y, far):
            tok[i, used:rows, lanes(other)] = blank
    for i in range(images):
        loads[i].wait()
        pad_rows(raw, tok, i, h)

    meet(friends)
    tokens = Gather(lambda i: tok.at[i, :, lanes(h)], tok, used, tok_sem)
    mixes = Gather(lambda i: mix.at[i, :, lanes(h)], mix, used, mix_sem)
    tokens.direct(0)
    gain_copies = [
        remote(gains.at[:, lanes(h)], gains.at[:, lanes(h)], gain_sem.at[k], gain_sem.at[3 + k], {"head": other})
        for k, other in enumerate((near_x, near_y, far))
    ]
    for copy in gain_copies:
        copy.start()
    tokens.direct(1)
    for copy in loads[images:]:
        copy.wait()
    split_rows(wstage, w_h, w_l, wstage.shape[0], 64)
    for k, other in enumerate((near_x, near_y, far)):
        remote(
            gains.at[:, lanes(other)], gains.at[:, lanes(other)], gain_sem.at[k], gain_sem.at[3 + k],
            {"head": other},
        ).wait_recv()
    row_ok = lax.broadcasted_iota(jnp.int32, (rows, LANES), 0) < length

    def project(i):

        for s in row_blocks(rows):
            n_h[s, :], n_l[s, :] = split(norm_parts(tok[i, s, :])[0] * gains[0:1, :])
        proj[i] = dot3((n_h[...], n_l[...]), (w_h[...], w_l[...]), "nn")
        key_feat = jnp.where(row_ok, positive(proj[i, :, lanes(1)]), 0.0)
        state[i, 0:HEAD_DIM, :] = fold(dot3(split(key_feat), split(proj[i, :, lanes(2)]), "tn"))
        state[i, HEAD_DIM:, :] = jnp.broadcast_to(
            jnp.sum(key_feat, axis=0, keepdims=True), (STATE - HEAD_DIM, LANES)
        )
        for d in range(1, seq):

            @pl.when(z + d < seq)
            def _():
                state_copy(i, d, d).start()

    def state_copy(i, d, step):
        return remote(
            state.at[i], state_in.at[d - 1, i], state_sem.at[0, d - 1, i], state_sem.at[1, d - 1, i],
            {"seq": lax.rem(z + step + seq, seq)},
        )

    def attend(i):
        prior[i] = jnp.zeros((STATE, LANES), F32)
        for d in range(1, seq):

            @pl.when(z >= d)
            def _():
                state_copy(i, d, -d).wait_recv()
                prior[i] = prior[i] + state_in[d - 1, i]

        query_feat = positive(proj[i, :, lanes(0)])
        key_feat = jnp.where(row_ok, positive(proj[i, :, lanes(1)]), 0.0)
        query_pair, key_pair = split(query_feat), split(key_feat)
        value_pair = split(proj[i, :, lanes(2)])
        total = prior[i, HEAD_DIM : HEAD_DIM + 1, :]
        ones = jnp.where(diagonal_mask(), 1.0, 0.0).astype(BF)
        num = dot3(query_pair, split(unfold(prior[i, 0:HEAD_DIM, :])), "nn")
        below = dot2(split(query_feat * total), ones, "nn")
        row = lax.broadcasted_iota(jnp.int32, (rows, rows), 0)
        col = lax.broadcasted_iota(jnp.int32, (rows, rows), 1)
        for mask in head_masks(rows):
            scores = dot3(query_pair, pick(mask, key_pair), "nt")
            score_pair = split(jnp.where(col <= row, scores, 0.0))
            num = num + dot3(score_pair, pick(mask, value_pair), "nn")
            below = below + dot2(score_pair, jnp.where(mask, 1.0, 0.0).astype(BF), "nn")
        den[i] = below
        mix[i, :, lanes(h)] = jnp.where(row_ok, num / below, 0.0)
        blank_rows = jnp.zeros((rows - used, LANES), F32)
        for other in (near_x, near_y, far):
            mix[i, used:rows, lanes(other)] = blank_rows

    mate = z + 1 - 2 * lax.rem(z, 2)

    def quarter(plane, core):
        return pl.ds(pl.multiple_of((2 * lax.rem(plane, 2) + core) * out_rows, out_rows), out_rows)

    own_rows = quarter(z, c)
    out_copies = [
        remote(
            wout_in.at[own_rows], wout.at[h, own_rows], out_sem.at[0, k], out_sem.at[1, k], {"head": other}
        )
        for k, other in enumerate((near_x, near_y, far))
    ]
    out_own = pltpu.make_async_copy(wout_in, wout.at[h], load_sem.at[images + 4])

    def out_arrival(k, other):
        return remote(
            wout.at[other, own_rows], wout.at[other, own_rows], out_sem.at[0, k], out_sem.at[1, k],
            {"head": other},
        )

    def mate_copy(k, other, plane):
        part = wout.at[other, quarter(plane, c)]
        return remote(part, part, mate_sem.at[0, k], mate_sem.at[1, k], {"seq": mate})

    def pair_copy(k, other, plane, core, late):
        part = wout.at[other, quarter(plane, core)]
        return remote(part, part, pair_sem.at[0, late, k], pair_sem.at[1, late, k], {"dp": 1 - c})

    peers = tuple(enumerate((near_x, near_y, far)))
    stores = []

    def store(src, dst):
        copy = pltpu.make_async_copy(src, dst, store_sem.at[len(stores)])
        copy.start()
        stores.append(copy)

    for t in range(images + 2):
        if t < images:
            tokens.forward(t)
            if t + 2 < images:
                tokens.direct(t + 2)
            elif t == images - 1:
                for copy in out_copies:
                    copy.start()
                out_own.start()
        if 1 <= t <= images:
            tokens.ready(t - 1)
            project(t - 1)
            store(tok.at[t - 1], tok_out.at[t - 1])
            store(proj.at[t - 1], proj_out.at[t - 1])
        if t == images + 1:
            for k, other in peers:
                out_arrival(k, other).wait_recv()
                mate_copy(k, other, z).start()
                pair_copy(k, other, z, c, 0).start()
        if t >= 2:
            attend(t - 2)
            mixes.direct(t - 2)
            store(den.at[t - 2], den_out.at[t - 2])
            store(prior.at[t - 2], prior_out.at[t - 2])
    store(gains, gains_out)
    out_own.wait()
    for i in range(images - 1):
        mixes.forward(i)
    for k, other in peers:
        mate_copy(k, other, mate).wait_recv()
        pair_copy(k, other, mate, c, 1).start()
    mixes.forward(images - 1)
    for k, other in peers:
        pair_copy(k, other, z, 1 - c, 0).wait_recv()
        pair_copy(k, other, mate, 1 - c, 1).wait_recv()
    store(wout, wout_out)
    for i in range(images):
        mixes.ready(i)
        store(mix.at[i], mix_out.at[i])
    for i in range(images):
        tokens.finish(i)
        mixes.finish(i)
        for d in range(1, seq):

            @pl.when(z + d < seq)
            def _(i=i, d=d):
                state_copy(i, d, d).wait_send()

    for copy in gain_copies + out_copies:
        copy.wait_send()
    for k, other in peers:
        mate_copy(k, other, z).wait_send()
        pair_copy(k, other, z, c, 0).wait_send()
        pair_copy(k, other, mate, c, 1).wait_send()
    for copy in stores:
        copy.wait()


def attend_call(tokens, gain_attn, gain_ffn, wqkv, wout):
    images, length, _ = tokens.shape
    used = round_up(length, 8)
    rows = padded(length)
    width = wqkv.shape[0] // 3
    heads_n = width // LANES
    dma = pltpu.SemaphoreType.DMA
    seq = lax.axis_size("seq")
    any_spec = pl.BlockSpec(memory_space=pl.ANY)
    vmem_spec = pl.BlockSpec(memory_space=pltpu.VMEM)
    shape = lambda *s: jax.ShapeDtypeStruct(s, F32)
    return pl.pallas_call(
        functools.partial(attend_kernel, (images, length, used, rows)),
        out_shape=(
            shape(images, rows, width),
            shape(8, width),
            shape(images, rows, 3 * LANES),
            shape(images, rows, LANES),
            shape(images, STATE, LANES),
            shape(images, rows, width),
            shape(heads_n, LANES, width),
        ),
        in_specs=[any_spec, vmem_spec, vmem_spec, any_spec, any_spec],
        out_specs=(any_spec,) * 7,
        scratch_shapes=[
            pltpu.VMEM((images, length, LANES), F32),
            pltpu.VMEM((images, rows, width), F32),
            pltpu.VMEM((images, rows, width), F32),
            pltpu.VMEM((8, width), F32),
            pltpu.VMEM((images, rows, 3 * LANES), F32),
            pltpu.VMEM((images, rows, LANES), F32),
            pltpu.VMEM((images, STATE, LANES), F32),
            pltpu.VMEM((images, STATE, LANES), F32),
            pltpu.VMEM((seq - 1, images, STATE, LANES), F32),
            pltpu.VMEM((width, 3 * LANES), F32),
            pltpu.VMEM((width, 3 * LANES), BF),
            pltpu.VMEM((width, 3 * LANES), BF),
            pltpu.VMEM((rows, width), BF),
            pltpu.VMEM((rows, width), BF),
            pltpu.VMEM((heads_n, LANES, width), F32),
            dma((images, Gather.SEMS)),
            dma((images, Gather.SEMS)),
            dma((6,)),
            dma((2, seq - 1, images)),
            dma((2, 3)),
            dma((2, 3)),
            dma((2, 2, 3)),
            dma((images + 5,)),
            dma((5 * images + 4,)),
        ],
        compiler_params=pltpu.CompilerParams(
            collective_id=0, has_side_effects=True, vmem_limit_bytes=VMEM_BYTES
        ),
    )(tokens, gain_attn, gain_ffn, wqkv, wout)


VMEM_BYTES = 60 * 1024 * 1024
class Scatter:
    SEMS = 12

    def __init__(self, part, buffers, rows, sems):
        self.part, self.buffers, self.sems = part, buffers, sems
        self.half = round_up(rows // 2, 8)
        self.rows = rows
        self.first, self.second = pl.ds(0, self.half), pl.ds(self.half, rows - self.half)
        self.left = pl.ds(0, rows - self.half)

    def slot(self, i, k):
        rows = self.first if k in (0, 2, 5) else self.left
        return self.buffers.at[i, k, rows]

    def copy(self, i, k, src, into=None):
        _, _, _, near_x, near_y, _ = place()
        into = k if into is None else into
        device = near_x if into in (0, 2, 4) else near_y
        return remote(
            src, self.slot(i, into), self.sems.at[i, into], self.sems.at[i, 6 + into], {"head": device}
        )

    def sent(self, i):
        _, _, _, near_x, near_y, far = place()
        part = self.part(i)
        return (
            self.copy(i, 2, part.at[self.first, lanes(far)]),
            self.copy(i, 3, part.at[self.second, lanes(far)]),
            self.copy(i, 0, part.at[self.first, lanes(near_x)]),
            self.copy(i, 1, part.at[self.second, lanes(near_y)]),
        )

    def passed(self, i):
        return (
            self.copy(i, 2, self.slot(i, 2), 5),
            self.copy(i, 3, self.slot(i, 3), 4),
        )

    def direct(self, i):
        for copy in self.sent(i):
            copy.start()

    def relay(self, i):
        _, _, _, near_x, near_y, _ = place()
        part = self.part(i)
        to_y, to_x = self.passed(i)
        self.copy(i, 2, self.slot(i, 2)).wait_recv()
        self.buffers[i, 2, self.first] = self.buffers[i, 2, self.first] + part[self.first, lanes(near_y)]
        to_y.start()
        self.copy(i, 3, self.slot(i, 3)).wait_recv()
        self.buffers[i, 3, self.left] = self.buffers[i, 3, self.left] + part[self.second, lanes(near_x)]
        to_x.start()

    def total(self, i):
        _, h, _, _, _, _ = place()
        part = self.part(i)
        for k in (0, 5, 1, 4):
            self.copy(i, k, self.slot(i, k)).wait_recv()
        first = (
            part[self.first, lanes(h)] + self.buffers[i, 0, self.first] + self.buffers[i, 5, self.first]
        )
        second = part[self.second, lanes(h)] + self.buffers[i, 1, self.left] + self.buffers[i, 4, self.left]
        return jnp.concatenate([first, second], axis=0)

    def finish(self, i):
        for copy in self.sent(i) + self.passed(i):
            copy.wait_send()


def activation(values):
    scale = 0.7978845608028654
    square = values * values
    bent = jnp.tanh(scale * values * (1.0 + 0.044715 * square))
    half = 0.5 * (1.0 + bent)
    slope = half + 0.5 * values * (1.0 - bent * bent) * (scale * (1.0 + 0.134145 * square))
    return values * half, slope


def to_lanes(first, second, rows):
    lane = lax.broadcasted_iota(jnp.int32, (rows, 128), 1)
    both = jnp.where(lane == 0, first, jnp.where(lane == 1, second, 0.0))
    both = jnp.concatenate([both, jnp.zeros((LANES - rows, 128), F32)], axis=0)
    return jnp.transpose(both)[0:8]


def to_columns(block, rows):
    tall = jnp.concatenate([block, jnp.zeros((120, LANES), F32)], axis=0)
    turned = jnp.transpose(tall)[0:rows]
    return turned[:, 0:1], turned[:, 1:2]


class Reduce:
    SEMS = 4
    RING_SEMS = 7
    RING = 12
    LATE = (12, 9, 6, 3, 0)

    def __init__(self, sems, ring_sems):
        self.sems, self.ring_sems, self.total = sems, ring_sems, sems.shape[0]
        self.chunks = []
        self.clock = 0
        self.ready = 0

    def chunk(self, mine, theirs, got, result, result_other, room):
        self.chunks.append(
            dict(mine=mine, theirs=theirs, got=got, result=result, result_other=result_other, slot=room)
        )

    def add(self, partial, arrived, result, rows, ring, columns):
        c = lax.axis_index("dp")
        half = partial.shape[0] // 2
        for j in columns:
            for r in range(half // rows):
                here = pl.ds(pl.multiple_of(c * half + r * rows, 8), rows)
                there = pl.ds(pl.multiple_of((1 - c) * half + r * rows, 8), rows)
                self.chunk(
                    partial.at[here, lanes(j)], partial.at[there, lanes(j)],
                    arrived.at[pl.ds(r * rows, rows), lanes(j)], result.at[here, lanes(j)], result.at[there, lanes(j)],
                    ring.at[len(self.chunks) % self.RING, :, pl.ds(0, rows)],
                )
        return len(self.chunks)

    def add_columns(self, partial, arrived, result, rows, ring):
        c = lax.axis_index("dp")
        depth = partial.shape[0]
        half = depth // 2
        blocks = partial.shape[1] // LANES
        for j in range(blocks):
            rows = rows // 2 if j == blocks - 1 else rows
            for r in range(half // rows):
                here = pl.multiple_of(c * half + r * rows, 8)
                there = pl.multiple_of((1 - c) * half + r * rows, 8)
                self.chunk(
                    partial.at[pl.ds(here, rows), lanes(j)], partial.at[pl.ds(there, rows), lanes(j)],
                    arrived.at[pl.ds(j * half + r * rows, rows)],
                    result.at[pl.ds(j * depth + here, rows)], result.at[pl.ds(j * depth + there, rows)],
                    ring.at[len(self.chunks) % self.RING, :, pl.ds(0, rows)],
                )
        return len(self.chunks)

    def side(self, k):
        z = lax.axis_index("seq")
        return z if k % 2 == 0 else 3 - z

    def device(self, k, y):
        return {"seq": y if k % 2 == 0 else 3 - y}

    def sem(self, k, n):
        return self.sems.at[k, n] if n < self.SEMS else self.ring_sems.at[k % self.RING, n - self.SEMS]

    def pair(self, k):
        chunk = self.chunks[k]
        c = lax.axis_index("dp")
        return remote(chunk["theirs"], chunk["got"], self.sem(k, 0), self.sem(k, 1), {"dp": 1 - c})

    def partial(self, k, into, y):
        chunk = self.chunks[k]
        return remote(
            chunk["mine"], chunk["slot"].at[into], self.sem(k, 4), self.sem(k, 5 + into), self.device(k, y)
        )

    def outcome(self, k, src, y, send):
        return remote(src, self.chunks[k]["result"], self.sem(k, send), self.sem(k, 7), self.device(k, y))

    def twin(self, k, src):
        c = lax.axis_index("dp")
        return remote(src, self.chunks[k]["result"], self.sem(k, 2), self.sem(k, 3), {"dp": 1 - c})

    def kept(self, k):
        chunk = self.chunks[k]
        return pltpu.make_async_copy(chunk["mine"], chunk["result"], self.sem(k, 10))

    def exchange(self, first, end):
        for k in range(first, end):
            self.pair(k).start()
        self.ready = end

    def combine(self, k):
        chunk, y = self.chunks[k], self.side(k)
        self.pair(k).wait_recv()
        chunk["mine"][...] = chunk["mine"][...] + chunk["got"][...]

        @pl.when(y == 0)
        def _():
            self.partial(k, 0, 1).start()

        @pl.when(y == 3)
        def _():
            self.partial(k, 0, 2).start()

    def middle(self, k):
        chunk, y = self.chunks[k], self.side(k)

        @pl.when(y == 2)
        def _():
            self.partial(k, 0, 3).wait_recv()
            chunk["mine"][...] = chunk["mine"][...] + chunk["slot"][0]
            self.partial(k, 1, 1).start()

    def root(self, k):
        chunk, y = self.chunks[k], self.side(k)

        @pl.when(y == 1)
        def _():
            self.partial(k, 0, 0).wait_recv()
            self.partial(k, 1, 2).wait_recv()
            chunk["mine"][...] = chunk["mine"][...] + chunk["slot"][0] + chunk["slot"][1]
            self.outcome(k, chunk["mine"], 2, 8).start()
            self.outcome(k, chunk["mine"], 0, 9).start()
            self.kept(k).start()
            self.twin(k, chunk["mine"]).start()

    def onward(self, k):
        chunk, y = self.chunks[k], self.side(k)

        @pl.when(y == 2)
        def _():
            self.outcome(k, chunk["result"], 1, 8).wait_recv()
            self.outcome(k, chunk["result"], 3, 8).start()
            self.twin(k, chunk["result"]).start()

    def leaf(self, k):
        chunk, y = self.chunks[k], self.side(k)

        @pl.when(y == 0)
        def _():
            self.outcome(k, chunk["result"], 1, 8).wait_recv()
            self.twin(k, chunk["result"]).start()

        @pl.when(y == 3)
        def _():
            self.outcome(k, chunk["result"], 2, 8).wait_recv()
            self.twin(k, chunk["result"]).start()

    def settle(self, k):
        chunk, y = self.chunks[k], self.side(k)

        @pl.when(y == 0)
        def _():
            self.partial(k, 0, 1).wait_send()

        @pl.when(y == 3)
        def _():
            self.partial(k, 0, 2).wait_send()

        @pl.when(y == 2)
        def _():
            self.partial(k, 1, 1).wait_send()
            self.outcome(k, chunk["result"], 3, 8).wait_send()

        @pl.when(y == 1)
        def _():
            self.outcome(k, chunk["mine"], 2, 8).wait_send()
            self.outcome(k, chunk["mine"], 0, 9).wait_send()
            self.kept(k).wait()

    def finish(self, k):
        chunk = self.chunks[k]
        c = lax.axis_index("dp")
        if k + self.RING >= self.total:
            self.settle(k)
        self.pair(k).wait_send()
        remote(
            chunk["result_other"], chunk["result_other"], self.sem(k, 2), self.sem(k, 3), {"dp": 1 - c}
        ).wait_recv()
        self.twin(k, chunk["result"]).wait_send()

    def tick(self, times=1):
        for _ in range(times):
            self.step()

    def step(self):
        if self.clock >= self.ready and self.ready < self.total:
            return
        stages = (self.leaf, self.onward, self.root, self.middle, self.combine)
        for late, act in zip(self.LATE, stages):
            chunk = self.clock - late
            if late == 0 and self.RING <= chunk < self.total:
                self.settle(chunk - self.RING)
            if 0 <= chunk < self.total:
                act(chunk)
        self.clock += 1

    def drain(self):
        while self.clock < self.total + self.LATE[0]:
            self.step()


CHUNK = 128
ROW_TILE = 16


def row_sums(total, value):
    return total + jnp.sum(value, axis=-1, keepdims=True)


def layer_kernel(
    dims,
    tok_in, mix_in, gains_in, wfull_in, up_in, bias, down_in, down_bias, grad_in,
    proj_in, den_in, prior_in, wout_in, wqkv_in,
    out_out, tok_grad_out, qkv_out, out_w_out, up_out, down_out, small_out,
    gains, grad, resid_grad, part_ffn, part, buf_norm, buf_tok, xhat_own, inv_own,
    d_down, d_up, d_small, got_ffn, got_out, got_qkv, got_small, state, state_in, ring, slope, proj, prior, turned_h, turned_l, d_out,
    grad_sem, norm_sem, back_sem, ffn_sem, tok_sem, state_sem, chunk_sem, ring_sem, load_sem, stage_sem, image_sem, store_sem,
):
    images, length, used, rows = dims
    width = grad.shape[2]
    hidden = up_in.shape[1]
    z, h, c, near_x, near_y, far = place()
    seq = lax.axis_size("seq")
    vmem = pltpu.VMEM
    tiles = width // LANES
    row_ok = lax.broadcasted_iota(jnp.int32, (rows, LANES), 0) < length

    small = (pltpu.make_async_copy(gains_in, gains, load_sem.at[0]),)

    grads = Gather(lambda i: grad.at[i, :, lanes(h)], grad, used, grad_sem)
    norm = Scatter(lambda i: part.at[i % 2], buf_norm, rows, norm_sem)
    back = Gather(lambda i: resid_grad.at[i, :, lanes(h)], resid_grad, used, back_sem)
    ffn = Scatter(lambda i: part_ffn.at[i], buf_norm, used, ffn_sem)
    toks = Scatter(lambda i: part.at[i % 2], buf_tok, rows, tok_sem)
    reduce = Reduce(chunk_sem, ring_sem)
    tick = reduce.tick
    stores = []

    def store(src, dst):
        copy = pltpu.make_async_copy(src, dst, store_sem.at[len(stores)])
        copy.start()
        stores.append(copy)

    def halves(source, high, low):
        split_rows(source, high, low, rows, ROW_TILE)

    def stats(i, weight, sums_with):
        first, second = [], []
        for s in row_blocks(rows):
            term = part[i % 2, s, :]
            first.append(jnp.sum(term * gains[weight, :], axis=-1, keepdims=True))
            second.append(jnp.sum(term * sums_with(s), axis=-1, keepdims=True))
        block = to_lanes(jnp.concatenate(first, axis=0), jnp.concatenate(second, axis=0), rows)
        for k in range(tiles):
            part[i % 2, rows - 8 : rows, lanes(k)] = block

    def norm_share(scatter, i, weight, hat, inv):
        both = scatter.total(i)
        mean, cross = to_columns(both[rows - 8 : rows], rows)
        own = jnp.where(row_ok, both, 0.0)
        scaled = own * gains[weight, lanes(h)]
        share = (scaled - mean * (1.0 / width) - hat * (cross * (1.0 / width))) * inv
        return share, own

    def resid_back(i):
        share, own = norm_share(norm, i, slice(1, 2), xhat_own[i], inv_own[i, :, 0:1])
        resid_grad[i, :, lanes(h)] = jnp.where(row_ok, grad[i, :, lanes(h)] + share, 0.0)
        for k, value in ((1, own * xhat_own[i]), (2, grad[i, :, lanes(h)])):
            d_small[8:9, lanes(k)] = d_small[8:9, lanes(k)] + jnp.sum(value, axis=0, keepdims=True)
        norm.finish(i)
        back.direct(i)
        grads.finish(i)
        for copy in image_copies(i):
            copy.start()

    dden_at, den_at, mixed_at, dnum_at = lanes(0), lanes(1), lanes(2), lanes(3)

    def image_copies(i):
        return (
            pltpu.make_async_copy(mix_in.at[i, :, lanes(h)], grad.at[i, :, mixed_at], load_sem.at[8 + 4 * i]),
            pltpu.make_async_copy(den_in.at[i], grad.at[i, :, den_at], load_sem.at[9 + 4 * i]),
        )

    def proj_copies(i):
        return (
            pltpu.make_async_copy(proj_in.at[i], proj.at[i], load_sem.at[10 + 4 * i]),
            pltpu.make_async_copy(prior_in.at[i], prior.at[i], load_sem.at[11 + 4 * i]),
        )

    def state_copy(i, step):
        return remote(
            state.at[i], state_in.at[i], state_sem.at[0, i], state_sem.at[1, i],
            {"seq": lax.rem(z + step + seq, seq)},
        )

    def hop(i, step):
        @pl.when(z == seq - 1 - step)
        def _():
            state_copy(i, 1).wait_recv()
            if step < seq - 1:
                state[i] = state[i] + state_in[i]
                state_copy(i, -1).start()

    def first_half(i, rg_h, rg_l):
        back.ready(i)
        for copy in image_copies(i):
            copy.wait()
        halves(resid_grad.at[i], rg_h, rg_l)
        dm = dot3((rg_h[...], rg_l[...]), (turned_h[...], turned_l[...]), "nn")
        ones = jnp.where(diagonal_mask(), 1.0, 0.0).astype(BF)
        inverse = 1.0 / grad[i, :, den_at]
        slope[i, :, dnum_at] = dm * inverse
        grad[i, :, dden_at] = -dot2(split(dm * grad[i, :, mixed_at]), ones, "nn") * inverse
        query_feat = positive(proj[i, :, lanes(0)])
        state[i, 0:HEAD_DIM, :] = fold(dot3(split(query_feat), split(slope[i, :, dnum_at]), "tn"))
        state[i, HEAD_DIM:, :] = jnp.broadcast_to(
            jnp.sum(query_feat * grad[i, :, dden_at], axis=0, keepdims=True), (STATE - HEAD_DIM, LANES)
        )
        @pl.when(z == seq - 1)
        def _():
            state_in[i] = jnp.zeros((STATE, LANES), F32)
            state_copy(i, -1).start()

        term = dot3(split(grad[i, :, mixed_at]), (rg_h[...], rg_l[...]), "tn")
        d_out[...] = term if i == 0 else d_out[...] + term

    def within(i):
        query_feat = positive(proj[i, :, lanes(0)])
        key_feat = jnp.where(row_ok, positive(proj[i, :, lanes(1)]), 0.0)
        query_pair, key_pair, value_pair = split(query_feat), split(key_feat), split(proj[i, :, lanes(2)])
        dden_i = grad[i, :, dden_at]
        dnum_pair = split(slope[i, :, dnum_at])
        prior_pair = split(unfold(prior[i, 0:HEAD_DIM, :]))
        fq = dot3(dnum_pair, prior_pair, "nt") + dden_i * prior[i, HEAD_DIM : HEAD_DIM + 1, :]
        fk = jnp.zeros((rows, LANES), F32)
        fv = jnp.zeros((rows, LANES), F32)
        row = lax.broadcasted_iota(jnp.int32, (rows, rows), 0)
        col = lax.broadcasted_iota(jnp.int32, (rows, rows), 1)
        causal = col <= row
        for k, mask in enumerate(head_masks(rows)):
            key_h, query_h = pick(mask, key_pair), pick(mask, query_pair)
            scores = split(jnp.where(causal, dot3(query_pair, key_h, "nt"), 0.0))
            pull = dot3(dnum_pair, pick(mask, value_pair), "nt")
            pull = pull + dden_i[:, k * HEAD_DIM : k * HEAD_DIM + 1]
            pull = split(jnp.where(causal, pull, 0.0))
            fq = fq + dot3(pull, key_h, "nn")
            fk = fk + dot3(pull, query_h, "tn")
            fv = fv + dot3(scores, pick(mask, dnum_pair), "tn")
        slope[i, :, lanes(0)] = fq
        slope[i, :, lanes(1)] = fk
        slope[i, :, lanes(2)] = fv

    def load_phase(raw):
        copies = [pltpu.make_async_copy(grad_in.at[i], raw.at[i], load_sem.at[3 + i]) for i in range(images)]
        for copy in copies + list(small):
            copy.start()
        start_loads()
        blank = jnp.zeros((rows - used, LANES), F32)
        for i in range(images):
            for other in (near_x, near_y, far):
                grad[i, used:rows, lanes(other)] = blank
                resid_grad[i, used:rows, lanes(other)] = blank
        d_small[...] = jnp.zeros_like(d_small)
        for i in range(images):
            copies[i].wait()
            pad_rows(raw, grad, i, h)

    def ffn_phase(
        wo_h, wo_l, up_h, up_l, pair_h, pair_l, n_h, n_l, hid_h, hid_l, ug_h, ug_l
    ):
        rooms = ((d_down, wo_h, wo_l), (d_up, up_h, up_l))

        def take(k):
            room, high, low = rooms[k]
            weight_loads[k].wait()
            split_rows(room, high, low, room.shape[0], 64)

        def turned(source, target):
            def one(k, _):
                s = lanes(k)
                target[:, s] = source[s, :].T
                return 0

            lax.fori_loop(0, tiles, one, 0)

        tok_copy, mix_copy = image_loads

        def forward(i):
            mix_copy(i).wait()
            halves(part.at[1], pair_h, pair_l)
            if i + 1 < images:
                mix_copy(i + 1).start()
            if i == 0:
                take(0)
            tok_copy(i).wait()
            part[0] = part[0] + dot3((pair_h[...], pair_l[...]), (wo_h[...], wo_l[...]), "nn")
            part_ffn[i, :, lanes(h)] = part[0, :, lanes(h)]
            grads.forward(i)
            if i + 2 < images:
                grads.direct(i + 2)

            for s in row_blocks(rows):
                hat, inv = norm_parts(part[0, s, :])
                part[0, s, :] = hat
                inv_own[i, s, :] = jnp.broadcast_to(inv, (ROW_TILE, 128))
                n_h[i, s, :], n_l[i, s, :] = split(hat * gains[1:2, :])
            xhat_own[i] = part[0, :, lanes(h)]
            if i + 1 < images:
                tok_copy(i + 1).start()
            if i == 0:
                take(1)
                weight_loads[2].start()
            slope[i] = dot3((n_h[i], n_l[i]), (up_h[...], up_l[...]), "nn") + bias[0:1, :]
            for s in row_blocks(rows):
                act, by = activation(slope[i, s, :])
                hid_h[i, s, :], hid_l[i, s, :] = split(act)
                slope[i, s, :] = by
            grads.ready(i)
            halves(grad.at[i], pair_h, pair_l)

            term = dot3((hid_h[i], hid_l[i]), (pair_h[...], pair_l[...]), "tn")
            d_down[...] = term if i == 0 else d_down[...] + term

        def hidden_back(i):
            halves(grad.at[i], pair_h, pair_l)

            part[i % 2] = dot3((pair_h[...], pair_l[...]), (up_h[...], up_l[...]), "nn")
            total = jnp.zeros((1, hidden), F32)
            for s in row_blocks(rows):
                ug = part[i % 2, s, :] * slope[i, s, :]
                ug_h[s, :], ug_l[s, :] = split(ug)
                total = total + jnp.sum(ug, axis=0, keepdims=True)
            d_small[0:1, :] = d_small[0:1, :] + total

        def up_grad(i):
            term = dot3((n_h[i], n_l[i]), (ug_h[...], ug_l[...]), "tn")
            d_up[...] = term if i == 0 else d_up[...] + term

        def norm_back(i):
            part[i % 2] = dot3((ug_h[...], ug_l[...]), (wo_h[...], wo_l[...]), "nn")
            stats(i, slice(1, 2), lambda s: n_h[i, s, :].astype(F32) + n_l[i, s, :].astype(F32))
            norm.direct(i)

        def down(i):
            resid = part_ffn[i, :, lanes(h)]

            part_ffn[i] = dot3((hid_h[i], hid_l[i]), (up_h[...], up_l[...]), "nt")
            part_ffn[i, :, lanes(h)] = part_ffn[i, :, lanes(h)] + resid

        for copy in small:
            copy.wait()
        for i in range(images):
            forward(i)
        reduce.exchange(0, down_chunks)
        turned(up_h, wo_h)
        turned(up_l, wo_l)
        tick()
        weight_loads[2].wait()

        def turn_down(k, _):
            s = lanes(k)
            up_h[:, s], up_l[:, s] = split(d_up[s, :].T)
            return 0

        lax.fori_loop(0, hidden // LANES, turn_down, 0)
        out_load.wait()
        for k in range(tiles):
            turned_h[lanes(k), :], turned_l[lanes(k), :] = split(d_out[:, lanes(k)].T)
        last = images - 1
        for i in range(images):
            hidden_back(i)
            tick()
            if i >= 1:
                norm.relay(i - 1)
            norm_back(i)
            tick()
            up_grad(i)
            if i == last:
                reduce.exchange(down_chunks, up_chunks)
            tick()
            if i >= 2:
                back.forward(i - 2)
                tick()
            if i >= 1:
                resid_back(i - 1)
                tick()
        for i in range(images):
            for copy in proj_copies(i):
                copy.wait()
        first_half(0, pair_h, pair_l)
        tick()
        norm.relay(last)
        back.forward(last - 1)
        down(0)
        tick()
        within(0)
        tick()
        resid_back(last)
        first_half(1, pair_h, pair_l)
        tick()
        hop(0, 1)
        down(1)
        tick()
        back.forward(last)
        within(1)
        tick()
        first_half(2, pair_h, pair_l)
        tick()
        hop(0, 2)
        hop(1, 1)
        down(2)
        tick()
        within(2)
        tick()
        hop(2, 1)
        down(3)
        tick()
        hop(0, 3)
        hop(1, 2)
        first_half(3, pair_h, pair_l)
        reduce.exchange(up_chunks, out_chunks)
        ffn.direct(0)
        ffn.direct(1)
        tick()
        hop(2, 2)
        within(3)
        tick()
        hop(1, 3)
        hop(3, 1)

    def attend_phase(
        wq_h, wq_l, tok, n_h, n_l, xhat, pg_h, pg_l, hat_own, root_own, d_qkv, out_trim, tok_trim,
    ):
        def tok_copy(i):
            return pltpu.make_async_copy(tok_in.at[i], tok.at[i % 2], image_sem.at[i % 2])

        weights = [
            pltpu.make_async_copy(wqkv_in.at[pl.ds(j * width, width)], d_qkv.at[:, lanes(j)], load_sem.at[1 + j])
            for j in range(3)
        ]
        for copy in weights:
            copy.start()
        tok_copy(0).start()
        tok_copy(1).start()
        qkv_chunks = reduce.add_columns(d_qkv, got_qkv, qkv_out, CHUNK, ring)
        all_chunks = reduce.add(d_small, got_small, small_out, 8, ring, range(1))

        def across(i):
            later_pair = split(unfold(state_in[i, 0:HEAD_DIM, :]))
            query, key, value = (proj[i, :, lanes(k)] for k in range(3))
            key_pair = split(jnp.where(row_ok, positive(key), 0.0))
            fk = slope[i, :, lanes(1)] + dot3(split(value), later_pair, "nt")
            fk = fk + state_in[i, HEAD_DIM : HEAD_DIM + 1, :]
            fv = slope[i, :, lanes(2)] + dot3(key_pair, later_pair, "nn")
            bend = lambda v: jnp.where(v > 0, 1.0, jnp.exp(jnp.minimum(v, 0.0)))
            pg_h[i, :, lanes(0)], pg_l[i, :, lanes(0)] = split(slope[i, :, lanes(0)] * bend(query))
            pg_h[i, :, lanes(1)], pg_l[i, :, lanes(1)] = split(jnp.where(row_ok, fk * bend(key), 0.0))
            pg_h[i, :, lanes(2)], pg_l[i, :, lanes(2)] = split(fv)

        def weight_grads(i):
            tok_copy(i).wait()

            for s in row_blocks(rows):
                hat, inv = norm_parts(tok[i % 2, s, :])
                xhat[s, :] = hat
                root_own[i, s, :] = jnp.broadcast_to(inv, (ROW_TILE, 128))
                n_h[i, s, :], n_l[i, s, :] = split(hat * gains[0:1, :])
            hat_own[i] = xhat[:, lanes(h)]
            if i + 2 < images:
                tok_copy(i + 2).start()

            term = dot3((n_h[i], n_l[i]), (pg_h[i], pg_l[i]), "tn")
            d_qkv[...] = term if i == 0 else d_qkv[...] + term

        def norm_back(i):
            if i >= 2:
                toks.finish(i - 2)

            part[i % 2] = dot3((pg_h[i], pg_l[i]), (wq_h[...], wq_l[...]), "nn")
            stats(i, slice(0, 1), lambda s: n_h[i, s, :].astype(F32) + n_l[i, s, :].astype(F32))
            toks.direct(i)

        def token_back(i):
            share, own = norm_share(toks, i, slice(0, 1), hat_own[i], root_own[i, :, 0:1])
            d_small[8:9, lanes(0)] = d_small[8:9, lanes(0)] + jnp.sum(own * hat_own[i], axis=0, keepdims=True)
            tok_trim[i] = (resid_grad[i, :, lanes(h)] + share)[0:length]
            store(tok_trim.at[i], tok_grad_out.at[i])

        def output(i):
            out_trim[i] = (ffn.total(i) + down_bias[0:1, :])[0:length]
            store(out_trim.at[i], out_out.at[i])

        tick()
        tick()
        for copy in weights:
            copy.wait()
        def turn(k, _):
            for j in range(3):
                wq_h[lanes(j), lanes(k)], wq_l[lanes(j), lanes(k)] = split(d_qkv[lanes(k), lanes(j)].T)
            return 0

        lax.fori_loop(0, tiles, turn, 0)
        tick()
        last = images - 1

        across(0)
        weight_grads(0)
        tick()
        hop(2, 3)
        hop(3, 2)
        ffn.relay(0)
        ffn.direct(2)
        across(1)
        weight_grads(1)
        tick()
        ffn.relay(1)
        ffn.direct(3)
        across(2)
        weight_grads(2)
        tick()
        tick()
        hop(3, 3)
        across(3)
        weight_grads(3)
        reduce.exchange(out_chunks, qkv_chunks)
        norm_back(0)
        tick()
        norm_back(1)
        tick()
        ffn.relay(2)
        output(0)
        toks.relay(0)
        tick()
        ffn.relay(3)
        output(1)
        token_back(0)
        norm_back(2)
        tick()
        toks.relay(1)
        tick()
        token_back(1)
        norm_back(3)
        tick()
        output(2)
        toks.relay(2)
        tick()
        output(3)
        token_back(2)
        toks.relay(3)
        tick()
        token_back(3)
        reduce.exchange(qkv_chunks, all_chunks)
        reduce.drain()
        for i in range(images):
            back.finish(i)
            ffn.finish(i)
            if i >= images - 2:
                toks.finish(i)

            @pl.when(z > 0)
            def _(i=i):
                state_copy(i, -1).wait_send()

        for k in range(all_chunks):
            reduce.finish(k)
        for copy in stores:
            copy.wait()

    weight_loads = [
        pltpu.make_async_copy(source, room, stage_sem.at[k])
        for k, (source, room) in enumerate(((wfull_in, d_down), (up_in, d_up), (down_in, d_up)))
    ]
    image_loads = (
        lambda i: pltpu.make_async_copy(tok_in.at[i], part.at[0], image_sem.at[0]),
        lambda i: pltpu.make_async_copy(mix_in.at[i], part.at[1], image_sem.at[1]),
    )
    out_load = pltpu.make_async_copy(wout_in, d_out, load_sem.at[1])

    def start_loads():
        weight_loads[0].start()
        for load in image_loads:
            load(0).start()
        weight_loads[1].start()
        out_load.start()
        for i in range(images):
            for copy in proj_copies(i):
                copy.start()

    friends = [{"head": near_x}, {"head": near_y}, {"dp": 1 - c}]
    friends += [{"seq": lax.rem(z + d, seq)} for d in range(1, seq)]
    greet(friends)
    pl.run_scoped(load_phase, vmem((images, length, LANES), F32))
    meet(friends)
    grads.direct(0)
    grads.direct(1)
    down_chunks = reduce.add(d_down, got_ffn.at[0], down_out, CHUNK, ring, range(tiles))
    up_chunks = reduce.add(d_up, got_ffn.at[1], up_out, CHUNK, ring, range(hidden // LANES))
    reduce.add(d_out, got_out, out_w_out, CHUNK, ring, range(tiles))
    out_chunks = reduce.add(d_small, got_small, small_out, 8, ring, range(1, tiles))
    pair = lambda *s: [vmem(s, BF), vmem(s, BF)]
    pl.run_scoped(
        ffn_phase,
        *pair(width, width), *pair(width, hidden),
        *pair(rows, width), *pair(images, rows, width), *pair(images, rows, hidden), *pair(rows, hidden),
    )
    pl.run_scoped(
        attend_phase,
        *pair(3 * LANES, width), vmem((2, rows, width), F32), *pair(images, rows, width), vmem((rows, width), F32),
        *pair(images, rows, 3 * LANES), vmem((images, rows, LANES), F32), vmem((images, rows, 128), F32),
        vmem((width, 3 * LANES), F32), vmem((images, length, LANES), F32), vmem((images, length, LANES), F32),
    )


def layer_call(tok, mix, gains, wfull, up_weight, up_bias, down_weight, down_bias, grads, proj, den, prior, wout, wqkv):
    images, length, _ = grads.shape
    rows, width = tok.shape[1:]
    hidden = up_weight.shape[1]
    used = round_up(length, 8)
    seq = lax.axis_size("seq")
    any_spec = pl.BlockSpec(memory_space=pl.ANY)
    vmem_spec = pl.BlockSpec(memory_space=pltpu.VMEM)
    shape = lambda *s: jax.ShapeDtypeStruct(s, F32)
    vmem, dma = pltpu.VMEM, pltpu.SemaphoreType.DMA
    half = round_up(rows // 2, 8)
    chunks = (2 * (hidden // 2 // CHUNK) + LANES // 2 // CHUNK + 1) * (width // LANES) + 4 * (width // 2 // CHUNK)
    return pl.pallas_call(
        functools.partial(layer_kernel, (images, length, used, rows)),
        out_shape=(
            shape(images, length, LANES),
            shape(images, length, LANES),
            shape(3 * width, LANES),
            shape(LANES, width),
            shape(width, hidden),
            shape(hidden, width),
            shape(16, width),
        ),
        in_specs=[any_spec] * 5 + [vmem_spec, any_spec, vmem_spec] + [any_spec] * 6,
        out_specs=(any_spec,) * 7,
        scratch_shapes=[
            vmem((8, width), F32),
            vmem((images, rows, width), F32), vmem((images, rows, width), F32), vmem((images, rows, width), F32),
            vmem((2, rows, width), F32), vmem((images, 6, half, LANES), F32), vmem((images, 6, half, LANES), F32),
            vmem((images, rows, LANES), F32), vmem((images, rows, 128), F32),
            vmem((hidden, width), F32), vmem((width, hidden), F32), vmem((16, width), F32),
            vmem((2, hidden // 2, width), F32), vmem((LANES // 2, width), F32), vmem((3 * width // 2, LANES), F32),
            vmem((8, width), F32), vmem((images, STATE, LANES), F32), vmem((images, STATE, LANES), F32),
            vmem((Reduce.RING, 2, CHUNK, LANES), F32),
            vmem((images, rows, hidden), F32), vmem((images, rows, 3 * LANES), F32), vmem((images, STATE, LANES), F32),
            vmem((width, LANES), BF), vmem((width, LANES), BF), vmem((LANES, width), F32),
            dma((images, Gather.SEMS)), dma((images, Scatter.SEMS)), dma((images, Gather.SEMS)),
            dma((images, Scatter.SEMS)), dma((images, Scatter.SEMS)), dma((2, images)),
            dma((chunks, Reduce.SEMS)), dma((Reduce.RING, Reduce.RING_SEMS)), dma((8 + 4 * images,)), dma((3,)), dma((2,)), dma((2 * images,)),
        ],
        compiler_params=pltpu.CompilerParams(
            collective_id=1, has_side_effects=True, vmem_limit_bytes=64 * 1024 * 1024
        ),
    )(tok, mix, gains, wfull, up_weight, up_bias, down_weight, down_bias, grads, proj, den, prior, wout, wqkv)


def fast_device(
    tokens,
    gain_attn,
    qkv_weight,
    out_weight,
    gain_ffn,
    up_weight,
    up_bias,
    down_weight,
    down_bias,
    out_grad,
):
    model_width, kinds, local_width = qkv_weight.shape
    if (tokens.shape[0], local_width, up_weight.shape[1]) != (4, LANES, model_width):
        return per_device(
            tokens, gain_attn, qkv_weight, out_weight, gain_ffn, up_weight, up_bias, down_weight, down_bias, out_grad
        )

    proj_weight = jnp.transpose(qkv_weight, (1, 0, 2)).reshape(kinds * model_width, local_width)
    tok, gains, proj, den, prior, mix, wfull = attend_call(
        tokens, gain_attn[None], gain_ffn[None], proj_weight, out_weight
    )
    output, tok_grad, d_qkv, d_out, d_up, d_down, small = layer_call(
        tok, mix, gains, wfull.reshape(model_width, model_width), up_weight, up_bias[None], down_weight,
        down_bias[None], out_grad, proj, den, prior, out_weight, proj_weight,
    )
    return (
        output,
        tok_grad,
        small[8, 0:LANES],
        jnp.transpose(d_qkv.reshape(kinds, model_width, local_width), (1, 0, 2)),
        d_out,
        small[8, LANES : 2 * LANES],
        d_up,
        small[0],
        d_down,
        small[8, 2 * LANES : 3 * LANES],
    )


def device_function(mesh):
    if (mesh.shape["seq"], mesh.shape["head"], mesh.shape["dp"]) == (4, 4, 2):
        return fast_device
    return per_device


def solution(mesh):
    return jax.shard_map(
        device_function(mesh),
        mesh=mesh,
        in_specs=(
            P("dp", "seq", "head"),
            P("head"),
            P(None, None, "head"),
            P("head", None),
            P("head"),
            P(None, "head"),
            P("head"),
            P("head", None),
            P("head"),
            P("dp", "seq", "head"),
        ),
        out_specs=(
            P("dp", "seq", "head"),
            P("dp", "seq", "head"),
            P("head"),
            P(None, None, "head"),
            P("head", None),
            P("head"),
            P(None, "head"),
            P("head"),
            P("head", None),
            P("head"),
        ),
        check_vma=False,
    )
```
